128 devices in a mesh: mem: 8 (over x, core), reg: 16 (over y, z).
Axes of the slice: x: 4, y: 4, z: 4, core: 2. Of those that a mesh axis runs over, the one named last changes fastest.
Arguments:
- prior_samples: float32 [256, 512, 1024], P('mem', 'reg'), may hold values from -6 to 6
- horizontal_flow_ratio: float32 [512, 1024], P('reg'), may hold values from -0.45 to 0.45
- vertical_flow_ratio: float32 [512, 1024], P('reg'), may hold values from -0.45 to 0.45
- obs_index: int32 [16, 2048], P('reg', 'mem'), may hold values from 0 to 4095
- obs_value: float32 [16, 2048], P('reg', 'mem'), may hold values from -6 to 6
- obs_weight: float32 [16, 2048], P('reg', 'mem'), may hold values from 0.00234375 to 0.0234375
Outputs:
- analysis: float32 [256, 512, 1024], P('mem', 'reg')
The draws below stay inside these ranges and needn't reach their ends.
All inputs are finite; a program needn't handle non-finite values.
Results may differ from the reference program's by a relative error of at most 0.0003.
Values sent between devices are 32-bit elements; how exact they have to be, the bound alone decides.
No kernel may reach another device: no remote copies, remote signals or barrier semaphores. Data moves between devices by JAX's collectives and lax.ppermute only.
A program may use at most 256 MiB of HBM per device.

```python
import math
import jax
import jax.numpy as jnp
from jax import lax

SAMPLE_NUMBER = 256
MESH_WIDTH = 1024
ROWS_DEV = 32
OBS_DEV = 256
SECTIONS = 4
NS_ITERS = 6
MESH_HEIGHT = 512
CB = 128
N_MEM = 8
N_REG = 16


def with_ends(array, stream_key, least, top_value):
    longest = array.shape.index(max(array.shape))
    spots = []
    for shift in (0, 1):
        where = [jax.random.randint(jax.random.fold_in(stream_key, axis), (), 0, length) for axis, length in enumerate(array.shape)]
        where[longest] = (where[longest] + shift) % array.shape[longest]
        spots.append(tuple(where))
    return array.at[spots[0]].set(least).at[spots[1]].set(top_value)


def block_scale(key, dims, split, least, top_value):
    def one(axis_at, blocks):
        heights = jax.random.uniform(jax.random.fold_in(jax.random.fold_in(key, 6), axis_at), (blocks,), jnp.float32, least / len(split), top_value / len(split))
        return jnp.repeat(jnp.exp(heights), dims[axis_at] // blocks).reshape((-1,) + (1,) * (len(dims) - axis_at - 1))

    factor_of = one(*split[0])
    for cut in split[1:]:
        factor_of = factor_of * one(*cut)
    return factor_of


def bell_draw(key, dims, scale, limit, split=(), kind=jnp.bfloat16):
    result = jax.random.normal(key, dims, jnp.float32) * scale
    if len(split) > 0:
        result = block_scale(key, dims, split, -0.22, 0.18) * result
    return jnp.clip(result, min=-limit, max=limit).astype(kind)


def setup_inputs(seed: int = 0) -> dict:
    streams_of = jax.random.split(jax.random.key(seed), 7)
    return {
        "prior_samples": bell_draw(streams_of[0], (SAMPLE_NUMBER, MESH_HEIGHT, MESH_WIDTH), 1.0, 6.0, ((0, 8), (1, 16)), jnp.float32),
        "horizontal_flow_ratio": jnp.clip(jax.random.uniform(streams_of[1], (MESH_HEIGHT, MESH_WIDTH), jnp.float32, -0.45, 0.45) * block_scale(streams_of[1], (MESH_HEIGHT, MESH_WIDTH), ((0, 16),), -0.4, 0.0), -0.45, 0.45),
        "vertical_flow_ratio": jnp.clip(jax.random.uniform(streams_of[2], (MESH_HEIGHT, MESH_WIDTH), jnp.float32, -0.45, 0.45) * block_scale(streams_of[2], (MESH_HEIGHT, MESH_WIDTH), ((0, 16),), -0.4, 0.0), -0.45, 0.45),
        "obs_index": with_ends(jax.random.randint(streams_of[3], (N_REG, N_MEM * OBS_DEV), 0, ROWS_DEV * CB), jax.random.fold_in(streams_of[3], 1), 0, (ROWS_DEV * CB) - 1).astype(jnp.int32),
        "obs_value": bell_draw(streams_of[4], (N_REG, N_MEM * OBS_DEV), 1.0, 6.0, ((0, 16), (1, 8)), jnp.float32),
        "obs_weight": jnp.clip(jnp.exp(math.log(0.0234375) - 2.3025851 * jax.random.uniform(streams_of[5], (N_REG, N_MEM * OBS_DEV), jnp.float32) ** block_scale(streams_of[5], (N_REG, N_MEM * OBS_DEV), ((0, 16), (1, 8)), -0.2, 0.2)), 0.00234375, 0.0234375),
    }


def advance(padded, horizontal_flow_ratio, vertical_flow_ratio):
    middle = padded[1:-1, :]
    lower_row = padded[:-2, :]
    upper_row = padded[2:, :]
    west_cell = jnp.roll(middle, 1, axis=1)
    east_cell = jnp.roll(middle, -1, axis=1)
    return middle - jnp.maximum(horizontal_flow_ratio, 0.0) * (middle - west_cell) - jnp.minimum(horizontal_flow_ratio, 0.0) * (east_cell - middle) - jnp.maximum(vertical_flow_ratio, 0.0) * (middle - lower_row) - jnp.minimum(vertical_flow_ratio, 0.0) * (upper_row - middle)

def transform_matrix(gram_sum, drive):
    count = gram_sum.shape[0]
    identity = jnp.eye(count, dtype=jnp.float32)
    gram = gram_sum + (count - 1.0) * identity
    scale = jnp.sqrt(jnp.sum(gram * gram))
    upper = gram / scale
    lower = identity
    for number in range(NS_ITERS):
        middle = 1.5 * identity - 0.5 * jnp.dot(lower, upper, precision=lax.Precision.HIGHEST)
        upper = jnp.dot(upper, middle, precision=lax.Precision.HIGHEST)
        lower = jnp.dot(middle, lower, precision=lax.Precision.HIGHEST)
    inner = jnp.dot(lower, drive, precision=lax.Precision.HIGHEST)
    wbar = jnp.dot(lower, inner, precision=lax.Precision.HIGHEST) / scale
    return jnp.sqrt(count - 1.0) * lower / jnp.sqrt(scale) + wbar[:, None]

def reference(prior_samples, horizontal_flow_ratio, vertical_flow_ratio, obs_index, obs_value, obs_weight):

    def lone_sample(field):
        for number in range(SECTIONS):
            padded = jnp.concatenate([field[-1:, :], field, field[:1, :]], axis=0)
            field = advance(padded, horizontal_flow_ratio, vertical_flow_ratio)
        return field
    predicted_field = lax.map(lone_sample, prior_samples)
    sample_tracers = predicted_field.reshape(SAMPLE_NUMBER, MESH_HEIGHT * MESH_WIDTH)
    mean_state = lax.optimization_barrier(jnp.mean(sample_tracers, axis=0))
    anomalies = sample_tracers - mean_state
    region = jnp.arange(N_REG, dtype=jnp.int32)[:, None]
    column_group = (jnp.arange(N_MEM * OBS_DEV, dtype=jnp.int32) // OBS_DEV)[None, :]
    grid_rows = region * ROWS_DEV + obs_index // CB
    grid_cols = column_group * CB + obs_index % CB
    places = (grid_rows * MESH_WIDTH + grid_cols).reshape(-1).astype(jnp.int32)
    obs_anom = jnp.take(anomalies, places, axis=1)
    innovation = obs_value.reshape(-1) - jnp.take(mean_state, places)
    weighted = obs_anom * obs_weight.reshape(-1)[None, :]
    gram_sum = jnp.dot(weighted, obs_anom.T, precision=lax.Precision.HIGHEST)
    drive = jnp.dot(weighted, innovation, precision=lax.Precision.HIGHEST)
    weights = transform_matrix(gram_sum, drive)
    analysis = mean_state[None, :] + jnp.dot(weights.T, anomalies, precision=lax.Precision.HIGHEST)
    return analysis.reshape(SAMPLE_NUMBER, MESH_HEIGHT, MESH_WIDTH)
```

```python
import functools

import jax
import jax.numpy as jnp
from jax import lax
from jax.experimental import pallas as pl
from jax.experimental.pallas import tpu as pltpu
from jax.sharding import PartitionSpec as P

SECTIONS = 4
NS_ITERS = 6
MEMBERS = 256
N_MEM = 8
N_REG = 16
OWN = MEMBERS // N_MEM
ROWS = 32
WIDTH = 1024
LANES = 128
GROUPS = WIDTH // LANES
OBS = 256
HALF_OBS = OBS * GROUPS // 2
HALO = SECTIONS
EDGE = 2 * HALO
VMEM = pl.BlockSpec(memory_space=pltpu.VMEM)
SMEM = pl.BlockSpec(memory_space=pltpu.SMEM)
PARAMS = pltpu.CompilerParams(vmem_limit_bytes=56 * 1024 * 1024)


def split(x):
    high = x.astype(jnp.bfloat16)
    return high, (x - high.astype(jnp.float32)).astype(jnp.bfloat16)


def dot3(a, b, dims=(((1,), (0,)), ((), ()))):
    dot = functools.partial(
        lax.dot_general, dimension_numbers=dims, preferred_element_type=jnp.float32
    )
    return dot(a[0], b[0]) + (dot(a[0], b[1]) + dot(a[1], b[0]))


def mul(a, b):
    return dot3(split(a), split(b))


def stencil_row(read, coef, write, i):
    lane = lax.broadcasted_iota(jnp.int32, (OWN, LANES), 1)
    middle = [read(i, j) for j in range(GROUPS)]
    right = [pltpu.roll(x, 1, 1) for x in middle]
    left = [pltpu.roll(x, LANES - 1, 1) for x in middle]
    for j in range(GROUPS):
        west = jnp.where(lane == 0, right[(j - 1) % GROUPS], right[j])
        east = jnp.where(lane == LANES - 1, left[(j + 1) % GROUPS], left[j])
        k = [coef(n, i, j) for n in range(5)]
        write(
            i,
            j,
            k[0] * middle[j]
            + k[1] * west
            + k[2] * east
            + k[3] * read(i - 1, j)
            + k[4] * read(i + 1, j),
        )


def coefficients(h, v, coef_ref, i):
    a, b = jnp.maximum(h, 0.0), jnp.minimum(h, 0.0)
    c, d = jnp.maximum(v, 0.0), jnp.minimum(v, 0.0)
    for n, k in enumerate((1.0 - a + b - c + d, a, -b, c, -d)):
        coef_ref[n, i] = jnp.broadcast_to(k, (8, WIDTH))


def sections(bufs, coef_ref, first, last, out_ref, out_at):
    def coef(n, i, j):
        k = coef_ref[n, i, :, j * LANES : (j + 1) * LANES]
        return jnp.concatenate([k] * (OWN // 8), axis=0)

    for s in range(1, SECTIONS + 1):
        src, dst = bufs[(s - 1) % 2], bufs[s % 2]

        def read(i, j):
            return src[i, :, j * LANES : (j + 1) * LANES]

        def write(i, j, x):
            if s == SECTIONS:
                out_ref[j, i + out_at] = x
            else:
                dst[i, :, j * LANES : (j + 1) * LANES] = x

        def body(i, carry):
            stencil_row(read, coef, write, i)
            return carry

        lax.fori_loop(first + s, last - s, body, 0)


def interior_kernel(prior_ref, h_ref, v_ref, out_ref, rim_ref, given, one, two, coef_ref, sems):
    copies = [
        pltpu.make_async_copy(
            prior_ref.at[:, j * LANES : (j + 1) * LANES], given.at[j], sems.at[j]
        )
        for j in range(GROUPS)
    ]
    for copy in copies:
        copy.start()
    for i in range(ROWS):
        coefficients(h_ref[i : i + 1], v_ref[i : i + 1], coef_ref, i)
    for j in range(GROUPS):
        at = slice(j * LANES, (j + 1) * LANES)
        copies[j].wait()
        for i in range(ROWS):
            x = given[j, pl.ds(i, OWN, stride=ROWS), :]
            one[i, :, at] = x
            if i < EDGE:
                rim_ref[0, i, :, at] = x
            if i >= ROWS - EDGE:
                rim_ref[1, i - ROWS + EDGE, :, at] = x
    sections((one, two), coef_ref, 0, ROWS, out_ref, -HALO)


def edge_kernel(rim_ref, low_ref, high_ref, h_ref, v_ref, out_ref, one, two, coef_ref):
    for side, (halo_ref, halo_at, own_at, own_first) in enumerate(
        ((low_ref, 0, HALO, 0), (high_ref, EDGE, 0, ROWS - EDGE))
    ):
        for i in range(HALO):
            one[halo_at + i] = halo_ref[i, :OWN]
            coefficients(
                halo_ref[i, OWN : OWN + 1], halo_ref[i, OWN + 1 : OWN + 2], coef_ref, halo_at + i
            )
        for i in range(EDGE):
            one[own_at + i] = rim_ref[side, i]
            coefficients(
                h_ref[own_first + i : own_first + i + 1],
                v_ref[own_first + i : own_first + i + 1],
                coef_ref,
                own_at + i,
            )
        sections((one, two), coef_ref, 0, HALO + EDGE, out_ref, -HALO + side * HALO)


def pick_kernel(inner_ref, edge_ref, index_ref, out_ref):
    for g in range(GROUPS):
        for t in range(OBS // LANES):
            place = index_ref[g : g + 1, t * LANES : (t + 1) * LANES]
            row = jnp.broadcast_to(place >> 7, (OWN, LANES))
            col = jnp.broadcast_to(place & (LANES - 1), (OWN, LANES))
            total = jnp.zeros((OWN, LANES), jnp.float32)
            for i in range(ROWS):
                if i < HALO:
                    x = edge_ref[g, i]
                elif i < ROWS - HALO:
                    x = inner_ref[g, i - HALO]
                else:
                    x = edge_ref[g, i - ROWS + EDGE]
                x = jnp.take_along_axis(x, col, axis=1, mode="promise_in_bounds")
                total = jnp.where(row == i, x, total)
            at = (g % 4) * OBS + t * LANES
            out_ref[g // 4, :, at : at + LANES] = total


def gram_kernel(core_ref, obs_ref, value_ref, weight_ref, keep_ref, send_ref):
    obs = obs_ref[...]
    mean = jnp.sum(obs, axis=0, keepdims=True) * (1.0 / MEMBERS)
    anomalies = obs - mean
    weighted = split(anomalies * weight_ref[...])
    innovation = jnp.broadcast_to(value_ref[...] - mean, (8, HALF_OBS))
    nt = (((1,), (1,)), ((), ()))
    gram = dot3(split(anomalies), weighted, nt)
    drive = dot3(split(innovation), weighted, nt)
    core = core_ref[0]
    half = MEMBERS // 2
    for c in range(2):

        @pl.when(core == c)
        def _():
            keep_ref[:half] = gram[c * half : (c + 1) * half]
            send_ref[:half] = gram[(1 - c) * half : (2 - c) * half]

    keep_ref[half:] = drive
    send_ref[half:] = drive


def weights_kernel(core_ref, mine_ref, other_ref, high_ref, low_ref, gram_ref):
    core = core_ref[0]
    half = MEMBERS // 2
    for c in range(2):

        @pl.when(core == c)
        def _():
            gram_ref[c * half : (c + 1) * half] = mine_ref[:half]
            gram_ref[(1 - c) * half : (2 - c) * half] = other_ref[:half]

    drive = mine_ref[half:]
    rows = lax.broadcasted_iota(jnp.int32, (MEMBERS, MEMBERS), 0)
    cols = lax.broadcasted_iota(jnp.int32, (MEMBERS, MEMBERS), 1)
    identity = (rows == cols).astype(jnp.float32)
    gram = gram_ref[...] + (MEMBERS - 1.0) * identity
    squares = jnp.sum(jnp.sum(gram * gram, axis=0, keepdims=True), axis=1, keepdims=True)
    scale = jnp.sqrt(squares)
    upper = gram / scale
    lower = 1.5 * identity - 0.5 * upper
    middle = lower
    for number in range(1, NS_ITERS):
        upper = mul(upper, middle)
        middle = 1.5 * identity - 0.5 * mul(lower, upper)
        lower = mul(middle, lower)
    lower_parts = split(lower)
    nt = (((1,), (1,)), ((), ()))
    inner = dot3(split(drive), lower_parts, nt)
    wbar = dot3(split(inner), lower_parts, nt)[:1] / scale
    weights = (MEMBERS - 1.0) ** 0.5 * lower / jnp.sqrt(scale) + wbar
    rest = (1.0 - jnp.sum(weights, axis=1, keepdims=True)) * (1.0 / MEMBERS)
    high, low = split(weights + rest)
    high_ref[...] = high
    low_ref[...] = low


def product_kernel(high_ref, low_ref, inner_ref, edge_ref, out_ref):
    weights = (high_ref[...], low_ref[...])
    cells = MEMBERS

    def pair(ref, i, r):
        parts = []
        for t in range(2):
            x = jnp.concatenate([ref[s, i + t] for s in range(N_MEM)], axis=0)
            parts.append(split(x))
        x = tuple(jnp.concatenate([parts[0][n], parts[1][n]], axis=1) for n in range(2))
        y = dot3(weights, x)
        for t in range(2):
            out_ref[pl.ds(r + t, cells, stride=ROWS), :] = y[:, t * LANES : (t + 1) * LANES]

    for i in range(0, HALO, 2):
        pair(edge_ref, i, i)
        pair(edge_ref, HALO + i, ROWS - HALO + i)

    def body(n, carry):
        pair(inner_ref, 2 * n, HALO + 2 * n)
        return carry

    lax.fori_loop(0, (ROWS - EDGE) // 2, body, 0)


def place_kernel(x_ref, out_ref, sems):
    copies = [
        pltpu.make_async_copy(
            x_ref.at[g], out_ref.at[:, :, g * LANES : (g + 1) * LANES], sems.at[g]
        )
        for g in range(GROUPS)
    ]
    for copy in copies:
        copy.start()
    for copy in copies:
        copy.wait()


def f32(*shape):
    return jax.ShapeDtypeStruct(shape, jnp.float32)


def swap(x, axis, bit):
    count = lax.axis_size(axis)
    return lax.ppermute(x, axis, [(i, i ^ bit) for i in range(count)])


def shift(x, axis, step):
    count = lax.axis_size(axis)
    return lax.ppermute(x, axis, [(i, (i + step) % count) for i in range(count)])


def local(
    prior_samples, horizontal_flow_ratio, vertical_flow_ratio, obs_index, obs_value, obs_weight
):
    h, v = horizontal_flow_ratio, vertical_flow_ratio
    mem = lax.axis_index("mem")
    core = (mem % 2).astype(jnp.int32).reshape(1)

    def rows_out(first):
        x = jnp.concatenate(
            [
                prior_samples[:, first : first + HALO],
                h[None, first : first + HALO],
                v[None, first : first + HALO],
            ],
            axis=0,
        )
        return jnp.pad(jnp.transpose(x, (1, 0, 2)), ((0, 0), (0, 6), (0, 0)))

    low = shift(rows_out(ROWS - HALO), "reg", 1)
    high = shift(rows_out(0), "reg", -1)

    facts = jnp.concatenate([obs_index.astype(jnp.float32), obs_value, obs_weight], axis=0)
    facts = lax.all_to_all(
        jnp.broadcast_to(facts[None], (N_MEM, 3, OBS)), "mem", 0, 0, tiled=True
    )
    index = facts[:, 0].astype(jnp.int32)
    half_facts = lax.dynamic_slice_in_dim(facts, core[0] * 4, 4, axis=0)
    value = half_facts[:, 1].reshape(1, HALF_OBS)
    weight = half_facts[:, 2].reshape(1, HALF_OBS)

    flat = prior_samples.reshape(OWN * ROWS, WIDTH)
    inner, rim = pl.pallas_call(
        interior_kernel,
        out_shape=[f32(GROUPS, ROWS - EDGE, OWN, LANES), f32(2, EDGE, OWN, WIDTH)],
        in_specs=[pl.BlockSpec(memory_space=pl.ANY), VMEM, VMEM],
        out_specs=[VMEM, VMEM],
        scratch_shapes=[
            pltpu.VMEM((GROUPS, OWN * ROWS, LANES), jnp.float32),
            pltpu.VMEM((ROWS, OWN, WIDTH), jnp.float32),
            pltpu.VMEM((ROWS, OWN, WIDTH), jnp.float32),
            pltpu.VMEM((5, ROWS, 8, WIDTH), jnp.float32),
            pltpu.SemaphoreType.DMA((GROUPS,)),
        ],
        compiler_params=PARAMS,
    )(flat, h, v)
    edge = pl.pallas_call(
        edge_kernel,
        out_shape=f32(GROUPS, EDGE, OWN, LANES),
        in_specs=[VMEM] * 5,
        out_specs=VMEM,
        scratch_shapes=[
            pltpu.VMEM((HALO + EDGE, OWN, WIDTH), jnp.float32),
            pltpu.VMEM((HALO + EDGE, OWN, WIDTH), jnp.float32),
            pltpu.VMEM((5, HALO + EDGE, 8, WIDTH), jnp.float32),
        ],
        compiler_params=PARAMS,
    )(rim, low, high, h, v)
    picked = pl.pallas_call(
        pick_kernel,
        out_shape=f32(2, OWN, HALF_OBS),
        in_specs=[VMEM] * 3,
        out_specs=VMEM,
        compiler_params=PARAMS,
    )(inner, edge, index)

    picked = jnp.broadcast_to(picked[None], (N_MEM // 2, 2, OWN, HALF_OBS))
    obs = lax.all_to_all(
        picked.reshape(N_MEM, OWN, HALF_OBS), "mem", 0, 0, tiled=True
    ).reshape(MEMBERS, HALF_OBS)

    inner, edge, obs = lax.optimization_barrier((inner, edge, obs))
    inner = lax.all_to_all(inner, "mem", 0, 0, tiled=True)
    edge = lax.all_to_all(edge, "mem", 0, 0, tiled=True)

    keep, send = pl.pallas_call(
        gram_kernel,
        out_shape=[f32(MEMBERS // 2 + 8, MEMBERS)] * 2,
        in_specs=[SMEM, VMEM, VMEM, VMEM],
        out_specs=[VMEM, VMEM],
        compiler_params=PARAMS,
    )(core, obs, value, weight)
    total = keep + swap(send, "mem", 1)
    for bit in (1, 2, 4, 8):
        total = total + swap(total, "reg", bit)
    other = swap(total, "mem", 1)

    bf16 = jax.ShapeDtypeStruct((MEMBERS, MEMBERS), jnp.bfloat16)
    weights = pl.pallas_call(
        weights_kernel,
        out_shape=[bf16, bf16],
        in_specs=[SMEM, VMEM, VMEM],
        out_specs=[VMEM, VMEM],
        scratch_shapes=[pltpu.VMEM((MEMBERS, MEMBERS), jnp.float32)],
        compiler_params=PARAMS,
    )(core, total, other)

    analysis = pl.pallas_call(
        product_kernel,
        out_shape=f32(MEMBERS * ROWS, LANES),
        in_specs=[VMEM] * 4,
        out_specs=VMEM,
        compiler_params=PARAMS,
    )(*weights, inner, edge)
    analysis = lax.all_to_all(
        analysis.reshape(N_MEM, OWN, ROWS, LANES), "mem", 0, 0, tiled=True
    )
    return pl.pallas_call(
        place_kernel,
        out_shape=f32(OWN, ROWS, WIDTH),
        in_specs=[pl.BlockSpec(memory_space=pl.ANY)],
        out_specs=pl.BlockSpec(memory_space=pl.ANY),
        scratch_shapes=[pltpu.SemaphoreType.DMA((GROUPS,))],
        compiler_params=PARAMS,
    )(analysis)


def solution(mesh):
    placed = (
        P("mem", "reg", None),
        P("reg", None),
        P("reg", None),
        P("reg", "mem"),
        P("reg", "mem"),
        P("reg", "mem"),
    )
    return jax.shard_map(
        local, mesh=mesh, in_specs=placed, out_specs=P("mem", "reg", None), check_vma=False
    )
```

```python
import functools

import jax
import jax.numpy as jnp
from jax import lax
from jax.experimental import pallas as pl
from jax.experimental.pallas import tpu as pltpu
from jax.sharding import PartitionSpec as P

SECTIONS = 4
NS_ITERS = 6
MEMBERS = 256
N_MEM = 8
N_REG = 16
OWN = MEMBERS // N_MEM
ROWS = 32
WIDTH = 1024
LANES = 128
GROUPS = WIDTH // LANES
OBS = 256
HALF_OBS = OBS * GROUPS // 2
HALO = SECTIONS
EDGE = 2 * HALO
VMEM = pl.BlockSpec(memory_space=pltpu.VMEM)
SMEM = pl.BlockSpec(memory_space=pltpu.SMEM)
PARAMS = pltpu.CompilerParams(vmem_limit_bytes=56 * 1024 * 1024)


def split(x):
    high = x.astype(jnp.bfloat16)
    return high, (x - high.astype(jnp.float32)).astype(jnp.bfloat16)


def dot3(a, b, dims=(((1,), (0,)), ((), ()))):
    dot = functools.partial(
        lax.dot_general, dimension_numbers=dims, preferred_element_type=jnp.float32
    )
    return dot(a[0], b[0]) + (dot(a[0], b[1]) + dot(a[1], b[0]))


def mul(a, b):
    return dot3(split(a), split(b))


def stencil_row(read, coef, write, i):
    lane = lax.broadcasted_iota(jnp.int32, (OWN, LANES), 1)
    first = read(i, 0)
    left_first = pltpu.roll(first, LANES - 1, 1)
    right_before = pltpu.roll(read(i, GROUPS - 1), 1, 1)
    middle, left = first, left_first
    for j in range(GROUPS):
        if j + 1 < GROUPS:
            after = read(i, j + 1)
            left_after = pltpu.roll(after, LANES - 1, 1)
        else:
            after, left_after = first, left_first
        right = pltpu.roll(middle, 1, 1)
        h, v = coef(0, i, j), coef(1, i, j)
        side = jnp.where(
            h > 0.0,
            jnp.where(lane == 0, right_before, right),
            jnp.where(lane == LANES - 1, left_after, left),
        )
        below = jnp.where(v > 0.0, read(i - 1, j), read(i + 1, j))
        ah, av = jnp.abs(h), jnp.abs(v)
        write(i, j, (1.0 - ah - av) * middle + ah * side + av * below)
        middle, left, right_before = after, left_after, right


def coefficients(h, v, coef_ref, i):
    coef_ref[0, i] = jnp.broadcast_to(h, (8, WIDTH))
    coef_ref[1, i] = jnp.broadcast_to(v, (8, WIDTH))


def sections(bufs, coef_ref, first, last, out_ref, out_at):
    def coef(n, i, j):
        k = coef_ref[n, i, :, j * LANES : (j + 1) * LANES]
        return jnp.concatenate([k] * (OWN // 8), axis=0)

    for s in range(1, SECTIONS + 1):
        src, dst = bufs[(s - 1) % 2], bufs[s % 2]

        def read(i, j):
            return src[i, :, j * LANES : (j + 1) * LANES]

        def write(i, j, x):
            if s == SECTIONS:
                out_ref[j, i + out_at] = x
            else:
                dst[i, :, j * LANES : (j + 1) * LANES] = x

        def body(i, carry):
            stencil_row(read, coef, write, i)
            return carry

        lax.fori_loop(first + s, last - s, body, 0)


def interior_kernel(prior_ref, h_ref, v_ref, out_ref, rim_ref, given, one, two, coef_ref, sems):
    copies = [
        pltpu.make_async_copy(
            prior_ref.at[:, j * LANES : (j + 1) * LANES], given.at[j], sems.at[j]
        )
        for j in range(GROUPS)
    ]
    for copy in copies:
        copy.start()
    for i in range(ROWS):
        coefficients(h_ref[i : i + 1], v_ref[i : i + 1], coef_ref, i)
    for j in range(GROUPS):
        at = slice(j * LANES, (j + 1) * LANES)
        copies[j].wait()
        for i in range(ROWS):
            x = given[j, pl.ds(i, OWN, stride=ROWS), :]
            one[i, :, at] = x
            if i < EDGE:
                rim_ref[0, i, :, at] = x
            if i >= ROWS - EDGE:
                rim_ref[1, i - ROWS + EDGE, :, at] = x
    sections((one, two), coef_ref, 0, ROWS, out_ref, -HALO)


def edge_kernel(rim_ref, low_ref, high_ref, h_ref, v_ref, out_ref, one, two, coef_ref):
    for side, (halo_ref, halo_at, own_at, own_first) in enumerate(
        ((low_ref, 0, HALO, 0), (high_ref, EDGE, 0, ROWS - EDGE))
    ):
        for i in range(HALO):
            one[halo_at + i] = halo_ref[i, :OWN]
            coefficients(
                halo_ref[i, OWN : OWN + 1], halo_ref[i, OWN + 1 : OWN + 2], coef_ref, halo_at + i
            )
        for i in range(EDGE):
            one[own_at + i] = rim_ref[side, i]
            coefficients(
                h_ref[own_first + i : own_first + i + 1],
                v_ref[own_first + i : own_first + i + 1],
                coef_ref,
                own_at + i,
            )
        sections((one, two), coef_ref, 0, HALO + EDGE, out_ref, -HALO + side * HALO)


def pick_kernel(inner_ref, edge_ref, index_ref, out_ref):
    for g in range(GROUPS):
        for t in range(OBS // LANES):
            place = index_ref[g : g + 1, t * LANES : (t + 1) * LANES]
            row = jnp.broadcast_to(place >> 7, (OWN, LANES))
            col = jnp.broadcast_to(place & (LANES - 1), (OWN, LANES))
            total = jnp.zeros((OWN, LANES), jnp.float32)
            for i in range(ROWS):
                if i < HALO:
                    x = edge_ref[g, i]
                elif i < ROWS - HALO:
                    x = inner_ref[g, i - HALO]
                else:
                    x = edge_ref[g, i - ROWS + EDGE]
                x = jnp.take_along_axis(x, col, axis=1, mode="promise_in_bounds")
                total = jnp.where(row == i, x, total)
            at = (g % 4) * OBS + t * LANES
            out_ref[g // 4, :, at : at + LANES] = total


def gram_kernel(core_ref, obs_ref, value_ref, weight_ref, keep_ref, send_ref):
    obs = obs_ref[...]
    mean = jnp.sum(obs, axis=0, keepdims=True) * (1.0 / MEMBERS)
    anomalies = obs - mean
    weighted = split(anomalies * weight_ref[...])
    innovation = jnp.broadcast_to(value_ref[...] - mean, (8, HALF_OBS))
    nt = (((1,), (1,)), ((), ()))
    gram = dot3(split(anomalies), weighted, nt)
    drive = dot3(split(innovation), weighted, nt)
    core = core_ref[0]
    half = MEMBERS // 2
    for c in range(2):

        @pl.when(core == c)
        def _():
            keep_ref[:half] = gram[c * half : (c + 1) * half]
            send_ref[:half] = gram[(1 - c) * half : (2 - c) * half]

    keep_ref[half:] = drive
    send_ref[half:] = drive


def weights_kernel(core_ref, mine_ref, other_ref, high_ref, low_ref, gram_ref):
    core = core_ref[0]
    half = MEMBERS // 2
    for c in range(2):

        @pl.when(core == c)
        def _():
            gram_ref[c * half : (c + 1) * half] = mine_ref[:half]
            gram_ref[(1 - c) * half : (2 - c) * half] = other_ref[:half]

    drive = mine_ref[half:]
    rows = lax.broadcasted_iota(jnp.int32, (MEMBERS, MEMBERS), 0)
    cols = lax.broadcasted_iota(jnp.int32, (MEMBERS, MEMBERS), 1)
    identity = (rows == cols).astype(jnp.float32)
    gram = gram_ref[...] + (MEMBERS - 1.0) * identity
    squares = jnp.sum(jnp.sum(gram * gram, axis=0, keepdims=True), axis=1, keepdims=True)
    scale = jnp.sqrt(squares)
    upper = gram / scale
    lower = 1.5 * identity - 0.5 * upper
    middle = lower
    for number in range(1, NS_ITERS):
        upper = mul(upper, middle)
        middle = 1.5 * identity - 0.5 * mul(lower, upper)
        lower = mul(middle, lower)
    lower_parts = split(lower)
    nt = (((1,), (1,)), ((), ()))
    inner = dot3(split(drive), lower_parts, nt)
    wbar = dot3(split(inner), lower_parts, nt)[:1] / scale
    weights = (MEMBERS - 1.0) ** 0.5 * lower / jnp.sqrt(scale) + wbar
    rest = (1.0 - jnp.sum(weights, axis=1, keepdims=True)) * (1.0 / MEMBERS)
    high, low = split(weights + rest)
    high_ref[...] = high
    low_ref[...] = low


def product_kernel(high_ref, low_ref, inner_ref, edge_ref, out_ref):
    weights = (high_ref[...], low_ref[...])

    def rows(ref, i, r):
        parts = [
            split(jnp.concatenate([ref[s, i + t] for s in range(N_MEM)], axis=0))
            for t in range(HALO)
        ]
        x = tuple(jnp.concatenate([p[n] for p in parts], axis=1) for n in range(2))
        y = dot3(weights, x)
        for t in range(HALO):
            out_ref[pl.ds(r + t, MEMBERS, stride=ROWS), :] = y[:, t * LANES : (t + 1) * LANES]

    rows(edge_ref, 0, 0)
    rows(edge_ref, HALO, ROWS - HALO)

    def body(n, carry):
        rows(inner_ref, HALO * n, HALO + HALO * n)
        return carry

    lax.fori_loop(0, (ROWS - EDGE) // HALO, body, 0)


def place_kernel(x_ref, out_ref):
    out_ref[...] = x_ref[0]


def f32(*shape):
    return jax.ShapeDtypeStruct(shape, jnp.float32)


def swap(x, axis, bit):
    count = lax.axis_size(axis)
    return lax.ppermute(x, axis, [(i, i ^ bit) for i in range(count)])


def shift(x, axis, step):
    count = lax.axis_size(axis)
    return lax.ppermute(x, axis, [(i, (i + step) % count) for i in range(count)])


def local(
    prior_samples, horizontal_flow_ratio, vertical_flow_ratio, obs_index, obs_value, obs_weight
):
    h, v = horizontal_flow_ratio, vertical_flow_ratio
    mem = lax.axis_index("mem")
    core = (mem % 2).astype(jnp.int32).reshape(1)

    def rows_out(first):
        x = jnp.concatenate(
            [
                prior_samples[:, first : first + HALO],
                h[None, first : first + HALO],
                v[None, first : first + HALO],
            ],
            axis=0,
        )
        return jnp.pad(jnp.transpose(x, (1, 0, 2)), ((0, 0), (0, 6), (0, 0)))

    low = shift(rows_out(ROWS - HALO), "reg", 1)
    high = shift(rows_out(0), "reg", -1)

    facts = jnp.concatenate([obs_index.astype(jnp.float32), obs_value, obs_weight], axis=0)
    facts = lax.all_to_all(
        jnp.broadcast_to(facts[None], (N_MEM, 3, OBS)), "mem", 0, 0, tiled=True
    )
    index = facts[:, 0].astype(jnp.int32)
    half_facts = lax.dynamic_slice_in_dim(facts, core[0] * 4, 4, axis=0)
    value = half_facts[:, 1].reshape(1, HALF_OBS)
    weight = half_facts[:, 2].reshape(1, HALF_OBS)

    flat = prior_samples.reshape(OWN * ROWS, WIDTH)
    inner, rim = pl.pallas_call(
        interior_kernel,
        out_shape=[f32(GROUPS, ROWS - EDGE, OWN, LANES), f32(2, EDGE, OWN, WIDTH)],
        in_specs=[pl.BlockSpec(memory_space=pl.ANY), VMEM, VMEM],
        out_specs=[VMEM, VMEM],
        scratch_shapes=[
            pltpu.VMEM((GROUPS, OWN * ROWS, LANES), jnp.float32),
            pltpu.VMEM((ROWS, OWN, WIDTH), jnp.float32),
            pltpu.VMEM((ROWS, OWN, WIDTH), jnp.float32),
            pltpu.VMEM((2, ROWS, 8, WIDTH), jnp.float32),
            pltpu.SemaphoreType.DMA((GROUPS,)),
        ],
        compiler_params=PARAMS,
    )(flat, h, v)
    edge = pl.pallas_call(
        edge_kernel,
        out_shape=f32(GROUPS, EDGE, OWN, LANES),
        in_specs=[VMEM] * 5,
        out_specs=VMEM,
        scratch_shapes=[
            pltpu.VMEM((HALO + EDGE, OWN, WIDTH), jnp.float32),
            pltpu.VMEM((HALO + EDGE, OWN, WIDTH), jnp.float32),
            pltpu.VMEM((2, HALO + EDGE, 8, WIDTH), jnp.float32),
        ],
        compiler_params=PARAMS,
    )(rim, low, high, h, v)
    picked = pl.pallas_call(
        pick_kernel,
        out_shape=f32(2, OWN, HALF_OBS),
        in_specs=[VMEM] * 3,
        out_specs=VMEM,
        compiler_params=PARAMS,
    )(inner, edge, index)

    picked = jnp.broadcast_to(picked[None], (N_MEM // 2, 2, OWN, HALF_OBS))
    obs = lax.all_to_all(
        picked.reshape(N_MEM, OWN, HALF_OBS), "mem", 0, 0, tiled=True
    ).reshape(MEMBERS, HALF_OBS)

    inner, edge, obs = lax.optimization_barrier((inner, edge, obs))
    inner = lax.all_to_all(inner, "mem", 0, 0, tiled=True)
    edge = lax.all_to_all(edge, "mem", 0, 0, tiled=True)

    keep, send = pl.pallas_call(
        gram_kernel,
        out_shape=[f32(MEMBERS // 2 + 8, MEMBERS)] * 2,
        in_specs=[SMEM, VMEM, VMEM, VMEM],
        out_specs=[VMEM, VMEM],
        compiler_params=PARAMS,
    )(core, obs, value, weight)
    total = keep + swap(send, "mem", 1)
    for bit in (1, 2, 4, 8):
        total = total + swap(total, "reg", bit)
    other = swap(total, "mem", 1)

    bf16 = jax.ShapeDtypeStruct((MEMBERS, MEMBERS), jnp.bfloat16)
    weights = pl.pallas_call(
        weights_kernel,
        out_shape=[bf16, bf16],
        in_specs=[SMEM, VMEM, VMEM],
        out_specs=[VMEM, VMEM],
        scratch_shapes=[pltpu.VMEM((MEMBERS, MEMBERS), jnp.float32)],
        compiler_params=PARAMS,
    )(core, total, other)

    analysis = pl.pallas_call(
        product_kernel,
        out_shape=f32(MEMBERS * ROWS, LANES),
        in_specs=[VMEM] * 4,
        out_specs=VMEM,
        compiler_params=PARAMS,
    )(*weights, inner, edge)
    analysis = lax.all_to_all(
        analysis.reshape(N_MEM, OWN, ROWS, LANES), "mem", 0, 0, tiled=True
    )
    return pl.pallas_call(
        place_kernel,
        grid=(GROUPS,),
        out_shape=f32(OWN, ROWS, WIDTH),
        in_specs=[pl.BlockSpec((1, OWN, ROWS, LANES), lambda g: (g, 0, 0, 0))],
        out_specs=pl.BlockSpec((OWN, ROWS, LANES), lambda g: (0, 0, g)),
        compiler_params=PARAMS,
    )(analysis)


def solution(mesh):
    placed = (
        P("mem", "reg", None),
        P("reg", None),
        P("reg", None),
        P("reg", "mem"),
        P("reg", "mem"),
        P("reg", "mem"),
    )
    return jax.shard_map(
        local, mesh=mesh, in_specs=placed, out_specs=P("mem", "reg", None), check_vma=False
    )
```

```python
import functools

import jax
import jax.numpy as jnp
from jax import lax
from jax.experimental import pallas as pl
from jax.experimental.pallas import tpu as pltpu
from jax.sharding import PartitionSpec as P

SECTIONS = 4
NS_ITERS = 6
MEMBERS = 256
N_MEM = 8
N_REG = 16
OWN = MEMBERS // N_MEM
ROWS = 32
WIDTH = 1024
LANES = 128
GROUPS = WIDTH // LANES
OBS = 256
HALF_OBS = OBS * GROUPS // 2
HALO = SECTIONS
EDGE = 2 * HALO
CHUNK = 8
VMEM = pl.BlockSpec(memory_space=pltpu.VMEM)
SMEM = pl.BlockSpec(memory_space=pltpu.SMEM)
PARAMS = pltpu.CompilerParams(vmem_limit_bytes=56 * 1024 * 1024)


def split(x):
    high = x.astype(jnp.bfloat16)
    return high, (x - high.astype(jnp.float32)).astype(jnp.bfloat16)


def dot3(a, b, dims=(((1,), (0,)), ((), ()))):
    dot = functools.partial(
        lax.dot_general, dimension_numbers=dims, preferred_element_type=jnp.float32
    )
    return dot(a[0], b[0]) + (dot(a[0], b[1]) + dot(a[1], b[0]))


def mul(a, b):
    return dot3(split(a), split(b))


def stencil_row(read, coef, write, i):
    lane = lax.broadcasted_iota(jnp.int32, (OWN, LANES), 1)
    first = read(i, 0)
    left_first = pltpu.roll(first, LANES - 1, 1)
    right_before = pltpu.roll(read(i, GROUPS - 1), 1, 1)
    middle, left = first, left_first
    for j in range(GROUPS):
        if j + 1 < GROUPS:
            after = read(i, j + 1)
            left_after = pltpu.roll(after, LANES - 1, 1)
        else:
            after, left_after = first, left_first
        right = pltpu.roll(middle, 1, 1)
        h, v = coef(0, i, j), coef(1, i, j)
        side = jnp.where(
            h > 0.0,
            jnp.where(lane == 0, right_before, right),
            jnp.where(lane == LANES - 1, left_after, left),
        )
        below = jnp.where(v > 0.0, read(i - 1, j), read(i + 1, j))
        ah, av = jnp.abs(h), jnp.abs(v)
        write(i, j, (1.0 - ah - av) * middle + ah * side + av * below)
        middle, left, right_before = after, left_after, right


def coefficients(h, v, coef_ref, i):
    coef_ref[0, i] = jnp.broadcast_to(h, (8, WIDTH))
    coef_ref[1, i] = jnp.broadcast_to(v, (8, WIDTH))


def sections(bufs, coef_ref, first, last, out_ref, out_at):
    def coef(n, i, j):
        k = coef_ref[n, i, :, j * LANES : (j + 1) * LANES]
        return jnp.concatenate([k] * (OWN // 8), axis=0)

    for s in range(1, SECTIONS + 1):
        src, dst = bufs[(s - 1) % 2], bufs[s % 2]

        def read(i, j):
            return src[i, :, j * LANES : (j + 1) * LANES]

        def write(i, j, x):
            if s == SECTIONS:
                out_ref[j, i + out_at] = x
            else:
                dst[i, :, j * LANES : (j + 1) * LANES] = x

        def body(i, carry):
            stencil_row(read, coef, write, i)
            return carry

        lax.fori_loop(first + s, last - s, body, 0)


def interior_kernel(
    prior_ref, h_ref, v_ref, out_ref, early_ref, rim_ref, given, one, two, coef_ref, sems
):
    copies = [
        pltpu.make_async_copy(
            prior_ref.at[:, j * LANES : (j + 1) * LANES], given.at[j], sems.at[j]
        )
        for j in range(GROUPS)
    ]
    for copy in copies:
        copy.start()
    for i in range(ROWS):
        coefficients(h_ref[i : i + 1], v_ref[i : i + 1], coef_ref, i)
    for j in range(GROUPS):
        at = slice(j * LANES, (j + 1) * LANES)
        copies[j].wait()
        for i in range(ROWS):
            x = given[j, pl.ds(i, OWN, stride=ROWS), :]
            one[i, :, at] = x
            if i < EDGE:
                rim_ref[0, i, :, at] = x
            if i >= ROWS - EDGE:
                rim_ref[1, i - ROWS + EDGE, :, at] = x
    sections((one, two), coef_ref, 0, ROWS, out_ref, -HALO)
    early_ref[...] = out_ref[:, CHUNK - HALO : 2 * CHUNK - HALO]


def edge_kernel(
    inner_ref, rim_ref, low_ref, high_ref, h_ref, v_ref, index_ref,
    obs_ref, rest_ref, field, one, two, coef_ref, in_sem, out_sems,
):
    load = pltpu.make_async_copy(inner_ref, field.at[:, HALO : ROWS - HALO], in_sem)
    load.start()
    for side, (halo_ref, halo_at, own_at, own_first) in enumerate(
        ((low_ref, 0, HALO, 0), (high_ref, EDGE, 0, ROWS - EDGE))
    ):
        for i in range(HALO):
            one[halo_at + i] = halo_ref[i, :OWN]
            coefficients(
                halo_ref[i, OWN : OWN + 1], halo_ref[i, OWN + 1 : OWN + 2], coef_ref, halo_at + i
            )
        for i in range(EDGE):
            one[own_at + i] = rim_ref[side, i]
            coefficients(
                h_ref[own_first + i : own_first + i + 1],
                v_ref[own_first + i : own_first + i + 1],
                coef_ref,
                own_at + i,
            )
        at = -HALO if side == 0 else ROWS - EDGE
        sections((one, two), coef_ref, 0, HALO + EDGE, field, at)
    load.wait()
    stores = [
        pltpu.make_async_copy(
            field.at[:, first : first + count], rest_ref.at[:, to : to + count], out_sems.at[n]
        )
        for n, (first, count, to) in enumerate(
            ((0, CHUNK, 0), (2 * CHUNK, ROWS - 2 * CHUNK, CHUNK))
        )
    ]
    for store in stores:
        store.start()
    for g in range(GROUPS):
        for t in range(OBS // LANES):
            place = index_ref[g : g + 1, t * LANES : (t + 1) * LANES]
            row = jnp.broadcast_to(place >> 7, (OWN, LANES))
            col = jnp.broadcast_to(place & (LANES - 1), (OWN, LANES))
            total = jnp.zeros((OWN, LANES), jnp.float32)
            for i in range(ROWS):
                x = jnp.take_along_axis(field[g, i], col, axis=1, mode="promise_in_bounds")
                total = jnp.where(row == i, x, total)
            at = (g % 4) * OBS + t * LANES
            for x in range(N_MEM // 2):
                obs_ref[2 * x + g // 4, :, at : at + LANES] = total
    for store in stores:
        store.wait()


def gram_kernel(core_ref, obs_ref, value_ref, weight_ref, keep_ref, send_ref):
    obs = obs_ref[...]
    mean = jnp.sum(obs, axis=0, keepdims=True) * (1.0 / MEMBERS)
    anomalies = obs - mean
    weighted = split(anomalies * weight_ref[...])
    innovation = jnp.broadcast_to(value_ref[...] - mean, (8, HALF_OBS))
    nt = (((1,), (1,)), ((), ()))
    gram = dot3(split(anomalies), weighted, nt)
    drive = dot3(split(innovation), weighted, nt)
    core = core_ref[0]
    half = MEMBERS // 2
    for c in range(2):

        @pl.when(core == c)
        def _():
            keep_ref[:half] = gram[c * half : (c + 1) * half]
            send_ref[:half] = gram[(1 - c) * half : (2 - c) * half]

    keep_ref[half:] = drive
    send_ref[half:] = drive


def weights_kernel(core_ref, mine_ref, other_ref, high_ref, low_ref, gram_ref):
    core = core_ref[0]
    half = MEMBERS // 2
    for c in range(2):

        @pl.when(core == c)
        def _():
            gram_ref[c * half : (c + 1) * half] = mine_ref[:half]
            gram_ref[(1 - c) * half : (2 - c) * half] = other_ref[:half]

    drive = mine_ref[half:]
    rows = lax.broadcasted_iota(jnp.int32, (MEMBERS, MEMBERS), 0)
    cols = lax.broadcasted_iota(jnp.int32, (MEMBERS, MEMBERS), 1)
    identity = (rows == cols).astype(jnp.float32)
    gram = gram_ref[...] + (MEMBERS - 1.0) * identity
    squares = jnp.sum(jnp.sum(gram * gram, axis=0, keepdims=True), axis=1, keepdims=True)
    scale = jnp.sqrt(squares)
    upper = gram / scale
    lower = 1.5 * identity - 0.5 * upper
    middle = lower
    for number in range(1, NS_ITERS):
        upper = mul(upper, middle)
        middle = 1.5 * identity - 0.5 * mul(lower, upper)
        lower = mul(middle, lower)
    lower_parts = split(lower)
    nt = (((1,), (1,)), ((), ()))
    inner = dot3(split(drive), lower_parts, nt)
    wbar = dot3(split(inner), lower_parts, nt)[:1] / scale
    weights = (MEMBERS - 1.0) ** 0.5 * lower / jnp.sqrt(scale) + wbar
    rest = (1.0 - jnp.sum(weights, axis=1, keepdims=True)) * (1.0 / MEMBERS)
    high, low = split(weights + rest)
    high_ref[...] = high
    low_ref[...] = low


def product_kernel(high_ref, low_ref, early_ref, rest_ref, out_ref):
    weights = (high_ref[...], low_ref[...])
    flat = out_ref.reshape(MEMBERS * CHUNK, LANES)

    def rows(ref):
        for half in range(0, CHUNK, HALO):
            parts = [
                split(jnp.concatenate([ref[s, half + t] for s in range(N_MEM)], axis=0))
                for t in range(HALO)
            ]
            x = tuple(jnp.concatenate([p[n] for p in parts], axis=1) for n in range(2))
            y = dot3(weights, x)
            for t in range(HALO):
                flat[pl.ds(half + t, MEMBERS, stride=CHUNK), :] = y[
                    :, t * LANES : (t + 1) * LANES
                ]

    step = pl.program_id(0)
    pl.when(step == 1)(lambda: rows(early_ref))
    pl.when(step != 1)(lambda: rows(rest_ref))


def place_kernel(x_ref, out_ref):
    out_ref[...] = x_ref[0]


def f32(*shape):
    return jax.ShapeDtypeStruct(shape, jnp.float32)


def swap(x, axis, bit):
    count = lax.axis_size(axis)
    return lax.ppermute(x, axis, [(i, i ^ bit) for i in range(count)])


def shift(x, axis, step):
    count = lax.axis_size(axis)
    return lax.ppermute(x, axis, [(i, (i + step) % count) for i in range(count)])


def local(
    prior_samples, horizontal_flow_ratio, vertical_flow_ratio, obs_index, obs_value, obs_weight
):
    h, v = horizontal_flow_ratio, vertical_flow_ratio
    mem = lax.axis_index("mem")
    core = (mem % 2).astype(jnp.int32).reshape(1)

    def rows_out(first):
        x = jnp.concatenate(
            [
                prior_samples[:, first : first + HALO],
                h[None, first : first + HALO],
                v[None, first : first + HALO],
            ],
            axis=0,
        )
        return jnp.pad(jnp.transpose(x, (1, 0, 2)), ((0, 0), (0, 6), (0, 0)))

    low = shift(rows_out(ROWS - HALO), "reg", 1)
    high = shift(rows_out(0), "reg", -1)

    facts = jnp.concatenate([obs_index.astype(jnp.float32), obs_value, obs_weight], axis=0)
    facts = lax.all_to_all(
        jnp.broadcast_to(facts[None], (N_MEM, 3, OBS)), "mem", 0, 0, tiled=True
    )
    index = facts[:, 0].astype(jnp.int32)
    half_facts = lax.dynamic_slice_in_dim(facts, core[0] * 4, 4, axis=0)
    value = half_facts[:, 1].reshape(1, HALF_OBS)
    weight = half_facts[:, 2].reshape(1, HALF_OBS)

    flat = prior_samples.reshape(OWN * ROWS, WIDTH)
    anywhere = pl.BlockSpec(memory_space=pl.ANY)
    inner, early, rim = pl.pallas_call(
        interior_kernel,
        out_shape=[
            f32(GROUPS, ROWS - EDGE, OWN, LANES),
            f32(GROUPS, CHUNK, OWN, LANES),
            f32(2, EDGE, OWN, WIDTH),
        ],
        in_specs=[anywhere, VMEM, VMEM],
        out_specs=[VMEM, VMEM, VMEM],
        scratch_shapes=[
            pltpu.VMEM((GROUPS, OWN * ROWS, LANES), jnp.float32),
            pltpu.VMEM((ROWS, OWN, WIDTH), jnp.float32),
            pltpu.VMEM((ROWS, OWN, WIDTH), jnp.float32),
            pltpu.VMEM((2, ROWS, 8, WIDTH), jnp.float32),
            pltpu.SemaphoreType.DMA((GROUPS,)),
        ],
        compiler_params=PARAMS,
    )(flat, h, v)
    early = lax.all_to_all(early, "mem", 0, 0, tiled=True)
    obs, rest = pl.pallas_call(
        edge_kernel,
        out_shape=[
            f32(N_MEM, OWN, HALF_OBS),
            f32(GROUPS, ROWS - CHUNK, OWN, LANES),
        ],
        in_specs=[anywhere] + [VMEM] * 6,
        out_specs=[VMEM, anywhere],
        scratch_shapes=[
            pltpu.VMEM((GROUPS, ROWS, OWN, LANES), jnp.float32),
            pltpu.VMEM((HALO + EDGE, OWN, WIDTH), jnp.float32),
            pltpu.VMEM((HALO + EDGE, OWN, WIDTH), jnp.float32),
            pltpu.VMEM((2, HALO + EDGE, 8, WIDTH), jnp.float32),
            pltpu.SemaphoreType.DMA,
            pltpu.SemaphoreType.DMA((2,)),
        ],
        compiler_params=PARAMS,
    )(inner, rim, low, high, h, v, index)
    obs = lax.all_to_all(obs, "mem", 0, 0, tiled=True).reshape(MEMBERS, HALF_OBS)

    keep, send = pl.pallas_call(
        gram_kernel,
        out_shape=[f32(MEMBERS // 2 + 8, MEMBERS)] * 2,
        in_specs=[SMEM, VMEM, VMEM, VMEM],
        out_specs=[VMEM, VMEM],
        compiler_params=PARAMS,
    )(core, obs, value, weight)
    rest, send = lax.optimization_barrier((rest, send))
    rest = lax.all_to_all(rest, "mem", 0, 0, tiled=True)
    total = keep + swap(send, "mem", 1)
    for bit in (1, 2, 4, 8):
        total = total + swap(total, "reg", bit)
    other = swap(total, "mem", 1)

    bf16 = jax.ShapeDtypeStruct((MEMBERS, MEMBERS), jnp.bfloat16)
    weights = pl.pallas_call(
        weights_kernel,
        out_shape=[bf16, bf16],
        in_specs=[SMEM, VMEM, VMEM],
        out_specs=[VMEM, VMEM],
        scratch_shapes=[pltpu.VMEM((MEMBERS, MEMBERS), jnp.float32)],
        compiler_params=PARAMS,
    )(core, total, other)

    whole = pl.BlockSpec((MEMBERS, MEMBERS), lambda n: (0, 0))
    block = (N_MEM, CHUNK, OWN, LANES)
    analysis = pl.pallas_call(
        product_kernel,
        grid=(ROWS // CHUNK,),
        out_shape=f32(N_MEM, OWN, ROWS, LANES),
        in_specs=[
            whole,
            whole,
            pl.BlockSpec(block, lambda n: (0, 0, 0, 0)),
            pl.BlockSpec(block, lambda n: (0, jnp.maximum(n - 1, 0), 0, 0)),
        ],
        out_specs=pl.BlockSpec((N_MEM, OWN, CHUNK, LANES), lambda n: (0, 0, n, 0)),
        compiler_params=PARAMS,
    )(*weights, early, rest)
    analysis = lax.all_to_all(analysis, "mem", 0, 0, tiled=True)
    return pl.pallas_call(
        place_kernel,
        grid=(GROUPS,),
        out_shape=f32(OWN, ROWS, WIDTH),
        in_specs=[pl.BlockSpec((1, OWN, ROWS, LANES), lambda g: (g, 0, 0, 0))],
        out_specs=pl.BlockSpec((OWN, ROWS, LANES), lambda g: (0, 0, g)),
        compiler_params=PARAMS,
    )(analysis)


def solution(mesh):
    placed = (
        P("mem", "reg", None),
        P("reg", None),
        P("reg", None),
        P("reg", "mem"),
        P("reg", "mem"),
        P("reg", "mem"),
    )
    return jax.shard_map(
        local, mesh=mesh, in_specs=placed, out_specs=P("mem", "reg", None), check_vma=False
    )
```

```python
import functools

import jax
import jax.numpy as jnp
from jax import lax
from jax.experimental import pallas as pl
from jax.experimental.pallas import tpu as pltpu
from jax.sharding import PartitionSpec as P

SECTIONS = 4
NS_ITERS = 6
MEMBERS = 256
N_MEM = 8
N_REG = 16
OWN = MEMBERS // N_MEM
ROWS = 32
WIDTH = 1024
LANES = 128
GROUPS = WIDTH // LANES
OBS = 256
HALF_OBS = OBS * GROUPS // 2
HALO = SECTIONS
EDGE = 2 * HALO
CHUNK = 8
PATHS = ((0, 0), (2, 0), (1, 0), (3, 0), (2, 1), (1, 1), (3, 1), (0, 1))
VMEM = pl.BlockSpec(memory_space=pltpu.VMEM)
SMEM = pl.BlockSpec(memory_space=pltpu.SMEM)


def params(mib):
    return pltpu.CompilerParams(vmem_limit_bytes=mib * 1024 * 1024)


def cost(us):
    return pl.CostEstimate(flops=0, bytes_accessed=us * 3_000_000, transcendentals=0)


def split(x):
    high = x.astype(jnp.bfloat16)
    return high, (x - high.astype(jnp.float32)).astype(jnp.bfloat16)


def dot3(a, b, dims=(((1,), (0,)), ((), ()))):
    dot = functools.partial(
        lax.dot_general, dimension_numbers=dims, preferred_element_type=jnp.float32
    )
    return dot(a[0], b[0]) + (dot(a[0], b[1]) + dot(a[1], b[0]))


def mul(a, b):
    return dot3(split(a), split(b))


def stencil_row(read, coef, write, i):
    lane = lax.broadcasted_iota(jnp.int32, (OWN, LANES), 1)
    first = read(i, 0)
    left_first = pltpu.roll(first, LANES - 1, 1)
    right_before = pltpu.roll(read(i, GROUPS - 1), 1, 1)
    middle, left = first, left_first
    for j in range(GROUPS):
        if j + 1 < GROUPS:
            after = read(i, j + 1)
            left_after = pltpu.roll(after, LANES - 1, 1)
        else:
            after, left_after = first, left_first
        right = pltpu.roll(middle, 1, 1)
        h, v = coef(0, i, j), coef(1, i, j)
        side = jnp.where(
            h > 0.0,
            jnp.where(lane == 0, right_before, right),
            jnp.where(lane == LANES - 1, left_after, left),
        )
        below = jnp.where(v > 0.0, read(i - 1, j), read(i + 1, j))
        ah, av = jnp.abs(h), jnp.abs(v)
        write(i, j, (1.0 - ah - av) * middle + ah * side + av * below)
        middle, left, right_before = after, left_after, right


def coefficients(h, v, coef_ref, i):
    coef_ref[0, i] = jnp.broadcast_to(h, (8, WIDTH))
    coef_ref[1, i] = jnp.broadcast_to(v, (8, WIDTH))


def sections(bufs, coef_ref, first, last, out_ref, out_at):
    def coef(n, i, j):
        k = coef_ref[n, i, :, j * LANES : (j + 1) * LANES]
        return jnp.concatenate([k] * (OWN // 8), axis=0)

    for s in range(1, SECTIONS + 1):
        src, dst = bufs[(s - 1) % 2], bufs[s % 2]

        def read(i, j):
            return src[i, :, j * LANES : (j + 1) * LANES]

        def write(i, j, x):
            if s == SECTIONS:
                out_ref[j, i + out_at] = x
            else:
                dst[i, :, j * LANES : (j + 1) * LANES] = x

        def body(i, carry):
            stencil_row(read, coef, write, i)
            return carry

        lax.fori_loop(first + s, last - s, body, 0)


def interior_kernel(
    prior_ref, h_ref, v_ref, out_ref, early_ref, rim_ref, given, one, two, coef_ref, sems
):
    copies = [
        pltpu.make_async_copy(
            prior_ref.at[:, j * LANES : (j + 1) * LANES], given.at[j], sems.at[j]
        )
        for j in range(GROUPS)
    ]
    for copy in copies:
        copy.start()
    for i in range(ROWS):
        coefficients(h_ref[i : i + 1], v_ref[i : i + 1], coef_ref, i)
    for j in range(GROUPS):
        at = slice(j * LANES, (j + 1) * LANES)
        copies[j].wait()
        for i in range(ROWS):
            x = given[j, pl.ds(i, OWN, stride=ROWS), :]
            one[i, :, at] = x
            if i < EDGE:
                rim_ref[0, i, :, at] = x
            if i >= ROWS - EDGE:
                rim_ref[1, i - ROWS + EDGE, :, at] = x
    sections((one, two), coef_ref, 0, ROWS, out_ref, -HALO)
    early_ref[...] = out_ref[:, CHUNK - HALO : 2 * CHUNK - HALO]


def edge_kernel(
    inner_ref, rim_ref, low_ref, high_ref, h_ref, v_ref, index_ref,
    obs_ref, rest_ref, field, one, two, coef_ref, in_sem, out_sems,
):
    load = pltpu.make_async_copy(inner_ref, field.at[:, HALO : ROWS - HALO], in_sem)
    load.start()
    for side, (halo_ref, halo_at, own_at, own_first) in enumerate(
        ((low_ref, 0, HALO, 0), (high_ref, EDGE, 0, ROWS - EDGE))
    ):
        for i in range(HALO):
            one[halo_at + i] = halo_ref[i, :OWN]
            coefficients(
                halo_ref[i, OWN : OWN + 1], halo_ref[i, OWN + 1 : OWN + 2], coef_ref, halo_at + i
            )
        for i in range(EDGE):
            one[own_at + i] = rim_ref[side, i]
            coefficients(
                h_ref[own_first + i : own_first + i + 1],
                v_ref[own_first + i : own_first + i + 1],
                coef_ref,
                own_at + i,
            )
        at = -HALO if side == 0 else ROWS - EDGE
        sections((one, two), coef_ref, 0, HALO + EDGE, field, at)
    load.wait()
    stores = [
        pltpu.make_async_copy(
            field.at[:, first : first + count], rest_ref.at[:, to : to + count], out_sems.at[n]
        )
        for n, (first, count, to) in enumerate(
            ((0, CHUNK, 0), (2 * CHUNK, ROWS - 2 * CHUNK, CHUNK))
        )
    ]
    for store in stores:
        store.start()
    for g in range(GROUPS):
        for t in range(OBS // LANES):
            place = index_ref[g : g + 1, t * LANES : (t + 1) * LANES]
            row = jnp.broadcast_to(place >> 7, (OWN, LANES))
            col = jnp.broadcast_to(place & (LANES - 1), (OWN, LANES))
            total = jnp.zeros((OWN, LANES), jnp.float32)
            for i in range(ROWS):
                x = jnp.take_along_axis(field[g, i], col, axis=1, mode="promise_in_bounds")
                total = jnp.where(row == i, x, total)
            at = (g % 4) * OBS + t * LANES
            for x in range(N_MEM // 2):
                obs_ref[2 * x + g // 4, :, at : at + LANES] = total
    for store in stores:
        store.wait()


def gram_kernel(core_ref, obs_ref, value_ref, weight_ref, keep_ref, send_ref):
    obs = obs_ref[...]
    mean = jnp.sum(obs, axis=0, keepdims=True) * (1.0 / MEMBERS)
    anomalies = obs - mean
    weighted = split(anomalies * weight_ref[...])
    innovation = jnp.broadcast_to(value_ref[...] - mean, (8, HALF_OBS))
    nt = (((1,), (1,)), ((), ()))
    gram = dot3(split(anomalies), weighted, nt)
    drive = dot3(split(innovation), weighted, nt)
    core = core_ref[0]
    half = MEMBERS // 2
    for c in range(2):

        @pl.when(core == c)
        def _():
            keep_ref[:half] = gram[c * half : (c + 1) * half]
            send_ref[:half] = gram[(1 - c) * half : (2 - c) * half]

    keep_ref[half:] = drive
    send_ref[half:] = drive


def weights_kernel(core_ref, order_ref, mine_ref, other_ref, high_ref, low_ref, gram_ref):
    core = core_ref[0]
    half = MEMBERS // 2
    for c in range(2):

        @pl.when(core == c)
        def _():
            gram_ref[c * half : (c + 1) * half] = mine_ref[:half]
            gram_ref[(1 - c) * half : (2 - c) * half] = other_ref[:half]

    drive = mine_ref[half:]
    rows = lax.broadcasted_iota(jnp.int32, (MEMBERS, MEMBERS), 0)
    cols = lax.broadcasted_iota(jnp.int32, (MEMBERS, MEMBERS), 1)
    identity = (rows == cols).astype(jnp.float32)
    gram = gram_ref[...] + (MEMBERS - 1.0) * identity
    squares = jnp.sum(jnp.sum(gram * gram, axis=0, keepdims=True), axis=1, keepdims=True)
    scale = jnp.sqrt(squares)
    upper = gram / scale
    lower = 1.5 * identity - 0.5 * upper
    middle = lower
    for number in range(1, NS_ITERS):
        upper = mul(upper, middle)
        middle = 1.5 * identity - 0.5 * mul(lower, upper)
        lower = mul(middle, lower)
    lower_parts = split(lower)
    nt = (((1,), (1,)), ((), ()))
    inner = dot3(split(drive), lower_parts, nt)
    wbar = dot3(split(inner), lower_parts, nt)[:1] / scale
    weights = (MEMBERS - 1.0) ** 0.5 * lower / jnp.sqrt(scale) + wbar
    rest = (1.0 - jnp.sum(weights, axis=1, keepdims=True)) * (1.0 / MEMBERS)
    gram_ref[...] = weights + rest
    for n in range(N_MEM):
        high, low = split(gram_ref[pl.ds(pl.multiple_of(order_ref[n] * OWN, OWN), OWN), :])
        high_ref[n * OWN : (n + 1) * OWN] = high
        low_ref[n * OWN : (n + 1) * OWN] = low


def product_kernel(high_ref, low_ref, early_ref, rest_ref, *out_refs):
    weights = (high_ref[...], low_ref[...])
    flat = [ref.reshape(OWN * CHUNK, LANES) for ref in out_refs]

    def rows(ref):
        for half in range(0, CHUNK, HALO):
            parts = [
                split(jnp.concatenate([ref[s, half + t] for s in range(N_MEM)], axis=0))
                for t in range(HALO)
            ]
            x = tuple(jnp.concatenate([p[n] for p in parts], axis=1) for n in range(2))
            y = dot3(weights, x)
            for t in range(HALO):
                for n in range(N_MEM):
                    flat[n][pl.ds(half + t, OWN, stride=CHUNK), :] = y[
                        n * OWN : (n + 1) * OWN, t * LANES : (t + 1) * LANES
                    ]

    step = pl.program_id(0)
    pl.when(step == 1)(lambda: rows(early_ref))
    pl.when(step != 1)(lambda: rows(rest_ref))


def place_first_kernel(group_ref, x_ref, out_ref):
    out_ref[...] = x_ref[...]


def place_kernel(group_ref, x_ref, before_ref, out_ref):
    out_ref[...] = x_ref[...]


def place(x, group, before=None):
    spec = pltpu.PrefetchScalarGridSpec(
        num_scalar_prefetch=1,
        grid=(1,),
        in_specs=[pl.BlockSpec((OWN, ROWS, LANES), lambda n, g: (0, 0, 0))]
        + ([] if before is None else [pl.BlockSpec(memory_space=pl.ANY)]),
        out_specs=pl.BlockSpec((OWN, ROWS, LANES), lambda n, g: (0, 0, g[0])),
    )
    return pl.pallas_call(
        place_first_kernel if before is None else place_kernel,
        grid_spec=spec,
        out_shape=f32(OWN, ROWS, WIDTH),
        input_output_aliases={} if before is None else {2: 0},
        compiler_params=params(8),
        cost_estimate=cost(1),
    )(group, x, *([] if before is None else [before]))


def f32(*shape):
    return jax.ShapeDtypeStruct(shape, jnp.float32)


def swap(x, axis, bit):
    count = lax.axis_size(axis)
    return lax.ppermute(x, axis, [(i, i ^ bit) for i in range(count)])


def shift(x, axis, step):
    count = lax.axis_size(axis)
    return lax.ppermute(x, axis, [(i, (i + step) % count) for i in range(count)])


def local(
    prior_samples, horizontal_flow_ratio, vertical_flow_ratio, obs_index, obs_value, obs_weight
):
    h, v = horizontal_flow_ratio, vertical_flow_ratio
    mem = lax.axis_index("mem")
    core = (mem % 2).astype(jnp.int32).reshape(1)
    order = jnp.stack(
        [((mem // 2 + a) % 4) * 2 + (mem % 2 + b) % 2 for a, b in PATHS]
    ).astype(jnp.int32)
    sources = [
        (((mem // 2 - a) % 4) * 2 + (mem % 2 + b) % 2).astype(jnp.int32).reshape(1)
        for a, b in PATHS
    ]

    def rows_out(first):
        x = jnp.concatenate(
            [
                prior_samples[:, first : first + HALO],
                h[None, first : first + HALO],
                v[None, first : first + HALO],
            ],
            axis=0,
        )
        return jnp.pad(jnp.transpose(x, (1, 0, 2)), ((0, 0), (0, 6), (0, 0)))

    bottom, top = rows_out(0), rows_out(ROWS - HALO)
    bottom, top, prior_samples, h, v = lax.optimization_barrier(
        (bottom, top, prior_samples, h, v)
    )
    low = shift(top, "reg", 1)
    high = shift(bottom, "reg", -1)

    facts = jnp.concatenate([obs_index.astype(jnp.float32), obs_value, obs_weight], axis=0)
    facts = lax.all_to_all(
        jnp.broadcast_to(facts[None], (N_MEM, 3, OBS)), "mem", 0, 0, tiled=True
    )
    index = facts[:, 0].astype(jnp.int32)
    half_facts = lax.dynamic_slice_in_dim(facts, core[0] * 4, 4, axis=0)
    value = half_facts[:, 1].reshape(1, HALF_OBS)
    weight = half_facts[:, 2].reshape(1, HALF_OBS)

    flat = prior_samples.reshape(OWN * ROWS, WIDTH)
    anywhere = pl.BlockSpec(memory_space=pl.ANY)
    inner, early, rim = pl.pallas_call(
        interior_kernel,
        out_shape=[
            f32(GROUPS, ROWS - EDGE, OWN, LANES),
            f32(GROUPS, CHUNK, OWN, LANES),
            f32(2, EDGE, OWN, WIDTH),
        ],
        in_specs=[anywhere, VMEM, VMEM],
        out_specs=[VMEM, VMEM, VMEM],
        scratch_shapes=[
            pltpu.VMEM((GROUPS, OWN * ROWS, LANES), jnp.float32),
            pltpu.VMEM((ROWS, OWN, WIDTH), jnp.float32),
            pltpu.VMEM((ROWS, OWN, WIDTH), jnp.float32),
            pltpu.VMEM((2, ROWS, 8, WIDTH), jnp.float32),
            pltpu.SemaphoreType.DMA((GROUPS,)),
        ],
        compiler_params=params(56),
        cost_estimate=cost(22),
    )(flat, h, v)
    early, low, high = lax.optimization_barrier((early, low, high))
    early = lax.all_to_all(early, "mem", 0, 0, tiled=True)
    obs, rest = pl.pallas_call(
        edge_kernel,
        out_shape=[
            f32(N_MEM, OWN, HALF_OBS),
            f32(GROUPS, ROWS - CHUNK, OWN, LANES),
        ],
        in_specs=[anywhere] + [VMEM] * 6,
        out_specs=[VMEM, anywhere],
        scratch_shapes=[
            pltpu.VMEM((GROUPS, ROWS, OWN, LANES), jnp.float32),
            pltpu.VMEM((HALO + EDGE, OWN, WIDTH), jnp.float32),
            pltpu.VMEM((HALO + EDGE, OWN, WIDTH), jnp.float32),
            pltpu.VMEM((2, HALO + EDGE, 8, WIDTH), jnp.float32),
            pltpu.SemaphoreType.DMA,
            pltpu.SemaphoreType.DMA((2,)),
        ],
        compiler_params=params(56),
        cost_estimate=cost(13),
    )(inner, rim, low, high, h, v, index)
    early, obs = lax.optimization_barrier((early, obs))
    obs = lax.all_to_all(obs, "mem", 0, 0, tiled=True).reshape(MEMBERS, HALF_OBS)

    keep, send = pl.pallas_call(
        gram_kernel,
        out_shape=[f32(MEMBERS // 2 + 8, MEMBERS)] * 2,
        in_specs=[SMEM, VMEM, VMEM, VMEM],
        out_specs=[VMEM, VMEM],
        compiler_params=params(12),
        cost_estimate=cost(3),
    )(core, obs, value, weight)
    rest, send = lax.optimization_barrier((rest, send))
    rest = lax.all_to_all(rest, "mem", 0, 0, tiled=True)
    total = keep + swap(send, "mem", 1)
    for bit in (1, 2, 4, 8):
        total = total + swap(total, "reg", bit)
    other = swap(total, "mem", 1)

    bf16 = jax.ShapeDtypeStruct((MEMBERS, MEMBERS), jnp.bfloat16)
    weights = pl.pallas_call(
        weights_kernel,
        out_shape=[bf16, bf16],
        in_specs=[SMEM, SMEM, VMEM, VMEM],
        out_specs=[VMEM, VMEM],
        scratch_shapes=[pltpu.VMEM((MEMBERS, MEMBERS), jnp.float32)],
        compiler_params=params(16),
        cost_estimate=cost(6),
    )(core, order, total, other)

    whole = pl.BlockSpec((MEMBERS, MEMBERS), lambda n: (0, 0))
    block = (N_MEM, CHUNK, OWN, LANES)
    analysis = pl.pallas_call(
        product_kernel,
        grid=(ROWS // CHUNK,),
        out_shape=[f32(OWN, ROWS, LANES)] * N_MEM,
        in_specs=[
            whole,
            whole,
            pl.BlockSpec(block, lambda n: (0, 0, 0, 0)),
            pl.BlockSpec(block, lambda n: (0, jnp.maximum(n - 1, 0), 0, 0)),
        ],
        out_specs=[pl.BlockSpec((OWN, CHUNK, LANES), lambda n: (0, n, 0))] * N_MEM,
        compiler_params=params(20),
        cost_estimate=cost(6),
    )(*weights, early, rest)
    result = place(analysis[0], sources[0])
    for x, (a, b), source in zip(analysis[1:], PATHS[1:], sources[1:]):
        arrived = lax.ppermute(
            x, "mem", [(i, ((i // 2 + a) % 4) * 2 + (i + b) % 2) for i in range(N_MEM)]
        )
        result = place(arrived, source, result)
    return result


def solution(mesh):
    placed = (
        P("mem", "reg", None),
        P("reg", None),
        P("reg", None),
        P("reg", "mem"),
        P("reg", "mem"),
        P("reg", "mem"),
    )
    return jax.shard_map(
        local, mesh=mesh, in_specs=placed, out_specs=P("mem", "reg", None), check_vma=False
    )
```

```python
import functools

import jax
import jax.numpy as jnp
from jax import lax
from jax.experimental import pallas as pl
from jax.experimental.pallas import tpu as pltpu
from jax.sharding import PartitionSpec as P

SECTIONS = 4
NS_ITERS = 6
MEMBERS = 256
N_MEM = 8
N_REG = 16
OWN = MEMBERS // N_MEM
ROWS = 32
WIDTH = 1024
LANES = 128
GROUPS = WIDTH // LANES
OBS = 256
HALF_OBS = OBS * GROUPS // 2
HALO = SECTIONS
EDGE = 2 * HALO
CHUNK = 8
SUB = 8
PATHS = ((0, 0), (2, 0), (1, 0), (3, 0), (2, 1), (1, 1), (3, 1), (0, 1))
VMEM = pl.BlockSpec(memory_space=pltpu.VMEM)
SMEM = pl.BlockSpec(memory_space=pltpu.SMEM)


def params(mib):
    return pltpu.CompilerParams(vmem_limit_bytes=mib * 1024 * 1024)


def cost(us):
    return pl.CostEstimate(flops=0, bytes_accessed=us * 3_000_000, transcendentals=0)


def split(x):
    high = x.astype(jnp.bfloat16)
    return high, (x - high.astype(jnp.float32)).astype(jnp.bfloat16)


def dot3(a, b, dims=(((1,), (0,)), ((), ()))):
    dot = functools.partial(
        lax.dot_general, dimension_numbers=dims, preferred_element_type=jnp.float32
    )
    return dot(a[0], b[0]) + (dot(a[0], b[1]) + dot(a[1], b[0]))


def mul(a, b):
    return dot3(split(a), split(b))


def coefficients(h, v, coef_ref, i):
    coef_ref[0, i] = jnp.broadcast_to(h, (SUB, WIDTH))
    coef_ref[1, i] = jnp.broadcast_to(v, (SUB, WIDTH))


def advance(src, dst, coef_ref, first, last, at, grouped):
    lane = lax.broadcasted_iota(jnp.int32, (SUB, LANES), 1)

    def tile(i, m):
        def read(row, j):
            return src[row, m : m + SUB, j * LANES : (j + 1) * LANES]

        middle = [read(i, j) for j in range(GROUPS)]
        right = [pltpu.roll(x, 1, 1) for x in middle]
        left = [pltpu.roll(x, LANES - 1, 1) for x in middle]
        results = []
        for j in range(GROUPS):
            h = coef_ref[0, i, :, j * LANES : (j + 1) * LANES]
            v = coef_ref[1, i, :, j * LANES : (j + 1) * LANES]
            side = jnp.where(
                h > 0.0,
                jnp.where(lane == 0, right[j - 1], right[j]),
                jnp.where(lane == LANES - 1, left[(j + 1) % GROUPS], left[j]),
            )
            below = jnp.where(v > 0.0, read(i - 1, j), read(i + 1, j))
            ah, av = jnp.abs(h), jnp.abs(v)
            results.append((1.0 - ah - av) * middle[j] + ah * side + av * below)
        for j, x in enumerate(results):
            if grouped:
                dst[j, i + at, m : m + SUB] = x
            else:
                dst[i + at, m : m + SUB, j * LANES : (j + 1) * LANES] = x

    def body(n, carry):
        start = jnp.minimum(first + n * HALO, last - HALO)
        for q in range(HALO):
            for m in range(0, OWN, SUB):
                tile(start + q, m)
        return carry

    lax.fori_loop(0, -(-(last - first) // HALO), body, 0)


def pack_kernel(parity_ref, prior_ref, h_ref, v_ref, a_ref, b_ref, given, sems):
    copies = []
    for side in range(2):
        rows = slice(side * (ROWS - SUB), side * (ROWS - SUB) + SUB)
        copies.append(
            [
                pltpu.make_async_copy(
                    prior_ref.at[:, rows, j * LANES : (j + 1) * LANES],
                    given.at[side, j],
                    sems.at[side, j],
                )
                for j in range(GROUPS)
            ]
        )
    for j in range(GROUPS):
        for side in range(2):
            copies[side][j].start()
    for side in range(2):
        for copy in copies[side]:
            copy.wait()
    parity = parity_ref[0]
    for even in range(2):

        @pl.when(parity == 1 - even)
        def _():
            for side in range(2):
                out_ref = a_ref if side == even else b_ref
                first = side * (ROWS - HALO)
                for i in range(HALO):
                    for j in range(GROUPS):
                        x = given.at[side, j].reshape(OWN * SUB, LANES)[
                            pl.ds(side * (SUB - HALO) + i, OWN, stride=SUB), :
                        ]
                        out_ref[i, :OWN, j * LANES : (j + 1) * LANES] = x
                    out_ref[i, OWN : OWN + 1] = h_ref[first + i : first + i + 1]
                    out_ref[i, OWN + 1 : OWN + 2] = v_ref[first + i : first + i + 1]


def interior_kernel(
    prior_ref, h_ref, v_ref,
    inner_ref, early_ref, rim_ref, given, one, two, field, coef_ref, sems, out_sems,
):
    copies = [
        pltpu.make_async_copy(
            prior_ref.at[:, j * LANES : (j + 1) * LANES], given.at[j], sems.at[j]
        )
        for j in range(GROUPS)
    ]
    for copy in copies:
        copy.start()
    for i in range(ROWS):
        coefficients(h_ref[i : i + 1], v_ref[i : i + 1], coef_ref, i)
    for j in range(GROUPS):
        at = slice(j * LANES, (j + 1) * LANES)
        copies[j].wait()
        for i in range(ROWS):
            one[i, :, at] = given[j, pl.ds(i, OWN, stride=ROWS), :]
    rims = [
        pltpu.make_async_copy(
            one.at[side * (ROWS - EDGE) : side * (ROWS - EDGE) + EDGE],
            rim_ref.at[side],
            out_sems.at[side],
        )
        for side in range(2)
    ]
    for copy in rims:
        copy.start()
    advance(one, two, coef_ref, 1, ROWS - 1, 0, False)
    for copy in rims:
        copy.wait()
    advance(two, one, coef_ref, 2, ROWS - 2, 0, False)
    advance(one, two, coef_ref, 3, ROWS - 3, 0, False)
    advance(two, field, coef_ref, CHUNK, 2 * CHUNK, -HALO, True)
    early = pltpu.make_async_copy(
        field.at[:, CHUNK - HALO : 2 * CHUNK - HALO], early_ref, out_sems.at[2]
    )
    early.start()
    advance(two, field, coef_ref, HALO, CHUNK, -HALO, True)
    middle = 2 * CHUNK - HALO
    upper = pltpu.make_async_copy(field.at[:, :middle], inner_ref.at[:, :middle], out_sems.at[3])
    upper.start()
    advance(two, field, coef_ref, 2 * CHUNK, ROWS - HALO, -HALO, True)
    lower = pltpu.make_async_copy(field.at[:, middle:], inner_ref.at[:, middle:], out_sems.at[4])
    lower.start()
    early.wait()
    upper.wait()
    lower.wait()


def edge_kernel(
    parity_ref, inner_ref, rim_ref, a_ref, b_ref, h_ref, v_ref, index_ref,
    obs_ref, rest_ref, field, one, two, coef_ref, in_sem, out_sems,
):
    load = pltpu.make_async_copy(inner_ref, field.at[:, HALO : ROWS - HALO], in_sem)
    load.start()
    odd = parity_ref[0] == 1
    for side, (near_ref, far_ref, halo_at, own_at, own_first) in enumerate(
        ((a_ref, b_ref, 0, HALO, 0), (b_ref, a_ref, EDGE, 0, ROWS - EDGE))
    ):
        for i in range(HALO):
            halo = jnp.where(odd, near_ref[i], far_ref[i])
            one[halo_at + i] = halo[:OWN]
            coefficients(halo[OWN : OWN + 1], halo[OWN + 1 : OWN + 2], coef_ref, halo_at + i)
        for i in range(EDGE):
            one[own_at + i] = rim_ref[side, i]
            coefficients(
                h_ref[own_first + i : own_first + i + 1],
                v_ref[own_first + i : own_first + i + 1],
                coef_ref,
                own_at + i,
            )
        last = HALO + EDGE
        advance(one, two, coef_ref, 1, last - 1, 0, False)
        advance(two, one, coef_ref, 2, last - 2, 0, False)
        advance(one, two, coef_ref, 3, last - 3, 0, False)
        at = -HALO if side == 0 else ROWS - EDGE
        advance(two, field, coef_ref, HALO, EDGE, at, True)
    load.wait()
    stores = [
        pltpu.make_async_copy(
            field.at[:, first : first + count], rest_ref.at[:, to : to + count], out_sems.at[n]
        )
        for n, (first, count, to) in enumerate(
            ((0, CHUNK, 0), (2 * CHUNK, ROWS - 2 * CHUNK, CHUNK))
        )
    ]
    for store in stores:
        store.start()
    for g in range(GROUPS):
        for t in range(OBS // LANES):
            place = index_ref[g : g + 1, t * LANES : (t + 1) * LANES]
            row = jnp.broadcast_to(place >> 7, (OWN, LANES))
            col = jnp.broadcast_to(place & (LANES - 1), (OWN, LANES))
            total = jnp.zeros((OWN, LANES), jnp.float32)
            for i in range(ROWS):
                x = jnp.take_along_axis(field[g, i], col, axis=1, mode="promise_in_bounds")
                total = jnp.where(row == i, x, total)
            at = (g % 4) * OBS + t * LANES
            for x in range(N_MEM // 2):
                obs_ref[2 * x + g // 4, :, at : at + LANES] = total
    for store in stores:
        store.wait()


def gram_kernel(core_ref, obs_ref, value_ref, weight_ref, keep_ref, send_ref):
    obs = obs_ref[...]
    mean = jnp.sum(obs, axis=0, keepdims=True) * (1.0 / MEMBERS)
    anomalies = obs - mean
    weighted = split(anomalies * weight_ref[...])
    innovation = jnp.broadcast_to(value_ref[...] - mean, (8, HALF_OBS))
    nt = (((1,), (1,)), ((), ()))
    gram = dot3(split(anomalies), weighted, nt)
    drive = dot3(split(innovation), weighted, nt)
    core = core_ref[0]
    half = MEMBERS // 2
    for c in range(2):

        @pl.when(core == c)
        def _():
            keep_ref[:half] = gram[c * half : (c + 1) * half]
            send_ref[:half] = gram[(1 - c) * half : (2 - c) * half]

    keep_ref[half:] = drive
    send_ref[half:] = drive


def weights_kernel(mem_ref, mine_ref, other_ref, out_ref, gram_ref):
    mem = mem_ref[0]
    core = lax.rem(mem, 2)
    half = MEMBERS // 2
    for c in range(2):

        @pl.when(core == c)
        def _():
            gram_ref[c * half : (c + 1) * half] = mine_ref[:half]
            gram_ref[(1 - c) * half : (2 - c) * half] = other_ref[:half]

    drive = mine_ref[half:]
    rows = lax.broadcasted_iota(jnp.int32, (MEMBERS, MEMBERS), 0)
    cols = lax.broadcasted_iota(jnp.int32, (MEMBERS, MEMBERS), 1)
    identity = (rows == cols).astype(jnp.float32)
    gram = gram_ref[...] + (MEMBERS - 1.0) * identity
    squares = jnp.sum(jnp.sum(gram * gram, axis=0, keepdims=True), axis=1, keepdims=True)
    scale = jnp.sqrt(squares)
    upper = gram / scale
    lower = 1.5 * identity - 0.5 * upper
    middle = lower
    for number in range(1, NS_ITERS):
        upper = mul(upper, middle)
        middle = 1.5 * identity - 0.5 * mul(lower, upper)
        lower = mul(middle, lower)
    lower_parts = split(lower)
    nt = (((1,), (1,)), ((), ()))
    inner = dot3(split(drive), lower_parts, nt)
    wbar = dot3(split(inner), lower_parts, nt)[:1] / scale
    weights = (MEMBERS - 1.0) ** 0.5 * lower / jnp.sqrt(scale) + wbar
    rest = (1.0 - jnp.sum(weights, axis=1, keepdims=True)) * (1.0 / MEMBERS)
    gram_ref[...] = weights + rest
    for n, (a, b) in enumerate(PATHS):
        place = lax.rem(mem // 2 + a, 4) * 2 + lax.rem(core + b, 2)
        high, low = split(gram_ref[pl.ds(pl.multiple_of(place * OWN, OWN), OWN), :])
        out_ref[n * OWN : (n + 1) * OWN] = high
        out_ref[MEMBERS + n * OWN : MEMBERS + (n + 1) * OWN] = low


def product_kernel(mem_ref, weights_ref, early_ref, rest_ref, *out_refs):
    weights = (weights_ref[:MEMBERS], weights_ref[MEMBERS:])
    flat = [ref.reshape(OWN * CHUNK, LANES) for ref in out_refs]

    def rows(ref):
        for half in range(0, CHUNK, HALO):
            parts = [
                split(jnp.concatenate([ref[s, half + t] for s in range(N_MEM)], axis=0))
                for t in range(HALO)
            ]
            x = tuple(jnp.concatenate([p[n] for p in parts], axis=1) for n in range(2))
            y = dot3(weights, x)
            for t in range(HALO):
                for n in range(N_MEM):
                    flat[n][pl.ds(half + t, OWN, stride=CHUNK), :] = y[
                        n * OWN : (n + 1) * OWN, t * LANES : (t + 1) * LANES
                    ]

    step = pl.program_id(0)
    pl.when(step == 1)(lambda: rows(early_ref))
    pl.when(step != 1)(lambda: rows(rest_ref))


def place_kernel(group_ref, x_ref, before_ref, out_ref):
    out_ref[...] = x_ref[...]


def place(x, group, before):
    return pl.pallas_call(
        place_kernel,
        grid_spec=pltpu.PrefetchScalarGridSpec(
            num_scalar_prefetch=1,
            grid=(1,),
            in_specs=[
                pl.BlockSpec((OWN, ROWS, LANES), lambda n, g: (0, 0, 0)),
                pl.BlockSpec(memory_space=pl.ANY),
            ],
            out_specs=pl.BlockSpec((OWN, ROWS, LANES), lambda n, g: (0, 0, g[0])),
        ),
        out_shape=f32(OWN, ROWS, WIDTH),
        input_output_aliases={2: 0},
        compiler_params=params(8),
        cost_estimate=cost(1),
    )(group, x, before)


def f32(*shape):
    return jax.ShapeDtypeStruct(shape, jnp.float32)


def swap(x, axis, bit):
    count = lax.axis_size(axis)
    return lax.ppermute(x, axis, [(i, i ^ bit) for i in range(count)])


def local(
    prior_samples, horizontal_flow_ratio, vertical_flow_ratio, obs_index, obs_value, obs_weight
):
    h, v = horizontal_flow_ratio, vertical_flow_ratio
    anywhere = pl.BlockSpec(memory_space=pl.ANY)
    mem = lax.axis_index("mem").astype(jnp.int32)
    core = (mem % 2).reshape(1)
    parity = (lax.axis_index("reg").astype(jnp.int32) % 2).reshape(1)
    sources = [
        (((mem // 2 - a) % 4) * 2 + (mem % 2 + b) % 2).reshape(1) for a, b in PATHS
    ]
    mem = mem.reshape(1)

    halo_a, halo_b = pl.pallas_call(
        pack_kernel,
        out_shape=[f32(HALO, OWN + SUB, WIDTH)] * 2,
        in_specs=[SMEM, anywhere, VMEM, VMEM],
        out_specs=[VMEM, VMEM],
        scratch_shapes=[
            pltpu.VMEM((2, GROUPS, OWN, SUB, LANES), jnp.float32),
            pltpu.SemaphoreType.DMA((2, GROUPS)),
        ],
        compiler_params=params(56),
    )(parity, prior_samples, h, v)
    halo_a, halo_b, prior_samples, h, v = lax.optimization_barrier(
        (halo_a, halo_b, prior_samples, h, v)
    )
    halo_a = lax.ppermute(halo_a, "reg", [(i, i ^ 1) for i in range(N_REG)])
    halo_b = lax.ppermute(
        halo_b, "reg", [(i, (i - 1 if i % 2 == 0 else i + 1) % N_REG) for i in range(N_REG)]
    )

    facts = jnp.concatenate([obs_index.astype(jnp.float32), obs_value, obs_weight], axis=0)
    facts = lax.all_to_all(
        jnp.broadcast_to(facts[None], (N_MEM, 3, OBS)), "mem", 0, 0, tiled=True
    )
    index = facts[:, 0].astype(jnp.int32)
    half_facts = lax.dynamic_slice_in_dim(facts, core[0] * 4, 4, axis=0)
    value = half_facts[:, 1].reshape(1, HALF_OBS)
    weight = half_facts[:, 2].reshape(1, HALF_OBS)

    inner, early, rim = pl.pallas_call(
        interior_kernel,
        out_shape=[
            f32(GROUPS, ROWS - EDGE, OWN, LANES),
            f32(GROUPS, CHUNK, OWN, LANES),
            f32(2, EDGE, OWN, WIDTH),
        ],
        in_specs=[anywhere, VMEM, VMEM],
        out_specs=[anywhere] * 3,
        scratch_shapes=[
            pltpu.VMEM((GROUPS, OWN * ROWS, LANES), jnp.float32),
            pltpu.VMEM((ROWS, OWN, WIDTH), jnp.float32),
            pltpu.VMEM((ROWS, OWN, WIDTH), jnp.float32),
            pltpu.VMEM((GROUPS, ROWS - EDGE, OWN, LANES), jnp.float32),
            pltpu.VMEM((2, ROWS, SUB, WIDTH), jnp.float32),
            pltpu.SemaphoreType.DMA((GROUPS,)),
            pltpu.SemaphoreType.DMA((5,)),
        ],
        compiler_params=params(56),
        cost_estimate=cost(17),
    )(prior_samples.reshape(OWN * ROWS, WIDTH), h, v)
    early, halo_a, halo_b = lax.optimization_barrier((early, halo_a, halo_b))
    early = lax.all_to_all(early, "mem", 0, 0, tiled=True)
    obs, rest = pl.pallas_call(
        edge_kernel,
        out_shape=[
            f32(N_MEM, OWN, HALF_OBS),
            f32(GROUPS, ROWS - CHUNK, OWN, LANES),
        ],
        in_specs=[SMEM, anywhere] + [VMEM] * 6,
        out_specs=[VMEM, anywhere],
        scratch_shapes=[
            pltpu.VMEM((GROUPS, ROWS, OWN, LANES), jnp.float32),
            pltpu.VMEM((HALO + EDGE, OWN, WIDTH), jnp.float32),
            pltpu.VMEM((HALO + EDGE, OWN, WIDTH), jnp.float32),
            pltpu.VMEM((2, HALO + EDGE, SUB, WIDTH), jnp.float32),
            pltpu.SemaphoreType.DMA,
            pltpu.SemaphoreType.DMA((2,)),
        ],
        compiler_params=params(56),
        cost_estimate=cost(13),
    )(parity, inner, rim, halo_a, halo_b, h, v, index)
    early, obs = lax.optimization_barrier((early, obs))
    obs = lax.all_to_all(obs, "mem", 0, 0, tiled=True).reshape(MEMBERS, HALF_OBS)

    keep, send = pl.pallas_call(
        gram_kernel,
        out_shape=[f32(MEMBERS // 2 + 8, MEMBERS)] * 2,
        in_specs=[SMEM, VMEM, VMEM, VMEM],
        out_specs=[VMEM, VMEM],
        compiler_params=params(12),
        cost_estimate=cost(3),
    )(core, obs, value, weight)
    rest, send = lax.optimization_barrier((rest, send))
    rest = lax.all_to_all(rest, "mem", 0, 0, tiled=True)
    total = keep + swap(send, "mem", 1)
    for bit in (1, 2, 4, 8):
        total = total + swap(total, "reg", bit)
    other = swap(total, "mem", 1)

    weights = pl.pallas_call(
        weights_kernel,
        out_shape=jax.ShapeDtypeStruct((2 * MEMBERS, MEMBERS), jnp.bfloat16),
        in_specs=[SMEM, VMEM, VMEM],
        out_specs=VMEM,
        scratch_shapes=[pltpu.VMEM((MEMBERS, MEMBERS), jnp.float32)],
        compiler_params=params(16),
        cost_estimate=cost(6),
    )(mem, total, other)

    block = (N_MEM, CHUNK, OWN, LANES)
    result, *analysis = pl.pallas_call(
        product_kernel,
        grid_spec=pltpu.PrefetchScalarGridSpec(
            num_scalar_prefetch=1,
            grid=(ROWS // CHUNK,),
            in_specs=[
                pl.BlockSpec((2 * MEMBERS, MEMBERS), lambda n, g: (0, 0)),
                pl.BlockSpec(block, lambda n, g: (0, 0, 0, 0)),
                pl.BlockSpec(block, lambda n, g: (0, jnp.maximum(n - 1, 0), 0, 0)),
            ],
            out_specs=[pl.BlockSpec((OWN, CHUNK, LANES), lambda n, g: (0, n, g[0]))]
            + [pl.BlockSpec((OWN, CHUNK, LANES), lambda n, g: (0, n, 0))] * (N_MEM - 1),
        ),
        out_shape=[f32(OWN, ROWS, WIDTH)] + [f32(OWN, ROWS, LANES)] * (N_MEM - 1),
        compiler_params=params(20),
        cost_estimate=cost(6),
    )(mem, weights, early, rest)
    for x, (a, b), source in zip(analysis, PATHS[1:], sources[1:]):
        arrived = lax.ppermute(
            x, "mem", [(i, ((i // 2 + a) % 4) * 2 + (i + b) % 2) for i in range(N_MEM)]
        )
        result = place(arrived, source, result)
    return result


def solution(mesh):
    placed = (
        P("mem", "reg", None),
        P("reg", None),
        P("reg", None),
        P("reg", "mem"),
        P("reg", "mem"),
        P("reg", "mem"),
    )
    return jax.shard_map(
        local, mesh=mesh, in_specs=placed, out_specs=P("mem", "reg", None), check_vma=False
    )
```

```python
import functools

import jax
import jax.numpy as jnp
from jax import lax
from jax.experimental import pallas as pl
from jax.experimental.pallas import tpu as pltpu
from jax.sharding import PartitionSpec as P

SECTIONS = 4
NS_ITERS = 6
MEMBERS = 256
N_MEM = 8
N_REG = 16
OWN = MEMBERS // N_MEM
ROWS = 32
WIDTH = 1024
LANES = 128
GROUPS = WIDTH // LANES
OBS = 256
HALF_OBS = OBS * GROUPS // 2
HALO = SECTIONS
EDGE = 2 * HALO
CHUNK = 8
SUB = 8
PATHS = ((0, 0), (2, 0), (1, 0), (3, 0), (2, 1), (1, 1), (3, 1), (0, 1))
VMEM = pl.BlockSpec(memory_space=pltpu.VMEM)
SMEM = pl.BlockSpec(memory_space=pltpu.SMEM)


def params(mib):
    return pltpu.CompilerParams(vmem_limit_bytes=mib * 1024 * 1024)


def cost(us):
    return pl.CostEstimate(flops=0, bytes_accessed=us * 3_000_000, transcendentals=0)


def split(x):
    high = x.astype(jnp.bfloat16)
    return high, (x - high.astype(jnp.float32)).astype(jnp.bfloat16)


def dot3(a, b, dims=(((1,), (0,)), ((), ()))):
    dot = functools.partial(
        lax.dot_general, dimension_numbers=dims, preferred_element_type=jnp.float32
    )
    return dot(a[0], b[0]) + (dot(a[0], b[1]) + dot(a[1], b[0]))


def mul(a, b):
    return dot3(split(a), split(b))


def coefficients(h, v, coef_ref, i):
    coef_ref[0, i] = jnp.broadcast_to(h, (SUB, WIDTH))
    coef_ref[1, i] = jnp.broadcast_to(v, (SUB, WIDTH))


def advance(src, dst, coef_ref, first, last, at, grouped):
    lane = lax.broadcasted_iota(jnp.int32, (SUB, LANES), 1)

    def tile(i, m):
        def read(row, j):
            return src[row, m : m + SUB, j * LANES : (j + 1) * LANES]

        middle = [read(i, j) for j in range(GROUPS)]
        right = [pltpu.roll(x, 1, 1) for x in middle]
        left = [pltpu.roll(x, LANES - 1, 1) for x in middle]
        results = []
        for j in range(GROUPS):
            h = coef_ref[0, i, :, j * LANES : (j + 1) * LANES]
            v = coef_ref[1, i, :, j * LANES : (j + 1) * LANES]
            side = jnp.where(
                h > 0.0,
                jnp.where(lane == 0, right[j - 1], right[j]),
                jnp.where(lane == LANES - 1, left[(j + 1) % GROUPS], left[j]),
            )
            below = jnp.where(v > 0.0, read(i - 1, j), read(i + 1, j))
            ah, av = jnp.abs(h), jnp.abs(v)
            results.append((1.0 - ah - av) * middle[j] + ah * side + av * below)
        for j, x in enumerate(results):
            if grouped:
                dst[j, i + at, m : m + SUB] = x
            else:
                dst[i + at, m : m + SUB, j * LANES : (j + 1) * LANES] = x

    def body(n, carry):
        start = jnp.minimum(first + n * HALO, last - HALO)
        for q in range(HALO):
            for m in range(0, OWN, SUB):
                tile(start + q, m)
        return carry

    lax.fori_loop(0, -(-(last - first) // HALO), body, 0)


def pack_kernel(parity_ref, prior_ref, h_ref, v_ref, a_ref, b_ref, given, sems):
    copies = []
    for side in range(2):
        rows = slice(side * (ROWS - SUB), side * (ROWS - SUB) + SUB)
        copies.append(
            [
                pltpu.make_async_copy(
                    prior_ref.at[:, rows, j * LANES : (j + 1) * LANES],
                    given.at[side, j],
                    sems.at[side, j],
                )
                for j in range(GROUPS)
            ]
        )
    for j in range(GROUPS):
        for side in range(2):
            copies[side][j].start()
    for side in range(2):
        for copy in copies[side]:
            copy.wait()
    parity = parity_ref[0]
    for even in range(2):

        @pl.when(parity == 1 - even)
        def _():
            for side in range(2):
                out_ref = a_ref if side == even else b_ref
                first = side * (ROWS - HALO)
                for i in range(HALO):
                    for j in range(GROUPS):
                        x = given.at[side, j].reshape(OWN * SUB, LANES)[
                            pl.ds(side * (SUB - HALO) + i, OWN, stride=SUB), :
                        ]
                        out_ref[i, :OWN, j * LANES : (j + 1) * LANES] = x
                    out_ref[i, OWN : OWN + 1] = h_ref[first + i : first + i + 1]
                    out_ref[i, OWN + 1 : OWN + 2] = v_ref[first + i : first + i + 1]


def interior_kernel(
    prior_ref, h_ref, v_ref,
    inner_ref, early_ref, rim_ref, given, one, two, field, coef_ref, sems, out_sems,
):
    copies = [
        pltpu.make_async_copy(
            prior_ref.at[:, j * LANES : (j + 1) * LANES], given.at[j], sems.at[j]
        )
        for j in range(GROUPS)
    ]
    for copy in copies:
        copy.start()
    for i in range(ROWS):
        coefficients(h_ref[i : i + 1], v_ref[i : i + 1], coef_ref, i)
    for j in range(GROUPS):
        at = slice(j * LANES, (j + 1) * LANES)
        copies[j].wait()
        for i in range(ROWS):
            one[i, :, at] = given[j, pl.ds(i, OWN, stride=ROWS), :]
    rims = [
        pltpu.make_async_copy(
            one.at[side * (ROWS - EDGE) : side * (ROWS - EDGE) + EDGE],
            rim_ref.at[side],
            out_sems.at[side],
        )
        for side in range(2)
    ]
    for copy in rims:
        copy.start()
    advance(one, two, coef_ref, 1, ROWS - 1, 0, False)
    for copy in rims:
        copy.wait()
    advance(two, one, coef_ref, 2, ROWS - 2, 0, False)
    advance(one, two, coef_ref, 3, ROWS - 3, 0, False)
    advance(two, field, coef_ref, CHUNK, 2 * CHUNK, -HALO, True)
    early = pltpu.make_async_copy(
        field.at[:, CHUNK - HALO : 2 * CHUNK - HALO], early_ref, out_sems.at[2]
    )
    early.start()
    advance(two, field, coef_ref, HALO, CHUNK, -HALO, True)
    middle = 2 * CHUNK - HALO
    upper = pltpu.make_async_copy(field.at[:, :middle], inner_ref.at[:, :middle], out_sems.at[3])
    upper.start()
    advance(two, field, coef_ref, 2 * CHUNK, ROWS - HALO, -HALO, True)
    lower = pltpu.make_async_copy(field.at[:, middle:], inner_ref.at[:, middle:], out_sems.at[4])
    lower.start()
    early.wait()
    upper.wait()
    lower.wait()


def edge_kernel(
    parity_ref, core_ref, inner_ref, rim_ref, a_ref, b_ref, h_ref, v_ref, index_ref,
    same_ref, flip_ref, rest_ref, obs_ref, field, one, two, coef_ref, in_sem, out_sems,
):
    load = pltpu.make_async_copy(inner_ref, field.at[:, HALO : ROWS - HALO], in_sem)
    load.start()
    odd = parity_ref[0] == 1
    for side, (near_ref, far_ref, halo_at, own_at, own_first) in enumerate(
        ((a_ref, b_ref, 0, HALO, 0), (b_ref, a_ref, EDGE, 0, ROWS - EDGE))
    ):
        for i in range(HALO):
            halo = jnp.where(odd, near_ref[i], far_ref[i])
            one[halo_at + i] = halo[:OWN]
            coefficients(halo[OWN : OWN + 1], halo[OWN + 1 : OWN + 2], coef_ref, halo_at + i)
        for i in range(EDGE):
            one[own_at + i] = rim_ref[side, i]
            coefficients(
                h_ref[own_first + i : own_first + i + 1],
                v_ref[own_first + i : own_first + i + 1],
                coef_ref,
                own_at + i,
            )
        last = HALO + EDGE
        advance(one, two, coef_ref, 1, last - 1, 0, False)
        advance(two, one, coef_ref, 2, last - 2, 0, False)
        advance(one, two, coef_ref, 3, last - 3, 0, False)
        at = -HALO if side == 0 else ROWS - EDGE
        advance(two, field, coef_ref, HALO, EDGE, at, True)
    load.wait()
    stores = [
        pltpu.make_async_copy(
            field.at[:, first : first + count], rest_ref.at[:, to : to + count], out_sems.at[n]
        )
        for n, (first, count, to) in enumerate(
            ((0, CHUNK, 0), (2 * CHUNK, ROWS - 2 * CHUNK, CHUNK))
        )
    ]
    for store in stores:
        store.start()
    for g in range(GROUPS):
        for t in range(OBS // LANES):
            place = index_ref[g : g + 1, t * LANES : (t + 1) * LANES]
            row = jnp.broadcast_to(place >> 7, (OWN, LANES))
            col = jnp.broadcast_to(place & (LANES - 1), (OWN, LANES))
            total = jnp.zeros((OWN, LANES), jnp.float32)
            for i in range(ROWS):
                x = jnp.take_along_axis(field[g, i], col, axis=1, mode="promise_in_bounds")
                total = jnp.where(row == i, x, total)
            at = (g % 4) * OBS + t * LANES
            obs_ref[lax.rem(core_ref[0] + g // 4, 2), :, at : at + LANES] = total
    same_ref[...] = obs_ref[0]
    flip_ref[...] = obs_ref[1]
    for store in stores:
        store.wait()


def gram_kernel(mem_ref, *refs):
    *from_refs, value_ref, weight_ref, keep_ref, send_ref, obs_ref = refs
    mem = mem_ref[0]
    core = lax.rem(mem, 2)
    for (a, b), ref in zip(PATHS, from_refs):
        source = lax.rem(mem // 2 + 4 - a, 4) * 2 + lax.rem(core + b, 2)
        obs_ref[pl.ds(pl.multiple_of(source * OWN, OWN), OWN), :] = ref[...]
    obs = obs_ref[...]
    mean = jnp.sum(obs, axis=0, keepdims=True) * (1.0 / MEMBERS)
    anomalies = obs - mean
    weighted = split(anomalies * weight_ref[...])
    innovation = jnp.broadcast_to(value_ref[...] - mean, (8, HALF_OBS))
    nt = (((1,), (1,)), ((), ()))
    gram = dot3(split(anomalies), weighted, nt)
    drive = dot3(split(innovation), weighted, nt)
    half = MEMBERS // 2
    for c in range(2):

        @pl.when(core == c)
        def _():
            keep_ref[:half] = gram[c * half : (c + 1) * half]
            send_ref[:half] = gram[(1 - c) * half : (2 - c) * half]

    keep_ref[half:] = drive
    send_ref[half:] = drive


def weights_kernel(mem_ref, mine_ref, other_ref, out_ref, gram_ref):
    mem = mem_ref[0]
    core = lax.rem(mem, 2)
    half = MEMBERS // 2
    for c in range(2):

        @pl.when(core == c)
        def _():
            gram_ref[c * half : (c + 1) * half] = mine_ref[:half]
            gram_ref[(1 - c) * half : (2 - c) * half] = other_ref[:half]

    drive = mine_ref[half:]
    rows = lax.broadcasted_iota(jnp.int32, (MEMBERS, MEMBERS), 0)
    cols = lax.broadcasted_iota(jnp.int32, (MEMBERS, MEMBERS), 1)
    identity = (rows == cols).astype(jnp.float32)
    gram = gram_ref[...] + (MEMBERS - 1.0) * identity
    squares = jnp.sum(jnp.sum(gram * gram, axis=0, keepdims=True), axis=1, keepdims=True)
    scale = jnp.sqrt(squares)
    upper = gram / scale
    lower = 1.5 * identity - 0.5 * upper
    middle = lower
    for number in range(1, NS_ITERS):
        upper = mul(upper, middle)
        middle = 1.5 * identity - 0.5 * mul(lower, upper)
        lower = mul(middle, lower)
    lower_parts = split(lower)
    nt = (((1,), (1,)), ((), ()))
    inner = dot3(split(drive), lower_parts, nt)
    wbar = dot3(split(inner), lower_parts, nt)[:1] / scale
    weights = (MEMBERS - 1.0) ** 0.5 * lower / jnp.sqrt(scale) + wbar
    rest = (1.0 - jnp.sum(weights, axis=1, keepdims=True)) * (1.0 / MEMBERS)
    gram_ref[...] = weights + rest
    for n, (a, b) in enumerate(PATHS):
        place = lax.rem(mem // 2 + a, 4) * 2 + lax.rem(core + b, 2)
        high, low = split(gram_ref[pl.ds(pl.multiple_of(place * OWN, OWN), OWN), :])
        out_ref[n * OWN : (n + 1) * OWN] = high
        out_ref[MEMBERS + n * OWN : MEMBERS + (n + 1) * OWN] = low


def product_kernel(mem_ref, weights_ref, x_ref, *refs):
    members = refs[-1].shape[0]

    def compute(out_refs):
        weights = (weights_ref[:MEMBERS], weights_ref[MEMBERS:])
        flat = [ref.reshape(members * CHUNK, LANES) for ref in out_refs]
        for half in range(0, CHUNK, HALO):
            parts = [
                split(jnp.concatenate([x_ref[s, half + t] for s in range(N_MEM)], axis=0))
                for t in range(HALO)
            ]
            x = tuple(jnp.concatenate([p[n] for p in parts], axis=1) for n in range(2))
            y = dot3(weights, x)
            for t in range(HALO):
                for n, ref in enumerate(flat):
                    ref[pl.ds(half + t, members, stride=CHUNK), :] = y[
                        n * members : (n + 1) * members, t * LANES : (t + 1) * LANES
                    ]

    if len(refs) == 1:
        compute(refs)
    else:
        step = pl.program_id(0)

        @pl.when(step == 1)
        def _():
            for n, ref in enumerate(refs[1:]):
                ref[...] = refs[0][n * OWN : (n + 1) * OWN]

        pl.when(step != 1)(lambda: compute(refs[1:]))


def product(mem, weights, x, done):
    early = pl.BlockSpec((MEMBERS, CHUNK, LANES), lambda n, g: (0, 0, 0))
    outs = [pl.BlockSpec((OWN, CHUNK, LANES), lambda n, g: (0, n, 0))] * (N_MEM - 1)
    if done:
        own = pl.BlockSpec((OWN, CHUNK, LANES), lambda n, g: (0, n, g[0]))
        shapes = [f32(OWN, ROWS, WIDTH)] + [f32(OWN, ROWS, LANES)] * (N_MEM - 1)
        grid = (ROWS // CHUNK,)
    else:
        own, outs, shapes, grid = early, [], [f32(MEMBERS, CHUNK, LANES)], (1,)
    return pl.pallas_call(
        product_kernel,
        grid_spec=pltpu.PrefetchScalarGridSpec(
            num_scalar_prefetch=1,
            grid=grid,
            in_specs=[
                pl.BlockSpec((2 * MEMBERS, MEMBERS), lambda n, g: (0, 0)),
                pl.BlockSpec(
                    (N_MEM, CHUNK, OWN, LANES), lambda n, g: (0, jnp.maximum(n - 1, 0), 0, 0)
                ),
            ]
            + [early] * len(done),
            out_specs=[own] + outs,
        ),
        out_shape=shapes,
        compiler_params=params(20),
        cost_estimate=cost(4 if done else 2),
    )(mem, weights, x, *done)


def place_kernel(group_ref, x_ref, before_ref, out_ref):
    out_ref[...] = x_ref[...]


def place(x, group, before):
    return pl.pallas_call(
        place_kernel,
        grid_spec=pltpu.PrefetchScalarGridSpec(
            num_scalar_prefetch=1,
            grid=(1,),
            in_specs=[
                pl.BlockSpec((OWN, ROWS, LANES), lambda n, g: (0, 0, 0)),
                pl.BlockSpec(memory_space=pl.ANY),
            ],
            out_specs=pl.BlockSpec((OWN, ROWS, LANES), lambda n, g: (0, 0, g[0])),
        ),
        out_shape=f32(OWN, ROWS, WIDTH),
        input_output_aliases={2: 0},
        compiler_params=params(8),
        cost_estimate=cost(1),
    )(group, x, before)


def f32(*shape):
    return jax.ShapeDtypeStruct(shape, jnp.float32)


def send_on(x, a, b):
    return lax.ppermute(
        x, "mem", [(i, ((i // 2 + a) % 4) * 2 + (i + b) % 2) for i in range(N_MEM)]
    )


def swap(x, axis, bit):
    count = lax.axis_size(axis)
    return lax.ppermute(x, axis, [(i, i ^ bit) for i in range(count)])


def local(
    prior_samples, horizontal_flow_ratio, vertical_flow_ratio, obs_index, obs_value, obs_weight
):
    h, v = horizontal_flow_ratio, vertical_flow_ratio
    anywhere = pl.BlockSpec(memory_space=pl.ANY)
    mem = lax.axis_index("mem").astype(jnp.int32)
    core = (mem % 2).reshape(1)
    parity = (lax.axis_index("reg").astype(jnp.int32) % 2).reshape(1)
    sources = [
        (((mem // 2 - a) % 4) * 2 + (mem % 2 + b) % 2).reshape(1) for a, b in PATHS
    ]
    mem = mem.reshape(1)

    halo_a, halo_b = pl.pallas_call(
        pack_kernel,
        out_shape=[f32(HALO, OWN + SUB, WIDTH)] * 2,
        in_specs=[SMEM, anywhere, VMEM, VMEM],
        out_specs=[VMEM, VMEM],
        scratch_shapes=[
            pltpu.VMEM((2, GROUPS, OWN, SUB, LANES), jnp.float32),
            pltpu.SemaphoreType.DMA((2, GROUPS)),
        ],
        compiler_params=params(56),
    )(parity, prior_samples, h, v)
    halo_a, halo_b, prior_samples, h, v = lax.optimization_barrier(
        (halo_a, halo_b, prior_samples, h, v)
    )
    halo_b = lax.ppermute(
        halo_b, "reg", [(i, (i - 1 if i % 2 == 0 else i + 1) % N_REG) for i in range(N_REG)]
    )
    halo_a = lax.ppermute(halo_a, "reg", [(i, i ^ 1) for i in range(N_REG)])

    facts = jnp.concatenate([obs_index.astype(jnp.float32), obs_value, obs_weight], axis=0)
    facts = lax.all_to_all(
        jnp.broadcast_to(facts[None], (N_MEM, 3, OBS)), "mem", 0, 0, tiled=True
    )
    index = facts[:, 0].astype(jnp.int32)
    half_facts = lax.dynamic_slice_in_dim(facts, core[0] * 4, 4, axis=0)
    value = half_facts[:, 1].reshape(1, HALF_OBS)
    weight = half_facts[:, 2].reshape(1, HALF_OBS)

    inner, early, rim = pl.pallas_call(
        interior_kernel,
        out_shape=[
            f32(GROUPS, ROWS - EDGE, OWN, LANES),
            f32(GROUPS, CHUNK, OWN, LANES),
            f32(2, EDGE, OWN, WIDTH),
        ],
        in_specs=[anywhere, VMEM, VMEM],
        out_specs=[anywhere] * 3,
        scratch_shapes=[
            pltpu.VMEM((GROUPS, OWN * ROWS, LANES), jnp.float32),
            pltpu.VMEM((ROWS, OWN, WIDTH), jnp.float32),
            pltpu.VMEM((ROWS, OWN, WIDTH), jnp.float32),
            pltpu.VMEM((GROUPS, ROWS - EDGE, OWN, LANES), jnp.float32),
            pltpu.VMEM((2, ROWS, SUB, WIDTH), jnp.float32),
            pltpu.SemaphoreType.DMA((GROUPS,)),
            pltpu.SemaphoreType.DMA((5,)),
        ],
        compiler_params=params(56),
        cost_estimate=cost(17),
    )(prior_samples.reshape(OWN * ROWS, WIDTH), h, v)
    early, halo_a, halo_b = lax.optimization_barrier((early, halo_a, halo_b))
    early = lax.all_to_all(early, "mem", 0, 0, tiled=True)
    same, flip, rest = pl.pallas_call(
        edge_kernel,
        out_shape=[
            f32(OWN, HALF_OBS),
            f32(OWN, HALF_OBS),
            f32(GROUPS, ROWS - CHUNK, OWN, LANES),
        ],
        in_specs=[SMEM, SMEM, anywhere] + [VMEM] * 6,
        out_specs=[VMEM, VMEM, anywhere],
        scratch_shapes=[
            pltpu.VMEM((2, OWN, HALF_OBS), jnp.float32),
            pltpu.VMEM((GROUPS, ROWS, OWN, LANES), jnp.float32),
            pltpu.VMEM((HALO + EDGE, OWN, WIDTH), jnp.float32),
            pltpu.VMEM((HALO + EDGE, OWN, WIDTH), jnp.float32),
            pltpu.VMEM((2, HALO + EDGE, SUB, WIDTH), jnp.float32),
            pltpu.SemaphoreType.DMA,
            pltpu.SemaphoreType.DMA((2,)),
        ],
        compiler_params=params(56),
        cost_estimate=cost(13),
    )(parity, core, inner, rim, halo_a, halo_b, h, v, index)
    obs = [same] + [send_on(flip if b else same, a, b) for a, b in PATHS[1:]]
    early, *obs = lax.optimization_barrier((early, *obs))

    keep, send = pl.pallas_call(
        gram_kernel,
        out_shape=[f32(MEMBERS // 2 + 8, MEMBERS)] * 2,
        in_specs=[SMEM] + [VMEM] * (N_MEM + 2),
        out_specs=[VMEM, VMEM],
        scratch_shapes=[pltpu.VMEM((MEMBERS, HALF_OBS), jnp.float32)],
        compiler_params=params(12),
        cost_estimate=cost(3),
    )(mem, *obs, value, weight)
    rest, send = lax.optimization_barrier((rest, send))
    rest = lax.all_to_all(rest, "mem", 0, 0, tiled=True)
    total = keep + swap(send, "mem", 1)
    for bit in (1, 2, 4, 8):
        total = total + swap(total, "reg", bit)
    other = swap(total, "mem", 1)

    weights = pl.pallas_call(
        weights_kernel,
        out_shape=jax.ShapeDtypeStruct((2 * MEMBERS, MEMBERS), jnp.bfloat16),
        in_specs=[SMEM, VMEM, VMEM],
        out_specs=VMEM,
        scratch_shapes=[pltpu.VMEM((MEMBERS, MEMBERS), jnp.float32)],
        compiler_params=params(16),
        cost_estimate=cost(6),
    )(mem, total, other)

    analysis = product(mem, weights, early, [])
    result, *analysis = product(mem, weights, rest, analysis)
    for x, (a, b), source in zip(analysis, PATHS[1:], sources[1:]):
        arrived = send_on(x, a, b)
        result = place(arrived, source, result)
    return result


def solution(mesh):
    placed = (
        P("mem", "reg", None),
        P("reg", None),
        P("reg", None),
        P("reg", "mem"),
        P("reg", "mem"),
        P("reg", "mem"),
    )
    return jax.shard_map(
        local, mesh=mesh, in_specs=placed, out_specs=P("mem", "reg", None), check_vma=False
    )
```

```python
import functools

import jax
import jax.numpy as jnp
from jax import lax
from jax.experimental import pallas as pl
from jax.experimental.pallas import tpu as pltpu
from jax.sharding import PartitionSpec as P

SECTIONS = 4
NS_ITERS = 6
MEMBERS = 256
N_MEM = 8
N_REG = 16
OWN = MEMBERS // N_MEM
ROWS = 32
WIDTH = 1024
LANES = 128
GROUPS = WIDTH // LANES
OBS = 256
HALF_OBS = OBS * GROUPS // 2
HALO = SECTIONS
EDGE = 2 * HALO
CHUNK = 8
SUB = 8
PATHS = ((0, 0), (2, 0), (1, 0), (3, 0), (2, 1), (1, 1), (3, 1), (0, 1))
VMEM = pl.BlockSpec(memory_space=pltpu.VMEM)
SMEM = pl.BlockSpec(memory_space=pltpu.SMEM)


def params(mib):
    return pltpu.CompilerParams(vmem_limit_bytes=mib * 1024 * 1024)


def cost(us):
    return pl.CostEstimate(flops=0, bytes_accessed=us * 3_000_000, transcendentals=0)


def split(x):
    high = x.astype(jnp.bfloat16)
    return high, (x - high.astype(jnp.float32)).astype(jnp.bfloat16)


def dot3(a, b, dims=(((1,), (0,)), ((), ()))):
    dot = functools.partial(
        lax.dot_general, dimension_numbers=dims, preferred_element_type=jnp.float32
    )
    return dot(a[0], b[0]) + (dot(a[0], b[1]) + dot(a[1], b[0]))


def mul(a, b):
    return dot3(split(a), split(b))


def coefficients(h, v, coef_ref, i):
    coef_ref[0, i] = jnp.broadcast_to(h, (SUB, WIDTH))
    coef_ref[1, i] = jnp.broadcast_to(v, (SUB, WIDTH))


def advance(src, dst, coef_ref, first, last, at, grouped):
    lane = lax.broadcasted_iota(jnp.int32, (SUB, LANES), 1)

    def tile(i, m):
        def read(row, j):
            return src[row, m : m + SUB, j * LANES : (j + 1) * LANES]

        middle = [read(i, j) for j in range(GROUPS)]
        right = [pltpu.roll(x, 1, 1) for x in middle]
        left = [pltpu.roll(x, LANES - 1, 1) for x in middle]
        results = []
        for j in range(GROUPS):
            h = coef_ref[0, i, :, j * LANES : (j + 1) * LANES]
            v = coef_ref[1, i, :, j * LANES : (j + 1) * LANES]
            side = jnp.where(
                h > 0.0,
                jnp.where(lane == 0, right[j - 1], right[j]),
                jnp.where(lane == LANES - 1, left[(j + 1) % GROUPS], left[j]),
            )
            below = jnp.where(v > 0.0, read(i - 1, j), read(i + 1, j))
            ah, av = jnp.abs(h), jnp.abs(v)
            results.append((1.0 - ah - av) * middle[j] + ah * side + av * below)
        for j, x in enumerate(results):
            if grouped:
                dst[j, i + at, m : m + SUB] = x
            else:
                dst[i + at, m : m + SUB, j * LANES : (j + 1) * LANES] = x

    def body(n, carry):
        start = jnp.minimum(first + n * HALO, last - HALO)
        for q in range(HALO):
            for m in range(0, OWN, SUB):
                tile(start + q, m)
        return carry

    lax.fori_loop(0, -(-(last - first) // HALO), body, 0)


def pack_kernel(parity_ref, prior_ref, h_ref, v_ref, a_ref, b_ref, given, sems):
    copies = []
    for side in range(2):
        rows = slice(side * (ROWS - SUB), side * (ROWS - SUB) + SUB)
        copies.append(
            [
                pltpu.make_async_copy(
                    prior_ref.at[:, rows, j * LANES : (j + 1) * LANES],
                    given.at[side, j],
                    sems.at[side, j],
                )
                for j in range(GROUPS)
            ]
        )
    for j in range(GROUPS):
        for side in range(2):
            copies[side][j].start()
    for side in range(2):
        for copy in copies[side]:
            copy.wait()
    parity = parity_ref[0]
    for even in range(2):

        @pl.when(parity == 1 - even)
        def _():
            for side in range(2):
                out_ref = a_ref if side == even else b_ref
                first = side * (ROWS - HALO)
                for i in range(HALO):
                    for j in range(GROUPS):
                        x = given.at[side, j].reshape(OWN * SUB, LANES)[
                            pl.ds(side * (SUB - HALO) + i, OWN, stride=SUB), :
                        ]
                        out_ref[i, :OWN, j * LANES : (j + 1) * LANES] = x
                    out_ref[i, OWN : OWN + 1] = h_ref[first + i : first + i + 1]
                    out_ref[i, OWN + 1 : OWN + 2] = v_ref[first + i : first + i + 1]


def interior_kernel(
    prior_ref, h_ref, v_ref,
    inner_ref, early_ref, rim_ref, given, one, two, field, coef_ref, sems, out_sems,
):
    copies = [
        pltpu.make_async_copy(
            prior_ref.at[:, j * LANES : (j + 1) * LANES], given.at[j], sems.at[j]
        )
        for j in range(GROUPS)
    ]
    for copy in copies:
        copy.start()
    for i in range(ROWS):
        coefficients(h_ref[i : i + 1], v_ref[i : i + 1], coef_ref, i)
    for j in range(GROUPS):
        at = slice(j * LANES, (j + 1) * LANES)
        copies[j].wait()
        for i in range(ROWS):
            one[i, :, at] = given[j, pl.ds(i, OWN, stride=ROWS), :]
    rims = [
        pltpu.make_async_copy(
            one.at[side * (ROWS - EDGE) : side * (ROWS - EDGE) + EDGE],
            rim_ref.at[side],
            out_sems.at[side],
        )
        for side in range(2)
    ]
    for copy in rims:
        copy.start()
    advance(one, two, coef_ref, 1, ROWS - 1, 0, False)
    for copy in rims:
        copy.wait()
    advance(two, one, coef_ref, 2, ROWS - 2, 0, False)
    advance(one, two, coef_ref, 3, ROWS - 3, 0, False)
    advance(two, field, coef_ref, CHUNK, 2 * CHUNK, -HALO, True)
    early = pltpu.make_async_copy(
        field.at[:, CHUNK - HALO : 2 * CHUNK - HALO], early_ref, out_sems.at[2]
    )
    early.start()
    advance(two, field, coef_ref, HALO, CHUNK, -HALO, True)
    middle = 2 * CHUNK - HALO
    upper = pltpu.make_async_copy(field.at[:, :middle], inner_ref.at[:, :middle], out_sems.at[3])
    upper.start()
    advance(two, field, coef_ref, 2 * CHUNK, ROWS - HALO, -HALO, True)
    lower = pltpu.make_async_copy(field.at[:, middle:], inner_ref.at[:, middle:], out_sems.at[4])
    lower.start()
    early.wait()
    upper.wait()
    lower.wait()


def edge_kernel(
    parity_ref, core_ref, inner_ref, rim_ref, a_ref, b_ref, h_ref, v_ref, facts_ref,
    same_ref, flip_ref, rest_ref, obs_ref, field, one, two, coef_ref, in_sem, out_sems,
):
    load = pltpu.make_async_copy(inner_ref, field.at[:, HALO : ROWS - HALO], in_sem)
    load.start()
    odd = parity_ref[0] == 1
    for side, (near_ref, far_ref, halo_at, own_at, own_first) in enumerate(
        ((a_ref, b_ref, 0, HALO, 0), (b_ref, a_ref, EDGE, 0, ROWS - EDGE))
    ):
        for i in range(HALO):
            halo = jnp.where(odd, near_ref[i], far_ref[i])
            one[halo_at + i] = halo[:OWN]
            coefficients(halo[OWN : OWN + 1], halo[OWN + 1 : OWN + 2], coef_ref, halo_at + i)
        for i in range(EDGE):
            one[own_at + i] = rim_ref[side, i]
            coefficients(
                h_ref[own_first + i : own_first + i + 1],
                v_ref[own_first + i : own_first + i + 1],
                coef_ref,
                own_at + i,
            )
        last = HALO + EDGE
        advance(one, two, coef_ref, 1, last - 1, 0, False)
        advance(two, one, coef_ref, 2, last - 2, 0, False)
        advance(one, two, coef_ref, 3, last - 3, 0, False)
        at = -HALO if side == 0 else ROWS - EDGE
        advance(two, field, coef_ref, HALO, EDGE, at, True)
    load.wait()
    stores = [
        pltpu.make_async_copy(
            field.at[:, first : first + count], rest_ref.at[:, to : to + count], out_sems.at[n]
        )
        for n, (first, count, to) in enumerate(
            ((0, CHUNK, 0), (2 * CHUNK, ROWS - 2 * CHUNK, CHUNK))
        )
    ]
    for store in stores:
        store.start()
    for g in range(GROUPS):
        for t in range(OBS // LANES):
            place = facts_ref[g, :1, t * LANES : (t + 1) * LANES].astype(jnp.int32)
            row = jnp.broadcast_to(place >> 7, (OWN, LANES))
            col = jnp.broadcast_to(place & (LANES - 1), (OWN, LANES))
            total = jnp.zeros((OWN, LANES), jnp.float32)
            for i in range(ROWS):
                x = jnp.take_along_axis(field[g, i], col, axis=1, mode="promise_in_bounds")
                total = jnp.where(row == i, x, total)
            at = (g % 4) * OBS + t * LANES
            obs_ref[lax.rem(core_ref[0] + g // 4, 2), :, at : at + LANES] = total
    same_ref[...] = obs_ref[0]
    flip_ref[...] = obs_ref[1]
    for store in stores:
        store.wait()


def gram_kernel(mem_ref, *refs):
    *from_refs, facts_ref, keep_ref, send_ref, obs_ref = refs
    mem = mem_ref[0]
    core = lax.rem(mem, 2)
    for (a, b), ref in zip(PATHS, from_refs):
        source = lax.rem(mem // 2 + 4 - a, 4) * 2 + lax.rem(core + b, 2)
        obs_ref[pl.ds(pl.multiple_of(source * OWN, OWN), OWN), :] = ref[...]
    obs = obs_ref[...]
    facts = jnp.concatenate([facts_ref[4 * core + q] for q in range(4)], axis=1)
    mean = jnp.sum(obs, axis=0, keepdims=True) * (1.0 / MEMBERS)
    anomalies = obs - mean
    weighted = split(anomalies * facts[2:3])
    innovation = jnp.broadcast_to(facts[1:2] - mean, (8, HALF_OBS))
    nt = (((1,), (1,)), ((), ()))
    gram = dot3(split(anomalies), weighted, nt)
    drive = dot3(split(innovation), weighted, nt)
    half = MEMBERS // 2
    for c in range(2):

        @pl.when(core == c)
        def _():
            keep_ref[:half] = gram[c * half : (c + 1) * half]
            send_ref[:half] = gram[(1 - c) * half : (2 - c) * half]

    keep_ref[half:] = drive
    send_ref[half:] = drive


def weights_kernel(mem_ref, mine_ref, other_ref, out_ref, gram_ref):
    mem = mem_ref[0]
    core = lax.rem(mem, 2)
    half = MEMBERS // 2
    for c in range(2):

        @pl.when(core == c)
        def _():
            gram_ref[c * half : (c + 1) * half] = mine_ref[:half]
            gram_ref[(1 - c) * half : (2 - c) * half] = other_ref[:half]

    drive = mine_ref[half:]
    rows = lax.broadcasted_iota(jnp.int32, (MEMBERS, MEMBERS), 0)
    cols = lax.broadcasted_iota(jnp.int32, (MEMBERS, MEMBERS), 1)
    identity = (rows == cols).astype(jnp.float32)
    gram = gram_ref[...] + (MEMBERS - 1.0) * identity
    squares = jnp.sum(jnp.sum(gram * gram, axis=0, keepdims=True), axis=1, keepdims=True)
    scale = jnp.sqrt(squares)
    upper = gram / scale
    lower = 1.5 * identity - 0.5 * upper
    middle = lower
    for number in range(1, NS_ITERS):
        upper = mul(upper, middle)
        middle = 1.5 * identity - 0.5 * mul(lower, upper)
        lower = mul(middle, lower)
    lower_parts = split(lower)
    nt = (((1,), (1,)), ((), ()))
    inner = dot3(split(drive), lower_parts, nt)
    wbar = dot3(split(inner), lower_parts, nt)[:1] / scale
    weights = (MEMBERS - 1.0) ** 0.5 * lower / jnp.sqrt(scale) + wbar
    rest = (1.0 - jnp.sum(weights, axis=1, keepdims=True)) * (1.0 / MEMBERS)
    gram_ref[...] = weights + rest
    for n, (a, b) in enumerate(PATHS):
        place = lax.rem(mem // 2 + a, 4) * 2 + lax.rem(core + b, 2)
        high, low = split(gram_ref[pl.ds(pl.multiple_of(place * OWN, OWN), OWN), :])
        out_ref[0, n * OWN : (n + 1) * OWN] = high
        out_ref[1, n * OWN : (n + 1) * OWN] = low


def product_kernel(mem_ref, weights_ref, early_ref, rest_ref, *out_refs):
    flat = [ref.reshape(OWN * CHUNK, LANES) for ref in out_refs]

    def compute(x_ref):
        weights = (weights_ref[0], weights_ref[1])
        for half in range(0, CHUNK, HALO):
            parts = [
                split(jnp.concatenate([x_ref[s, half + t] for s in range(N_MEM)], axis=0))
                for t in range(HALO)
            ]
            x = tuple(jnp.concatenate([p[n] for p in parts], axis=1) for n in range(2))
            y = dot3(weights, x)
            for t in range(HALO):
                for n, ref in enumerate(flat):
                    ref[pl.ds(half + t, OWN, stride=CHUNK), :] = y[
                        n * OWN : (n + 1) * OWN, t * LANES : (t + 1) * LANES
                    ]

    step = pl.program_id(0)
    pl.when(step == 1)(lambda: compute(early_ref))
    pl.when(step != 1)(lambda: compute(rest_ref))


def product(mem, weights, early, rest, part):
    outs = [pl.BlockSpec((OWN, CHUNK, LANES), lambda n, g: (0, n, 0))] * (N_MEM // 2)
    shapes = [f32(OWN, ROWS, LANES)] * (N_MEM // 2)
    if part == 0:
        outs[0] = pl.BlockSpec((OWN, CHUNK, LANES), lambda n, g: (0, n, g[0]))
        shapes[0] = f32(OWN, ROWS, WIDTH)
    block = (N_MEM, CHUNK, OWN, LANES)
    return pl.pallas_call(
        product_kernel,
        grid_spec=pltpu.PrefetchScalarGridSpec(
            num_scalar_prefetch=1,
            grid=(ROWS // CHUNK,),
            in_specs=[
                pl.BlockSpec((2, MEMBERS // 2, MEMBERS), lambda n, g: (0, part, 0)),
                pl.BlockSpec(block, lambda n, g: (0, 0, 0, 0)),
                pl.BlockSpec(block, lambda n, g: (0, jnp.maximum(n - 1, 0), 0, 0)),
            ],
            out_specs=outs,
        ),
        out_shape=shapes,
        compiler_params=params(16),
        cost_estimate=cost(3),
    )(mem, weights, early, rest)


def place_kernel(group_ref, x_ref, before_ref, out_ref):
    out_ref[...] = x_ref[...]


def place(x, group, before):
    return pl.pallas_call(
        place_kernel,
        grid_spec=pltpu.PrefetchScalarGridSpec(
            num_scalar_prefetch=1,
            grid=(1,),
            in_specs=[
                pl.BlockSpec((OWN, ROWS, LANES), lambda n, g: (0, 0, 0)),
                pl.BlockSpec(memory_space=pl.ANY),
            ],
            out_specs=pl.BlockSpec((OWN, ROWS, LANES), lambda n, g: (0, 0, g[0])),
        ),
        out_shape=f32(OWN, ROWS, WIDTH),
        input_output_aliases={2: 0},
        compiler_params=params(8),
        cost_estimate=cost(1),
    )(group, x, before)


def f32(*shape):
    return jax.ShapeDtypeStruct(shape, jnp.float32)


def send_on(x, a, b):
    return lax.ppermute(
        x, "mem", [(i, ((i // 2 + a) % 4) * 2 + (i + b) % 2) for i in range(N_MEM)]
    )


def swap(x, axis, bit):
    count = lax.axis_size(axis)
    return lax.ppermute(x, axis, [(i, i ^ bit) for i in range(count)])


def local(
    prior_samples, horizontal_flow_ratio, vertical_flow_ratio, obs_index, obs_value, obs_weight
):
    h, v = horizontal_flow_ratio, vertical_flow_ratio
    anywhere = pl.BlockSpec(memory_space=pl.ANY)
    mem = lax.axis_index("mem").astype(jnp.int32)
    core = (mem % 2).reshape(1)
    parity = (lax.axis_index("reg").astype(jnp.int32) % 2).reshape(1)
    sources = [
        (((mem // 2 - a) % 4) * 2 + (mem % 2 + b) % 2).reshape(1) for a, b in PATHS
    ]
    mem = mem.reshape(1)

    halo_a, halo_b = pl.pallas_call(
        pack_kernel,
        out_shape=[f32(HALO, OWN + SUB, WIDTH)] * 2,
        in_specs=[SMEM, anywhere, VMEM, VMEM],
        out_specs=[VMEM, VMEM],
        scratch_shapes=[
            pltpu.VMEM((2, GROUPS, OWN, SUB, LANES), jnp.float32),
            pltpu.SemaphoreType.DMA((2, GROUPS)),
        ],
        compiler_params=params(56),
    )(parity, prior_samples, h, v)
    halo_a, halo_b, prior_samples, h, v = lax.optimization_barrier(
        (halo_a, halo_b, prior_samples, h, v)
    )
    halo_b = lax.ppermute(
        halo_b, "reg", [(i, (i - 1 if i % 2 == 0 else i + 1) % N_REG) for i in range(N_REG)]
    )
    halo_a = lax.ppermute(halo_a, "reg", [(i, i ^ 1) for i in range(N_REG)])

    facts = jnp.concatenate(
        [obs_index.astype(jnp.float32), obs_value, obs_weight, jnp.zeros((SUB - 3, OBS))], axis=0
    )
    facts = lax.all_to_all(
        jnp.broadcast_to(facts[None], (N_MEM, SUB, OBS)), "mem", 0, 0, tiled=True
    )

    inner, early, rim = pl.pallas_call(
        interior_kernel,
        out_shape=[
            f32(GROUPS, ROWS - EDGE, OWN, LANES),
            f32(GROUPS, CHUNK, OWN, LANES),
            f32(2, EDGE, OWN, WIDTH),
        ],
        in_specs=[anywhere, VMEM, VMEM],
        out_specs=[anywhere] * 3,
        scratch_shapes=[
            pltpu.VMEM((GROUPS, OWN * ROWS, LANES), jnp.float32),
            pltpu.VMEM((ROWS, OWN, WIDTH), jnp.float32),
            pltpu.VMEM((ROWS, OWN, WIDTH), jnp.float32),
            pltpu.VMEM((GROUPS, ROWS - EDGE, OWN, LANES), jnp.float32),
            pltpu.VMEM((2, ROWS, SUB, WIDTH), jnp.float32),
            pltpu.SemaphoreType.DMA((GROUPS,)),
            pltpu.SemaphoreType.DMA((5,)),
        ],
        compiler_params=params(56),
        cost_estimate=cost(17),
    )(prior_samples.reshape(OWN * ROWS, WIDTH), h, v)
    early, halo_a, halo_b = lax.optimization_barrier((early, halo_a, halo_b))
    early = lax.all_to_all(early, "mem", 0, 0, tiled=True)
    same, flip, rest = pl.pallas_call(
        edge_kernel,
        out_shape=[
            f32(OWN, HALF_OBS),
            f32(OWN, HALF_OBS),
            f32(GROUPS, ROWS - CHUNK, OWN, LANES),
        ],
        in_specs=[SMEM, SMEM, anywhere] + [VMEM] * 6,
        out_specs=[VMEM, VMEM, anywhere],
        scratch_shapes=[
            pltpu.VMEM((2, OWN, HALF_OBS), jnp.float32),
            pltpu.VMEM((GROUPS, ROWS, OWN, LANES), jnp.float32),
            pltpu.VMEM((HALO + EDGE, OWN, WIDTH), jnp.float32),
            pltpu.VMEM((HALO + EDGE, OWN, WIDTH), jnp.float32),
            pltpu.VMEM((2, HALO + EDGE, SUB, WIDTH), jnp.float32),
            pltpu.SemaphoreType.DMA,
            pltpu.SemaphoreType.DMA((2,)),
        ],
        compiler_params=params(56),
        cost_estimate=cost(13),
    )(parity, core, inner, rim, halo_a, halo_b, h, v, facts)
    obs = [same] + [send_on(flip if b else same, a, b) for a, b in PATHS[1:]]
    early, rest, *obs = lax.optimization_barrier((early, rest, *obs))
    rest = lax.all_to_all(rest, "mem", 0, 0, tiled=True)

    keep, send = pl.pallas_call(
        gram_kernel,
        out_shape=[f32(MEMBERS // 2 + 8, MEMBERS)] * 2,
        in_specs=[SMEM] + [VMEM] * (N_MEM + 1),
        out_specs=[VMEM, VMEM],
        scratch_shapes=[pltpu.VMEM((MEMBERS, HALF_OBS), jnp.float32)],
        compiler_params=params(12),
        cost_estimate=cost(3),
    )(mem, *obs, facts)
    total = keep + swap(send, "mem", 1)
    for bit in (1, 2, 4, 8):
        total = total + swap(total, "reg", bit)
    other = swap(total, "mem", 1)

    weights = pl.pallas_call(
        weights_kernel,
        out_shape=jax.ShapeDtypeStruct((2, MEMBERS, MEMBERS), jnp.bfloat16),
        in_specs=[SMEM, VMEM, VMEM],
        out_specs=VMEM,
        scratch_shapes=[pltpu.VMEM((MEMBERS, MEMBERS), jnp.float32)],
        compiler_params=params(16),
        cost_estimate=cost(6),
    )(mem, total, other)

    result, *analysis = product(mem, weights, early, rest, 0)
    analysis = analysis + list(product(mem, weights, early, rest, 1))
    for x, (a, b), source in zip(analysis, PATHS[1:], sources[1:]):
        arrived = send_on(x, a, b)
        result = place(arrived, source, result)
    return result


def solution(mesh):
    placed = (
        P("mem", "reg", None),
        P("reg", None),
        P("reg", None),
        P("reg", "mem"),
        P("reg", "mem"),
        P("reg", "mem"),
    )
    return jax.shard_map(
        local, mesh=mesh, in_specs=placed, out_specs=P("mem", "reg", None), check_vma=False
    )
```

```python
import functools

import jax
import jax.numpy as jnp
from jax import lax
from jax.experimental import pallas as pl
from jax.experimental.pallas import tpu as pltpu
from jax.sharding import PartitionSpec as P

SECTIONS = 4
NS_ITERS = 6
MEMBERS = 256
N_MEM = 8
N_REG = 16
OWN = MEMBERS // N_MEM
ROWS = 32
WIDTH = 1024
LANES = 128
GROUPS = WIDTH // LANES
OBS = 256
HALF_OBS = OBS * GROUPS // 2
HALO = SECTIONS
EDGE = 2 * HALO
CHUNK = 8
SUB = 8
PATHS = ((0, 0), (2, 0), (1, 0), (3, 0), (2, 1), (1, 1), (3, 1), (0, 1))
VMEM = pl.BlockSpec(memory_space=pltpu.VMEM)
SMEM = pl.BlockSpec(memory_space=pltpu.SMEM)


def params(mib):
    return pltpu.CompilerParams(vmem_limit_bytes=mib * 1024 * 1024)


def cost(us):
    return pl.CostEstimate(flops=0, bytes_accessed=us * 3_000_000, transcendentals=0)


def split(x):
    high = x.astype(jnp.bfloat16)
    return high, (x - high.astype(jnp.float32)).astype(jnp.bfloat16)


def dot3(a, b, dims=(((1,), (0,)), ((), ()))):
    dot = functools.partial(
        lax.dot_general, dimension_numbers=dims, preferred_element_type=jnp.float32
    )
    return dot(a[0], b[0]) + (dot(a[0], b[1]) + dot(a[1], b[0]))


def mul(a, b):
    return dot3(split(a), split(b))


def coefficients(h, v, coef_ref, i):
    coef_ref[0, i] = jnp.broadcast_to(h, (SUB, WIDTH))
    coef_ref[1, i] = jnp.broadcast_to(v, (SUB, WIDTH))


def advance(src, dst, coef_ref, first, last, at, grouped):
    lane = lax.broadcasted_iota(jnp.int32, (SUB, LANES), 1)

    def tile(i, m):
        def read(row, j):
            return src[row, m : m + SUB, j * LANES : (j + 1) * LANES]

        middle = [read(i, j) for j in range(GROUPS)]
        right = [pltpu.roll(x, 1, 1) for x in middle]
        left = [pltpu.roll(x, LANES - 1, 1) for x in middle]
        results = []
        for j in range(GROUPS):
            h = coef_ref[0, i, :, j * LANES : (j + 1) * LANES]
            v = coef_ref[1, i, :, j * LANES : (j + 1) * LANES]
            side = jnp.where(
                h > 0.0,
                jnp.where(lane == 0, right[j - 1], right[j]),
                jnp.where(lane == LANES - 1, left[(j + 1) % GROUPS], left[j]),
            )
            below = jnp.where(v > 0.0, read(i - 1, j), read(i + 1, j))
            ah, av = jnp.abs(h), jnp.abs(v)
            results.append((1.0 - ah - av) * middle[j] + ah * side + av * below)
        for j, x in enumerate(results):
            if grouped:
                dst[j, i + at, m : m + SUB] = x
            else:
                dst[i + at, m : m + SUB, j * LANES : (j + 1) * LANES] = x

    def body(n, carry):
        start = jnp.minimum(first + n * HALO, last - HALO)
        for q in range(HALO):
            for m in range(0, OWN, SUB):
                tile(start + q, m)
        return carry

    lax.fori_loop(0, -(-(last - first) // HALO), body, 0)


def pack_kernel(parity_ref, prior_ref, h_ref, v_ref, a_ref, b_ref, given, sems):
    copies = []
    for side in range(2):
        rows = slice(side * (ROWS - SUB), side * (ROWS - SUB) + SUB)
        copies.append(
            [
                pltpu.make_async_copy(
                    prior_ref.at[:, rows, j * LANES : (j + 1) * LANES],
                    given.at[side, j],
                    sems.at[side, j],
                )
                for j in range(GROUPS)
            ]
        )
    for j in range(GROUPS):
        for side in range(2):
            copies[side][j].start()
    for side in range(2):
        for copy in copies[side]:
            copy.wait()
    parity = parity_ref[0]
    for even in range(2):

        @pl.when(parity == 1 - even)
        def _():
            for side in range(2):
                out_ref = a_ref if side == even else b_ref
                first = side * (ROWS - HALO)
                for i in range(HALO):
                    for j in range(GROUPS):
                        x = given.at[side, j].reshape(OWN * SUB, LANES)[
                            pl.ds(side * (SUB - HALO) + i, OWN, stride=SUB), :
                        ]
                        out_ref[i, :OWN, j * LANES : (j + 1) * LANES] = x
                    out_ref[i, OWN : OWN + 1] = h_ref[first + i : first + i + 1]
                    out_ref[i, OWN + 1 : OWN + 2] = v_ref[first + i : first + i + 1]


def interior_kernel(
    prior_ref, h_ref, v_ref,
    inner_ref, early_ref, rim_ref, given, one, two, field, coef_ref, sems, out_sems,
):
    copies = [
        pltpu.make_async_copy(
            prior_ref.at[:, j * LANES : (j + 1) * LANES], given.at[j], sems.at[j]
        )
        for j in range(GROUPS)
    ]
    for copy in copies:
        copy.start()
    for i in range(ROWS):
        coefficients(h_ref[i : i + 1], v_ref[i : i + 1], coef_ref, i)
    for j in range(GROUPS):
        at = slice(j * LANES, (j + 1) * LANES)
        copies[j].wait()
        for i in range(ROWS):
            one[i, :, at] = given[j, pl.ds(i, OWN, stride=ROWS), :]
    rims = [
        pltpu.make_async_copy(
            one.at[side * (ROWS - EDGE) : side * (ROWS - EDGE) + EDGE],
            rim_ref.at[side],
            out_sems.at[side],
        )
        for side in range(2)
    ]
    for copy in rims:
        copy.start()
    advance(one, two, coef_ref, 1, ROWS - 1, 0, False)
    for copy in rims:
        copy.wait()
    advance(two, one, coef_ref, 2, ROWS - 2, 0, False)
    advance(one, two, coef_ref, 3, ROWS - 3, 0, False)
    advance(two, field, coef_ref, CHUNK, 2 * CHUNK, -HALO, True)
    early = pltpu.make_async_copy(
        field.at[:, CHUNK - HALO : 2 * CHUNK - HALO], early_ref, out_sems.at[2]
    )
    early.start()
    advance(two, field, coef_ref, HALO, CHUNK, -HALO, True)
    middle = 2 * CHUNK - HALO
    upper = pltpu.make_async_copy(field.at[:, :middle], inner_ref.at[:, :middle], out_sems.at[3])
    upper.start()
    advance(two, field, coef_ref, 2 * CHUNK, ROWS - HALO, -HALO, True)
    lower = pltpu.make_async_copy(field.at[:, middle:], inner_ref.at[:, middle:], out_sems.at[4])
    lower.start()
    early.wait()
    upper.wait()
    lower.wait()


def edge_kernel(
    parity_ref, core_ref, inner_ref, rim_ref, a_ref, b_ref, h_ref, v_ref, facts_ref,
    same_ref, flip_ref, rest_ref, obs_ref, field, one, two, coef_ref, in_sem, out_sems,
):
    load = pltpu.make_async_copy(inner_ref, field.at[:, HALO : ROWS - HALO], in_sem)
    load.start()
    odd = parity_ref[0] == 1
    for side, (near_ref, far_ref, halo_at, own_at, own_first) in enumerate(
        ((a_ref, b_ref, 0, HALO, 0), (b_ref, a_ref, EDGE, 0, ROWS - EDGE))
    ):
        for i in range(HALO):
            halo = jnp.where(odd, near_ref[i], far_ref[i])
            one[halo_at + i] = halo[:OWN]
            coefficients(halo[OWN : OWN + 1], halo[OWN + 1 : OWN + 2], coef_ref, halo_at + i)
        for i in range(EDGE):
            one[own_at + i] = rim_ref[side, i]
            coefficients(
                h_ref[own_first + i : own_first + i + 1],
                v_ref[own_first + i : own_first + i + 1],
                coef_ref,
                own_at + i,
            )
        last = HALO + EDGE
        advance(one, two, coef_ref, 1, last - 1, 0, False)
        advance(two, one, coef_ref, 2, last - 2, 0, False)
        advance(one, two, coef_ref, 3, last - 3, 0, False)
        at = -HALO if side == 0 else ROWS - EDGE
        advance(two, field, coef_ref, HALO, EDGE, at, True)
    load.wait()
    stores = [
        pltpu.make_async_copy(
            field.at[:, first : first + count], rest_ref.at[:, to : to + count], out_sems.at[n]
        )
        for n, (first, count, to) in enumerate(
            ((0, CHUNK, 0), (2 * CHUNK, ROWS - 2 * CHUNK, CHUNK))
        )
    ]
    for store in stores:
        store.start()
    for g in range(GROUPS):
        for t in range(OBS // LANES):
            place = facts_ref[g, :1, t * LANES : (t + 1) * LANES].astype(jnp.int32)
            row = jnp.broadcast_to(place >> 7, (OWN, LANES))
            col = jnp.broadcast_to(place & (LANES - 1), (OWN, LANES))
            total = jnp.zeros((OWN, LANES), jnp.float32)
            for i in range(ROWS):
                x = jnp.take_along_axis(field[g, i], col, axis=1, mode="promise_in_bounds")
                total = jnp.where(row == i, x, total)
            at = (g % 4) * OBS + t * LANES
            obs_ref[lax.rem(core_ref[0] + g // 4, 2), :, at : at + LANES] = total
    same_ref[...] = obs_ref[0]
    flip_ref[...] = obs_ref[1]
    for store in stores:
        store.wait()


def gram_kernel(mem_ref, *refs):
    *from_refs, facts_ref, keep_ref, send_ref, obs_ref = refs
    mem = mem_ref[0]
    core = lax.rem(mem, 2)
    for (a, b), ref in zip(PATHS, from_refs):
        source = lax.rem(mem // 2 + 4 - a, 4) * 2 + lax.rem(core + b, 2)
        obs_ref[pl.ds(pl.multiple_of(source * OWN, OWN), OWN), :] = ref[...]
    obs = obs_ref[...]
    facts = jnp.concatenate([facts_ref[4 * core + q] for q in range(4)], axis=1)
    mean = jnp.sum(obs, axis=0, keepdims=True) * (1.0 / MEMBERS)
    anomalies = obs - mean
    weighted = split(anomalies * facts[2:3])
    innovation = jnp.broadcast_to(facts[1:2] - mean, (8, HALF_OBS))
    nt = (((1,), (1,)), ((), ()))
    gram = dot3(split(anomalies), weighted, nt)
    drive = dot3(split(innovation), weighted, nt)
    half = MEMBERS // 2
    for c in range(2):

        @pl.when(core == c)
        def _():
            keep_ref[:half] = gram[c * half : (c + 1) * half]
            send_ref[:half] = gram[(1 - c) * half : (2 - c) * half]

    keep_ref[half:] = drive
    send_ref[half:] = drive


def weights_kernel(mem_ref, mine_ref, other_ref, out_ref, gram_ref):
    mem = mem_ref[0]
    core = lax.rem(mem, 2)
    half = MEMBERS // 2
    for c in range(2):

        @pl.when(core == c)
        def _():
            gram_ref[c * half : (c + 1) * half] = mine_ref[:half]
            gram_ref[(1 - c) * half : (2 - c) * half] = other_ref[:half]

    drive = mine_ref[half:]
    rows = lax.broadcasted_iota(jnp.int32, (MEMBERS, MEMBERS), 0)
    cols = lax.broadcasted_iota(jnp.int32, (MEMBERS, MEMBERS), 1)
    identity = (rows == cols).astype(jnp.float32)
    gram = gram_ref[...] + (MEMBERS - 1.0) * identity
    squares = jnp.sum(jnp.sum(gram * gram, axis=0, keepdims=True), axis=1, keepdims=True)
    scale = jnp.sqrt(squares)
    upper = gram / scale
    lower = 1.5 * identity - 0.5 * upper
    middle = lower
    for number in range(1, NS_ITERS):
        upper = mul(upper, middle)
        middle = 1.5 * identity - 0.5 * mul(lower, upper)
        lower = mul(middle, lower)
    lower_parts = split(lower)
    nt = (((1,), (1,)), ((), ()))
    inner = dot3(split(drive), lower_parts, nt)
    wbar = dot3(split(inner), lower_parts, nt)[:1] / scale
    weights = (MEMBERS - 1.0) ** 0.5 * lower / jnp.sqrt(scale) + wbar
    rest = (1.0 - jnp.sum(weights, axis=1, keepdims=True)) * (1.0 / MEMBERS)
    gram_ref[...] = weights + rest
    for n, (a, b) in enumerate(PATHS):
        place = lax.rem(mem // 2 + a, 4) * 2 + lax.rem(core + b, 2)
        high, low = split(gram_ref[pl.ds(pl.multiple_of(place * OWN, OWN), OWN), :])
        out_ref[0, n * OWN : (n + 1) * OWN] = high
        out_ref[1, n * OWN : (n + 1) * OWN] = low


def product_kernel(mem_ref, weights_ref, early_ref, rest_ref, *out_refs):
    flat = [ref.reshape(OWN * CHUNK, LANES) for ref in out_refs]

    def compute(x_ref):
        weights = (weights_ref[0], weights_ref[1])
        for half in range(0, CHUNK, HALO):
            parts = [
                split(jnp.concatenate([x_ref[s, half + t] for s in range(N_MEM)], axis=0))
                for t in range(HALO)
            ]
            x = tuple(jnp.concatenate([p[n] for p in parts], axis=1) for n in range(2))
            y = dot3(weights, x)
            for t in range(HALO):
                for n, ref in enumerate(flat):
                    ref[pl.ds(half + t, OWN, stride=CHUNK), :] = y[
                        n * OWN : (n + 1) * OWN, t * LANES : (t + 1) * LANES
                    ]

    step = pl.program_id(0)
    pl.when(step == 1)(lambda: compute(early_ref))
    pl.when(step != 1)(lambda: compute(rest_ref))


def product(mem, weights, early, rest, part):
    outs = [pl.BlockSpec((OWN, CHUNK, LANES), lambda n, g: (0, n, 0))] * (N_MEM // 2)
    shapes = [f32(OWN, ROWS, LANES)] * (N_MEM // 2)
    if part == 0:
        outs[0] = pl.BlockSpec((OWN, CHUNK, LANES), lambda n, g: (0, n, g[0]))
        shapes[0] = f32(OWN, ROWS, WIDTH)
    block = (N_MEM, CHUNK, OWN, LANES)
    return pl.pallas_call(
        product_kernel,
        grid_spec=pltpu.PrefetchScalarGridSpec(
            num_scalar_prefetch=1,
            grid=(ROWS // CHUNK,),
            in_specs=[
                pl.BlockSpec((2, MEMBERS // 2, MEMBERS), lambda n, g: (0, part, 0)),
                pl.BlockSpec(block, lambda n, g: (0, 0, 0, 0)),
                pl.BlockSpec(block, lambda n, g: (0, jnp.maximum(n - 1, 0), 0, 0)),
            ],
            out_specs=outs,
        ),
        out_shape=shapes,
        compiler_params=params(16),
        cost_estimate=cost(3),
    )(mem, weights, early, rest)


def place_kernel(group_ref, x_ref, before_ref, out_ref):
    out_ref[...] = x_ref[...]


def place(x, group, before):
    return pl.pallas_call(
        place_kernel,
        grid_spec=pltpu.PrefetchScalarGridSpec(
            num_scalar_prefetch=1,
            grid=(1,),
            in_specs=[
                pl.BlockSpec((OWN, ROWS, LANES), lambda n, g: (0, 0, 0)),
                pl.BlockSpec(memory_space=pl.ANY),
            ],
            out_specs=pl.BlockSpec((OWN, ROWS, LANES), lambda n, g: (0, 0, g[0])),
        ),
        out_shape=f32(OWN, ROWS, WIDTH),
        input_output_aliases={2: 0},
        compiler_params=params(8),
        cost_estimate=cost(1),
    )(group, x, before)


def f32(*shape):
    return jax.ShapeDtypeStruct(shape, jnp.float32)


def send_on(x, a, b):
    return lax.ppermute(
        x, "mem", [(i, ((i // 2 + a) % 4) * 2 + (i + b) % 2) for i in range(N_MEM)]
    )


def swap(x, axis, bit):
    count = lax.axis_size(axis)
    return lax.ppermute(x, axis, [(i, i ^ bit) for i in range(count)])


def local(
    prior_samples, horizontal_flow_ratio, vertical_flow_ratio, obs_index, obs_value, obs_weight
):
    h, v = horizontal_flow_ratio, vertical_flow_ratio
    anywhere = pl.BlockSpec(memory_space=pl.ANY)
    mem = lax.axis_index("mem").astype(jnp.int32)
    core = (mem % 2).reshape(1)
    parity = (lax.axis_index("reg").astype(jnp.int32) % 2).reshape(1)
    sources = [
        (((mem // 2 - a) % 4) * 2 + (mem % 2 + b) % 2).reshape(1) for a, b in PATHS
    ]
    mem = mem.reshape(1)

    halo_a, halo_b = pl.pallas_call(
        pack_kernel,
        out_shape=[f32(HALO, OWN + SUB, WIDTH)] * 2,
        in_specs=[SMEM, anywhere, VMEM, VMEM],
        out_specs=[VMEM, VMEM],
        scratch_shapes=[
            pltpu.VMEM((2, GROUPS, OWN, SUB, LANES), jnp.float32),
            pltpu.SemaphoreType.DMA((2, GROUPS)),
        ],
        compiler_params=params(56),
    )(parity, prior_samples, h, v)
    halo_a, halo_b, prior_samples, h, v = lax.optimization_barrier(
        (halo_a, halo_b, prior_samples, h, v)
    )
    halo_b = lax.ppermute(
        halo_b, "reg", [(i, (i - 1 if i % 2 == 0 else i + 1) % N_REG) for i in range(N_REG)]
    )
    halo_a = lax.ppermute(halo_a, "reg", [(i, i ^ 1) for i in range(N_REG)])

    facts = jnp.concatenate(
        [obs_index.astype(jnp.float32), obs_value, obs_weight, jnp.zeros((SUB - 3, OBS))], axis=0
    )
    facts = lax.all_to_all(
        jnp.broadcast_to(facts[None], (N_MEM, SUB, OBS)), "mem", 0, 0, tiled=True
    )

    inner, early, rim = pl.pallas_call(
        interior_kernel,
        out_shape=[
            f32(GROUPS, ROWS - EDGE, OWN, LANES),
            f32(GROUPS, CHUNK, OWN, LANES),
            f32(2, EDGE, OWN, WIDTH),
        ],
        in_specs=[anywhere, VMEM, VMEM],
        out_specs=[anywhere] * 3,
        scratch_shapes=[
            pltpu.VMEM((GROUPS, OWN * ROWS, LANES), jnp.float32),
            pltpu.VMEM((ROWS, OWN, WIDTH), jnp.float32),
            pltpu.VMEM((ROWS, OWN, WIDTH), jnp.float32),
            pltpu.VMEM((GROUPS, ROWS - EDGE, OWN, LANES), jnp.float32),
            pltpu.VMEM((2, ROWS, SUB, WIDTH), jnp.float32),
            pltpu.SemaphoreType.DMA((GROUPS,)),
            pltpu.SemaphoreType.DMA((5,)),
        ],
        compiler_params=params(56),
        cost_estimate=cost(17),
    )(prior_samples.reshape(OWN * ROWS, WIDTH), h, v)
    early, halo_a, halo_b = lax.optimization_barrier((early, halo_a, halo_b))
    early = lax.all_to_all(early, "mem", 0, 0, tiled=True)
    same, flip, rest = pl.pallas_call(
        edge_kernel,
        out_shape=[
            f32(OWN, HALF_OBS),
            f32(OWN, HALF_OBS),
            f32(GROUPS, ROWS - CHUNK, OWN, LANES),
        ],
        in_specs=[SMEM, SMEM, anywhere] + [VMEM] * 6,
        out_specs=[VMEM, VMEM, anywhere],
        scratch_shapes=[
            pltpu.VMEM((2, OWN, HALF_OBS), jnp.float32),
            pltpu.VMEM((GROUPS, ROWS, OWN, LANES), jnp.float32),
            pltpu.VMEM((HALO + EDGE, OWN, WIDTH), jnp.float32),
            pltpu.VMEM((HALO + EDGE, OWN, WIDTH), jnp.float32),
            pltpu.VMEM((2, HALO + EDGE, SUB, WIDTH), jnp.float32),
            pltpu.SemaphoreType.DMA,
            pltpu.SemaphoreType.DMA((2,)),
        ],
        compiler_params=params(56),
        cost_estimate=cost(13),
    )(parity, core, inner, rim, halo_a, halo_b, h, v, facts)
    obs = [same] + [send_on(flip if b else same, a, b) for a, b in PATHS[1:]]
    early, *obs = lax.optimization_barrier((early, *obs))

    keep, send = pl.pallas_call(
        gram_kernel,
        out_shape=[f32(MEMBERS // 2 + 8, MEMBERS)] * 2,
        in_specs=[SMEM] + [VMEM] * (N_MEM + 1),
        out_specs=[VMEM, VMEM],
        scratch_shapes=[pltpu.VMEM((MEMBERS, HALF_OBS), jnp.float32)],
        compiler_params=params(12),
        cost_estimate=cost(3),
    )(mem, *obs, facts)
    rest, send = lax.optimization_barrier((rest, send))
    rest = lax.all_to_all(rest, "mem", 0, 0, tiled=True)
    total = keep + swap(send, "mem", 1)
    for bit in (1, 2, 4, 8):
        total = total + swap(total, "reg", bit)
    other = swap(total, "mem", 1)

    weights = pl.pallas_call(
        weights_kernel,
        out_shape=jax.ShapeDtypeStruct((2, MEMBERS, MEMBERS), jnp.bfloat16),
        in_specs=[SMEM, VMEM, VMEM],
        out_specs=VMEM,
        scratch_shapes=[pltpu.VMEM((MEMBERS, MEMBERS), jnp.float32)],
        compiler_params=params(16),
        cost_estimate=cost(6),
    )(mem, total, other)

    result, *analysis = product(mem, weights, early, rest, 0)
    analysis = analysis + list(product(mem, weights, early, rest, 1))
    for x, (a, b), source in zip(analysis, PATHS[1:], sources[1:]):
        arrived = send_on(x, a, b)
        result = place(arrived, source, result)
    return result


def solution(mesh):
    placed = (
        P("mem", "reg", None),
        P("reg", None),
        P("reg", None),
        P("reg", "mem"),
        P("reg", "mem"),
        P("reg", "mem"),
    )
    return jax.shard_map(
        local, mesh=mesh, in_specs=placed, out_specs=P("mem", "reg", None), check_vma=False
    )
```

```python
import functools

import jax
import jax.numpy as jnp
from jax import lax
from jax.experimental import pallas as pl
from jax.experimental.pallas import tpu as pltpu
from jax.sharding import PartitionSpec as P

SECTIONS = 4
NS_ITERS = 6
MEMBERS = 256
N_MEM = 8
N_REG = 16
OWN = MEMBERS // N_MEM
ROWS = 32
WIDTH = 1024
LANES = 128
GROUPS = WIDTH // LANES
OBS = 256
HALF_OBS = OBS * GROUPS // 2
HALO = SECTIONS
EDGE = 2 * HALO
CHUNK = 8
SUB = 8
PATHS = ((0, 0), (2, 0), (1, 0), (3, 0), (2, 1), (1, 1), (3, 1), (0, 1))
VMEM = pl.BlockSpec(memory_space=pltpu.VMEM)
SMEM = pl.BlockSpec(memory_space=pltpu.SMEM)


def params(mib):
    return pltpu.CompilerParams(vmem_limit_bytes=mib * 1024 * 1024)


def cost(us):
    return pl.CostEstimate(flops=0, bytes_accessed=us * 3_000_000, transcendentals=0)


def split(x):
    high = x.astype(jnp.bfloat16)
    return high, (x - high.astype(jnp.float32)).astype(jnp.bfloat16)


def dot3(a, b, dims=(((1,), (0,)), ((), ()))):
    dot = functools.partial(
        lax.dot_general, dimension_numbers=dims, preferred_element_type=jnp.float32
    )
    return dot(a[0], b[0]) + (dot(a[0], b[1]) + dot(a[1], b[0]))


def mul(a, b):
    return dot3(split(a), split(b))


def coefficients(h, v, coef_ref, i):
    coef_ref[0, i] = jnp.broadcast_to(h, (SUB, WIDTH))
    coef_ref[1, i] = jnp.broadcast_to(v, (SUB, WIDTH))


def advance(src, dst, coef_ref, first, last, at, grouped):
    lane = lax.broadcasted_iota(jnp.int32, (SUB, LANES), 1)

    def tile(i, m):
        def read(row, j):
            return src[row, m : m + SUB, j * LANES : (j + 1) * LANES]

        middle = [read(i, j) for j in range(GROUPS)]
        right = [pltpu.roll(x, 1, 1) for x in middle]
        left = [pltpu.roll(x, LANES - 1, 1) for x in middle]
        results = []
        for j in range(GROUPS):
            h = coef_ref[0, i, :, j * LANES : (j + 1) * LANES]
            v = coef_ref[1, i, :, j * LANES : (j + 1) * LANES]
            side = jnp.where(
                h > 0.0,
                jnp.where(lane == 0, right[j - 1], right[j]),
                jnp.where(lane == LANES - 1, left[(j + 1) % GROUPS], left[j]),
            )
            below = jnp.where(v > 0.0, read(i - 1, j), read(i + 1, j))
            ah, av = jnp.abs(h), jnp.abs(v)
            results.append((1.0 - ah - av) * middle[j] + ah * side + av * below)
        for j, x in enumerate(results):
            if grouped:
                dst[j, i + at, m : m + SUB] = x
            else:
                dst[i + at, m : m + SUB, j * LANES : (j + 1) * LANES] = x

    def body(n, carry):
        start = jnp.minimum(first + n * HALO, last - HALO)
        for q in range(HALO):
            for m in range(0, OWN, SUB):
                tile(start + q, m)
        return carry

    lax.fori_loop(0, -(-(last - first) // HALO), body, 0)


def turn_kernel(
    parity_ref, prior_ref, h_ref, v_ref, a_ref, b_ref, turned_ref, given, one, sems, out_sems
):
    loads = [
        pltpu.make_async_copy(
            prior_ref.at[:, j * LANES : (j + 1) * LANES], given.at[j], sems.at[j]
        )
        for j in range(GROUPS)
    ]
    for load in loads:
        load.start()
    stores = []
    for j in range(GROUPS):
        at = slice(j * LANES, (j + 1) * LANES)
        loads[j].wait()
        for i in range(ROWS):
            one[i, :, at] = given[j, pl.ds(i, OWN, stride=ROWS), :]
        stores.append(
            pltpu.make_async_copy(one.at[:, :, at], turned_ref.at[:, :, at], out_sems.at[j])
        )
        stores[j].start()
    parity = parity_ref[0]
    for even in range(2):

        @pl.when(parity == 1 - even)
        def _():
            for side in range(2):
                out_ref = a_ref if side == even else b_ref
                for i in range(HALO):
                    row = side * (ROWS - HALO) + i
                    out_ref[i, :OWN] = one[row]
                    out_ref[i, OWN : OWN + 1] = h_ref[row : row + 1]
                    out_ref[i, OWN + 1 : OWN + 2] = v_ref[row : row + 1]

    for store in stores:
        store.wait()


def interior_kernel(
    turned_ref, h_ref, v_ref,
    inner_ref, early_ref, one, two, field, coef_ref, sems, out_sems,
):
    loads = [
        pltpu.make_async_copy(
            turned_ref.at[n * CHUNK : (n + 1) * CHUNK],
            one.at[n * CHUNK : (n + 1) * CHUNK],
            sems.at[n],
        )
        for n in range(ROWS // CHUNK)
    ]
    for load in loads:
        load.start()
    for i in range(ROWS):
        coefficients(h_ref[i : i + 1], v_ref[i : i + 1], coef_ref, i)
    for n, load in enumerate(loads):
        load.wait()
        advance(one, two, coef_ref, max(n * CHUNK - 1, 1), (n + 1) * CHUNK - 1, 0, False)
    advance(two, one, coef_ref, 2, ROWS - 2, 0, False)
    advance(one, two, coef_ref, 3, ROWS - 3, 0, False)
    advance(two, field, coef_ref, CHUNK, 2 * CHUNK, -HALO, True)
    early = pltpu.make_async_copy(
        field.at[:, CHUNK - HALO : 2 * CHUNK - HALO], early_ref, out_sems.at[0]
    )
    early.start()
    advance(two, field, coef_ref, HALO, CHUNK, -HALO, True)
    middle = 2 * CHUNK - HALO
    upper = pltpu.make_async_copy(field.at[:, :middle], inner_ref.at[:, :middle], out_sems.at[1])
    upper.start()
    advance(two, field, coef_ref, 2 * CHUNK, ROWS - HALO, -HALO, True)
    lower = pltpu.make_async_copy(field.at[:, middle:], inner_ref.at[:, middle:], out_sems.at[2])
    lower.start()
    early.wait()
    upper.wait()
    lower.wait()


def edge_kernel(
    parity_ref, core_ref, inner_ref, turned_ref, a_ref, b_ref, h_ref, v_ref, facts_ref,
    same_ref, flip_ref, rest_ref, obs_ref, field, ones, two, coef_ref, in_sem, out_sems, own_sems,
):
    load = pltpu.make_async_copy(inner_ref, field.at[:, HALO : ROWS - HALO], in_sem)
    load.start()
    owns = [
        pltpu.make_async_copy(
            turned_ref.at[side * (ROWS - EDGE) : side * (ROWS - EDGE) + EDGE],
            ones.at[side, (1 - side) * HALO : (1 - side) * HALO + EDGE],
            own_sems.at[side],
        )
        for side in range(2)
    ]
    for own in owns:
        own.start()
    odd = parity_ref[0] == 1
    for side, (near_ref, far_ref, halo_at, own_at, own_first) in enumerate(
        ((a_ref, b_ref, 0, HALO, 0), (b_ref, a_ref, EDGE, 0, ROWS - EDGE))
    ):
        for i in range(HALO):
            halo = jnp.where(odd, near_ref[i], far_ref[i])
            ones[side, halo_at + i] = halo[:OWN]
            coefficients(halo[OWN : OWN + 1], halo[OWN + 1 : OWN + 2], coef_ref, halo_at + i)
        for i in range(EDGE):
            coefficients(
                h_ref[own_first + i : own_first + i + 1],
                v_ref[own_first + i : own_first + i + 1],
                coef_ref,
                own_at + i,
            )
        last = HALO + EDGE
        one = ones.at[side]
        owns[side].wait()
        advance(one, two, coef_ref, 1, last - 1, 0, False)
        advance(two, one, coef_ref, 2, last - 2, 0, False)
        advance(one, two, coef_ref, 3, last - 3, 0, False)
        at = -HALO if side == 0 else ROWS - EDGE
        advance(two, field, coef_ref, HALO, EDGE, at, True)
    load.wait()
    stores = [
        pltpu.make_async_copy(
            field.at[:, first : first + count], rest_ref.at[:, to : to + count], out_sems.at[n]
        )
        for n, (first, count, to) in enumerate(
            ((0, CHUNK, 0), (2 * CHUNK, ROWS - 2 * CHUNK, CHUNK))
        )
    ]
    for store in stores:
        store.start()
    for g in range(GROUPS):
        for t in range(OBS // LANES):
            place = facts_ref[g, :1, t * LANES : (t + 1) * LANES].astype(jnp.int32)
            row = jnp.broadcast_to(place >> 7, (OWN, LANES))
            col = jnp.broadcast_to(place & (LANES - 1), (OWN, LANES))
            total = jnp.zeros((OWN, LANES), jnp.float32)
            for i in range(ROWS):
                x = jnp.take_along_axis(field[g, i], col, axis=1, mode="promise_in_bounds")
                total = jnp.where(row == i, x, total)
            at = (g % 4) * OBS + t * LANES
            obs_ref[lax.rem(core_ref[0] + g // 4, 2), :, at : at + LANES] = total
    same_ref[...] = obs_ref[0]
    flip_ref[...] = obs_ref[1]
    for store in stores:
        store.wait()


def gram_kernel(mem_ref, *refs):
    *from_refs, facts_ref, keep_ref, send_ref, obs_ref = refs
    mem = mem_ref[0]
    core = lax.rem(mem, 2)
    for (a, b), ref in zip(PATHS, from_refs):
        source = lax.rem(mem // 2 + 4 - a, 4) * 2 + lax.rem(core + b, 2)
        obs_ref[pl.ds(pl.multiple_of(source * OWN, OWN), OWN), :] = ref[...]
    obs = obs_ref[...]
    facts = jnp.concatenate([facts_ref[4 * core + q] for q in range(4)], axis=1)
    mean = jnp.sum(obs, axis=0, keepdims=True) * (1.0 / MEMBERS)
    anomalies = obs - mean
    weighted = split(anomalies * facts[2:3])
    innovation = jnp.broadcast_to(facts[1:2] - mean, (8, HALF_OBS))
    nt = (((1,), (1,)), ((), ()))
    gram = dot3(split(anomalies), weighted, nt)
    drive = dot3(split(innovation), weighted, nt)
    half = MEMBERS // 2
    for c in range(2):

        @pl.when(core == c)
        def _():
            keep_ref[:half] = gram[c * half : (c + 1) * half]
            send_ref[:half] = gram[(1 - c) * half : (2 - c) * half]

    keep_ref[half:] = drive
    send_ref[half:] = drive


def weights_kernel(mem_ref, mine_ref, other_ref, out_ref, gram_ref):
    mem = mem_ref[0]
    core = lax.rem(mem, 2)
    half = MEMBERS // 2
    for c in range(2):

        @pl.when(core == c)
        def _():
            gram_ref[c * half : (c + 1) * half] = mine_ref[:half]
            gram_ref[(1 - c) * half : (2 - c) * half] = other_ref[:half]

    drive = mine_ref[half:]
    rows = lax.broadcasted_iota(jnp.int32, (MEMBERS, MEMBERS), 0)
    cols = lax.broadcasted_iota(jnp.int32, (MEMBERS, MEMBERS), 1)
    identity = (rows == cols).astype(jnp.float32)
    gram = gram_ref[...] + (MEMBERS - 1.0) * identity
    squares = jnp.sum(jnp.sum(gram * gram, axis=0, keepdims=True), axis=1, keepdims=True)
    scale = jnp.sqrt(squares)
    upper = gram / scale
    lower = 1.5 * identity - 0.5 * upper
    middle = lower
    for number in range(1, NS_ITERS):
        upper = mul(upper, middle)
        middle = 1.5 * identity - 0.5 * mul(lower, upper)
        lower = mul(middle, lower)
    lower_parts = split(lower)
    nt = (((1,), (1,)), ((), ()))
    inner = dot3(split(drive), lower_parts, nt)
    wbar = dot3(split(inner), lower_parts, nt)[:1] / scale
    weights = (MEMBERS - 1.0) ** 0.5 * lower / jnp.sqrt(scale) + wbar
    rest = (1.0 - jnp.sum(weights, axis=1, keepdims=True)) * (1.0 / MEMBERS)
    gram_ref[...] = weights + rest
    for n, (a, b) in enumerate(PATHS):
        place = lax.rem(mem // 2 + a, 4) * 2 + lax.rem(core + b, 2)
        high, low = split(gram_ref[pl.ds(pl.multiple_of(place * OWN, OWN), OWN), :])
        out_ref[0, n * OWN : (n + 1) * OWN] = high
        out_ref[1, n * OWN : (n + 1) * OWN] = low


def product_kernel(mem_ref, weights_ref, early_ref, rest_ref, *out_refs):
    flat = [ref.reshape(OWN * CHUNK, LANES) for ref in out_refs]

    def compute(x_ref):
        weights = (weights_ref[0], weights_ref[1])
        for half in range(0, CHUNK, HALO):
            parts = [
                split(jnp.concatenate([x_ref[s, half + t] for s in range(N_MEM)], axis=0))
                for t in range(HALO)
            ]
            x = tuple(jnp.concatenate([p[n] for p in parts], axis=1) for n in range(2))
            y = dot3(weights, x)
            for t in range(HALO):
                for n, ref in enumerate(flat):
                    ref[pl.ds(half + t, OWN, stride=CHUNK), :] = y[
                        n * OWN : (n + 1) * OWN, t * LANES : (t + 1) * LANES
                    ]

    step = pl.program_id(0)
    pl.when(step == 1)(lambda: compute(early_ref))
    pl.when(step != 1)(lambda: compute(rest_ref))


def product(mem, weights, early, rest):
    outs = [pl.BlockSpec((OWN, CHUNK, LANES), lambda n, g: (0, n, g[0]))]
    outs += [pl.BlockSpec((OWN, CHUNK, LANES), lambda n, g: (0, n, 0))] * (N_MEM - 1)
    block = (N_MEM, CHUNK, OWN, LANES)
    return pl.pallas_call(
        product_kernel,
        grid_spec=pltpu.PrefetchScalarGridSpec(
            num_scalar_prefetch=1,
            grid=(ROWS // CHUNK,),
            in_specs=[
                pl.BlockSpec((2, MEMBERS, MEMBERS), lambda n, g: (0, 0, 0)),
                pl.BlockSpec(block, lambda n, g: (0, 0, 0, 0)),
                pl.BlockSpec(block, lambda n, g: (0, jnp.maximum(n - 1, 0), 0, 0)),
            ],
            out_specs=outs,
        ),
        out_shape=[f32(OWN, ROWS, WIDTH)] + [f32(OWN, ROWS, LANES)] * (N_MEM - 1),
        compiler_params=params(20),
        cost_estimate=cost(6),
    )(mem, weights, early, rest)


def place_kernel(group_ref, x_ref, before_ref, out_ref):
    out_ref[...] = x_ref[...]


def place(x, group, before):
    return pl.pallas_call(
        place_kernel,
        grid_spec=pltpu.PrefetchScalarGridSpec(
            num_scalar_prefetch=1,
            grid=(1,),
            in_specs=[
                pl.BlockSpec((OWN, ROWS, LANES), lambda n, g: (0, 0, 0)),
                pl.BlockSpec(memory_space=pl.ANY),
            ],
            out_specs=pl.BlockSpec((OWN, ROWS, LANES), lambda n, g: (0, 0, g[0])),
        ),
        out_shape=f32(OWN, ROWS, WIDTH),
        input_output_aliases={2: 0},
        compiler_params=params(8),
        cost_estimate=cost(1),
    )(group, x, before)


def f32(*shape):
    return jax.ShapeDtypeStruct(shape, jnp.float32)


def send_on(x, a, b):
    return lax.ppermute(
        x, "mem", [(i, ((i // 2 + a) % 4) * 2 + (i + b) % 2) for i in range(N_MEM)]
    )


def swap(x, axis, bit):
    count = lax.axis_size(axis)
    return lax.ppermute(x, axis, [(i, i ^ bit) for i in range(count)])


def local(
    prior_samples, horizontal_flow_ratio, vertical_flow_ratio, obs_index, obs_value, obs_weight
):
    h, v = horizontal_flow_ratio, vertical_flow_ratio
    anywhere = pl.BlockSpec(memory_space=pl.ANY)
    mem = lax.axis_index("mem").astype(jnp.int32)
    core = (mem % 2).reshape(1)
    parity = (lax.axis_index("reg").astype(jnp.int32) % 2).reshape(1)
    sources = [
        (((mem // 2 - a) % 4) * 2 + (mem % 2 + b) % 2).reshape(1) for a, b in PATHS
    ]
    mem = mem.reshape(1)

    halo_a, halo_b, turned = pl.pallas_call(
        turn_kernel,
        out_shape=[f32(HALO, OWN + SUB, WIDTH)] * 2 + [f32(ROWS, OWN, WIDTH)],
        in_specs=[SMEM, anywhere, VMEM, VMEM],
        out_specs=[VMEM, VMEM, anywhere],
        scratch_shapes=[
            pltpu.VMEM((GROUPS, OWN * ROWS, LANES), jnp.float32),
            pltpu.VMEM((ROWS, OWN, WIDTH), jnp.float32),
            pltpu.SemaphoreType.DMA((GROUPS,)),
            pltpu.SemaphoreType.DMA((GROUPS,)),
        ],
        compiler_params=params(56),
    )(parity, prior_samples.reshape(OWN * ROWS, WIDTH), h, v)
    halo_a, halo_b, turned, h, v = lax.optimization_barrier((halo_a, halo_b, turned, h, v))
    halo_b = lax.ppermute(
        halo_b, "reg", [(i, (i - 1 if i % 2 == 0 else i + 1) % N_REG) for i in range(N_REG)]
    )
    halo_a = lax.ppermute(halo_a, "reg", [(i, i ^ 1) for i in range(N_REG)])

    facts = jnp.concatenate(
        [obs_index.astype(jnp.float32), obs_value, obs_weight, jnp.zeros((SUB - 3, OBS))], axis=0
    )
    facts = lax.all_to_all(
        jnp.broadcast_to(facts[None], (N_MEM, SUB, OBS)), "mem", 0, 0, tiled=True
    )

    inner, early = pl.pallas_call(
        interior_kernel,
        out_shape=[
            f32(GROUPS, ROWS - EDGE, OWN, LANES),
            f32(GROUPS, CHUNK, OWN, LANES),
        ],
        in_specs=[anywhere, VMEM, VMEM],
        out_specs=[anywhere] * 2,
        scratch_shapes=[
            pltpu.VMEM((ROWS, OWN, WIDTH), jnp.float32),
            pltpu.VMEM((ROWS, OWN, WIDTH), jnp.float32),
            pltpu.VMEM((GROUPS, ROWS - EDGE, OWN, LANES), jnp.float32),
            pltpu.VMEM((2, ROWS, SUB, WIDTH), jnp.float32),
            pltpu.SemaphoreType.DMA((ROWS // CHUNK,)),
            pltpu.SemaphoreType.DMA((3,)),
        ],
        compiler_params=params(56),
        cost_estimate=cost(13),
    )(turned, h, v)
    early, halo_a, halo_b = lax.optimization_barrier((early, halo_a, halo_b))
    early = lax.all_to_all(early, "mem", 0, 0, tiled=True)
    same, flip, rest = pl.pallas_call(
        edge_kernel,
        out_shape=[
            f32(OWN, HALF_OBS),
            f32(OWN, HALF_OBS),
            f32(GROUPS, ROWS - CHUNK, OWN, LANES),
        ],
        in_specs=[SMEM, SMEM, anywhere, anywhere] + [VMEM] * 5,
        out_specs=[VMEM, VMEM, anywhere],
        scratch_shapes=[
            pltpu.VMEM((2, OWN, HALF_OBS), jnp.float32),
            pltpu.VMEM((GROUPS, ROWS, OWN, LANES), jnp.float32),
            pltpu.VMEM((2, HALO + EDGE, OWN, WIDTH), jnp.float32),
            pltpu.VMEM((HALO + EDGE, OWN, WIDTH), jnp.float32),
            pltpu.VMEM((2, HALO + EDGE, SUB, WIDTH), jnp.float32),
            pltpu.SemaphoreType.DMA,
            pltpu.SemaphoreType.DMA((2,)),
            pltpu.SemaphoreType.DMA((2,)),
        ],
        compiler_params=params(56),
        cost_estimate=cost(13),
    )(parity, core, inner, turned, halo_a, halo_b, h, v, facts)
    obs = [same] + [send_on(flip if b else same, a, b) for a, b in PATHS[1:]]
    early, *obs = lax.optimization_barrier((early, *obs))

    keep, send = pl.pallas_call(
        gram_kernel,
        out_shape=[f32(MEMBERS // 2 + 8, MEMBERS)] * 2,
        in_specs=[SMEM] + [VMEM] * (N_MEM + 1),
        out_specs=[VMEM, VMEM],
        scratch_shapes=[pltpu.VMEM((MEMBERS, HALF_OBS), jnp.float32)],
        compiler_params=params(12),
        cost_estimate=cost(3),
    )(mem, *obs, facts)
    rest, send = lax.optimization_barrier((rest, send))
    rest = lax.all_to_all(rest, "mem", 0, 0, tiled=True)
    total = keep + swap(send, "mem", 1)
    for bit in (1, 2, 4, 8):
        total = total + swap(total, "reg", bit)
    other = swap(total, "mem", 1)

    weights = pl.pallas_call(
        weights_kernel,
        out_shape=jax.ShapeDtypeStruct((2, MEMBERS, MEMBERS), jnp.bfloat16),
        in_specs=[SMEM, VMEM, VMEM],
        out_specs=VMEM,
        scratch_shapes=[pltpu.VMEM((MEMBERS, MEMBERS), jnp.float32)],
        compiler_params=params(16),
        cost_estimate=cost(6),
    )(mem, total, other)

    result, *analysis = product(mem, weights, early, rest)
    for x, (a, b), source in zip(analysis, PATHS[1:], sources[1:]):
        arrived = send_on(x, a, b)
        result = place(arrived, source, result)
    return result


def solution(mesh):
    placed = (
        P("mem", "reg", None),
        P("reg", None),
        P("reg", None),
        P("reg", "mem"),
        P("reg", "mem"),
        P("reg", "mem"),
    )
    return jax.shard_map(
        local, mesh=mesh, in_specs=placed, out_specs=P("mem", "reg", None), check_vma=False
    )
```

```python
import functools

import jax
import jax.numpy as jnp
from jax import lax
from jax.experimental import pallas as pl
from jax.experimental.pallas import tpu as pltpu
from jax.sharding import PartitionSpec as P

SECTIONS = 4
NS_ITERS = 6
MEMBERS = 256
N_MEM = 8
N_REG = 16
OWN = MEMBERS // N_MEM
ROWS = 32
WIDTH = 1024
LANES = 128
GROUPS = WIDTH // LANES
OBS = 256
HALF_OBS = OBS * GROUPS // 2
HALO = SECTIONS
EDGE = 2 * HALO
CHUNK = 8
SUB = 8
PATHS = ((0, 0), (2, 0), (1, 0), (3, 0), (2, 1), (1, 1), (3, 1), (0, 1))
VMEM = pl.BlockSpec(memory_space=pltpu.VMEM)
SMEM = pl.BlockSpec(memory_space=pltpu.SMEM)


def params(mib):
    return pltpu.CompilerParams(vmem_limit_bytes=mib * 1024 * 1024)


def cost(us):
    return pl.CostEstimate(flops=0, bytes_accessed=us * 3_000_000, transcendentals=0)


def split(x):
    high = x.astype(jnp.bfloat16)
    return high, (x - high.astype(jnp.float32)).astype(jnp.bfloat16)


def dot3(a, b, dims=(((1,), (0,)), ((), ()))):
    dot = functools.partial(
        lax.dot_general, dimension_numbers=dims, preferred_element_type=jnp.float32
    )
    return dot(a[0], b[0]) + (dot(a[0], b[1]) + dot(a[1], b[0]))


def mul(a, b):
    return dot3(split(a), split(b))


def coefficients(h, v, coef_ref, i):
    coef_ref[0, i] = jnp.broadcast_to(h, (SUB, WIDTH))
    coef_ref[1, i] = jnp.broadcast_to(v, (SUB, WIDTH))


def advance(src, dst, coef_ref, first, last, at, grouped):
    lane = lax.broadcasted_iota(jnp.int32, (SUB, LANES), 1)

    def tile(i, m):
        def read(row, j):
            return src[row, m : m + SUB, j * LANES : (j + 1) * LANES]

        middle = [read(i, j) for j in range(GROUPS)]
        right = [pltpu.roll(x, 1, 1) for x in middle]
        left = [pltpu.roll(x, LANES - 1, 1) for x in middle]
        results = []
        for j in range(GROUPS):
            h = coef_ref[0, i, :, j * LANES : (j + 1) * LANES]
            v = coef_ref[1, i, :, j * LANES : (j + 1) * LANES]
            side = jnp.where(
                h > 0.0,
                jnp.where(lane == 0, right[j - 1], right[j]),
                jnp.where(lane == LANES - 1, left[(j + 1) % GROUPS], left[j]),
            )
            below = jnp.where(v > 0.0, read(i - 1, j), read(i + 1, j))
            ah, av = jnp.abs(h), jnp.abs(v)
            results.append((1.0 - ah - av) * middle[j] + ah * side + av * below)
        for j, x in enumerate(results):
            if grouped:
                dst[j, i + at, m : m + SUB] = x
            else:
                dst[i + at, m : m + SUB, j * LANES : (j + 1) * LANES] = x

    def body(n, carry):
        start = jnp.minimum(first + n * HALO, last - HALO)
        for q in range(HALO):
            for m in range(0, OWN, SUB):
                tile(start + q, m)
        return carry

    lax.fori_loop(0, -(-(last - first) // HALO), body, 0)


def turn_kernel(
    parity_ref, prior_ref, h_ref, v_ref, index_ref, value_ref, weight_ref,
    a_ref, b_ref, facts_ref, turned_ref, given, one, sems, out_sems,
):
    loads = [
        pltpu.make_async_copy(
            prior_ref.at[:, j * LANES : (j + 1) * LANES], given.at[j], sems.at[j]
        )
        for j in range(GROUPS)
    ]
    for load in loads:
        load.start()
    for n in range(N_MEM):
        facts_ref[n] = jnp.zeros((SUB, OBS), jnp.float32)
        facts_ref[n, 0:1] = index_ref[...].astype(jnp.float32)
        facts_ref[n, 1:2] = value_ref[...]
        facts_ref[n, 2:3] = weight_ref[...]
    stores = []
    for j in range(GROUPS):
        at = slice(j * LANES, (j + 1) * LANES)
        loads[j].wait()
        one[:, :, at] = jnp.swapaxes(given[j].reshape(OWN, ROWS, LANES), 0, 1)
        stores.append(
            pltpu.make_async_copy(one.at[:, :, at], turned_ref.at[:, :, at], out_sems.at[j])
        )
        stores[j].start()
    parity = parity_ref[0]
    for even in range(2):

        @pl.when(parity == 1 - even)
        def _():
            for side in range(2):
                out_ref = a_ref if side == even else b_ref
                for i in range(HALO):
                    row = side * (ROWS - HALO) + i
                    out_ref[i, :OWN] = one[row]
                    out_ref[i, OWN : OWN + 1] = h_ref[row : row + 1]
                    out_ref[i, OWN + 1 : OWN + 2] = v_ref[row : row + 1]

    for store in stores:
        store.wait()


def interior_kernel(
    turned_ref, h_ref, v_ref,
    inner_ref, early_ref, one, two, field, coef_ref, sems, out_sems,
):
    loads = [
        pltpu.make_async_copy(
            turned_ref.at[n * CHUNK : (n + 1) * CHUNK],
            one.at[n * CHUNK : (n + 1) * CHUNK],
            sems.at[n],
        )
        for n in range(ROWS // CHUNK)
    ]
    for load in loads:
        load.start()
    for i in range(ROWS):
        coefficients(h_ref[i : i + 1], v_ref[i : i + 1], coef_ref, i)
    for n, load in enumerate(loads):
        load.wait()
        advance(one, two, coef_ref, max(n * CHUNK - 1, 1), (n + 1) * CHUNK - 1, 0, False)
    advance(two, one, coef_ref, 2, ROWS - 2, 0, False)
    advance(one, two, coef_ref, 3, ROWS - 3, 0, False)
    advance(two, field, coef_ref, CHUNK, 2 * CHUNK, -HALO, True)
    early = pltpu.make_async_copy(
        field.at[:, CHUNK - HALO : 2 * CHUNK - HALO], early_ref, out_sems.at[0]
    )
    early.start()
    advance(two, field, coef_ref, HALO, CHUNK, -HALO, True)
    middle = 2 * CHUNK - HALO
    upper = pltpu.make_async_copy(field.at[:, :middle], inner_ref.at[:, :middle], out_sems.at[1])
    upper.start()
    advance(two, field, coef_ref, 2 * CHUNK, ROWS - HALO, -HALO, True)
    lower = pltpu.make_async_copy(field.at[:, middle:], inner_ref.at[:, middle:], out_sems.at[2])
    lower.start()
    early.wait()
    upper.wait()
    lower.wait()


def edge_kernel(
    parity_ref, core_ref, inner_ref, turned_ref, a_ref, b_ref, h_ref, v_ref, facts_ref,
    same_ref, flip_ref, own_ref, rest_ref, obs_ref, field, ones, two, coef_ref, in_sem, out_sems, own_sems,
):
    load = pltpu.make_async_copy(inner_ref, field.at[:, HALO : ROWS - HALO], in_sem)
    load.start()
    owns = [
        pltpu.make_async_copy(
            turned_ref.at[side * (ROWS - EDGE) : side * (ROWS - EDGE) + EDGE],
            ones.at[side, (1 - side) * HALO : (1 - side) * HALO + EDGE],
            own_sems.at[side],
        )
        for side in range(2)
    ]
    for own in owns:
        own.start()
    odd = parity_ref[0] == 1
    for side, (near_ref, far_ref, halo_at, own_at, own_first) in enumerate(
        ((a_ref, b_ref, 0, HALO, 0), (b_ref, a_ref, EDGE, 0, ROWS - EDGE))
    ):
        for i in range(HALO):
            halo = jnp.where(odd, near_ref[i], far_ref[i])
            ones[side, halo_at + i] = halo[:OWN]
            coefficients(halo[OWN : OWN + 1], halo[OWN + 1 : OWN + 2], coef_ref, halo_at + i)
        for i in range(EDGE):
            coefficients(
                h_ref[own_first + i : own_first + i + 1],
                v_ref[own_first + i : own_first + i + 1],
                coef_ref,
                own_at + i,
            )
        last = HALO + EDGE
        one = ones.at[side]
        owns[side].wait()
        advance(one, two, coef_ref, 1, last - 1, 0, False)
        advance(two, one, coef_ref, 2, last - 2, 0, False)
        advance(one, two, coef_ref, 3, last - 3, 0, False)
        at = -HALO if side == 0 else ROWS - EDGE
        advance(two, field, coef_ref, HALO, EDGE, at, True)
    load.wait()
    stores = [
        pltpu.make_async_copy(
            field.at[:, first : first + count], rest_ref.at[:, to : to + count], out_sems.at[n]
        )
        for n, (first, count, to) in enumerate(
            ((0, CHUNK, 0), (2 * CHUNK, ROWS - 2 * CHUNK, CHUNK))
        )
    ]
    for store in stores:
        store.start()
    for g in range(GROUPS):
        for t in range(OBS // LANES):
            place = facts_ref[g, :1, t * LANES : (t + 1) * LANES].astype(jnp.int32)
            row = jnp.broadcast_to(place >> 7, (OWN, LANES))
            col = jnp.broadcast_to(place & (LANES - 1), (OWN, LANES))
            total = jnp.zeros((OWN, LANES), jnp.float32)
            for i in range(ROWS):
                x = jnp.take_along_axis(field[g, i], col, axis=1, mode="promise_in_bounds")
                total = jnp.where(row == i, x, total)
            at = (g % 4) * OBS + t * LANES
            obs_ref[lax.rem(core_ref[0] + g // 4, 2), :, at : at + LANES] = total
    same_ref[...] = obs_ref[0]
    flip_ref[...] = obs_ref[1]
    own_ref[:OWN] = obs_ref[0]
    own_ref[OWN:] = jnp.concatenate([facts_ref[4 * core_ref[0] + q] for q in range(4)], axis=1)
    for store in stores:
        store.wait()


def gram_kernel(mem_ref, *refs):
    *from_refs, keep_ref, send_ref, obs_ref = refs
    mem = mem_ref[0]
    core = lax.rem(mem, 2)
    for (a, b), ref in zip(PATHS, from_refs):
        source = lax.rem(mem // 2 + 4 - a, 4) * 2 + lax.rem(core + b, 2)
        obs_ref[pl.ds(pl.multiple_of(source * OWN, OWN), OWN), :] = ref[:OWN]
    obs = obs_ref[...]
    facts = from_refs[0][OWN:]
    mean = jnp.sum(obs, axis=0, keepdims=True) * (1.0 / MEMBERS)
    anomalies = obs - mean
    weighted = split(anomalies * facts[2:3])
    innovation = jnp.broadcast_to(facts[1:2] - mean, (8, HALF_OBS))
    nt = (((1,), (1,)), ((), ()))
    gram = dot3(split(anomalies), weighted, nt)
    drive = dot3(split(innovation), weighted, nt)
    half = MEMBERS // 2
    for c in range(2):

        @pl.when(core == c)
        def _():
            keep_ref[:half] = gram[c * half : (c + 1) * half]
            send_ref[:half] = gram[(1 - c) * half : (2 - c) * half]

    keep_ref[half:] = drive
    send_ref[half:] = drive


def weights_kernel(mem_ref, mine_ref, other_ref, out_ref, gram_ref):
    mem = mem_ref[0]
    core = lax.rem(mem, 2)
    half = MEMBERS // 2
    for c in range(2):

        @pl.when(core == c)
        def _():
            gram_ref[c * half : (c + 1) * half] = mine_ref[:half]
            gram_ref[(1 - c) * half : (2 - c) * half] = other_ref[:half]

    drive = mine_ref[half:]
    rows = lax.broadcasted_iota(jnp.int32, (MEMBERS, MEMBERS), 0)
    cols = lax.broadcasted_iota(jnp.int32, (MEMBERS, MEMBERS), 1)
    identity = (rows == cols).astype(jnp.float32)
    gram = gram_ref[...] + (MEMBERS - 1.0) * identity
    squares = jnp.sum(jnp.sum(gram * gram, axis=0, keepdims=True), axis=1, keepdims=True)
    scale = jnp.sqrt(squares)
    upper = gram / scale
    lower = 1.5 * identity - 0.5 * upper
    middle = lower
    for number in range(1, NS_ITERS):
        upper = mul(upper, middle)
        middle = 1.5 * identity - 0.5 * mul(lower, upper)
        lower = mul(middle, lower)
    lower_parts = split(lower)
    nt = (((1,), (1,)), ((), ()))
    inner = dot3(split(drive), lower_parts, nt)
    wbar = dot3(split(inner), lower_parts, nt)[:1] / scale
    weights = (MEMBERS - 1.0) ** 0.5 * lower / jnp.sqrt(scale) + wbar
    rest = (1.0 - jnp.sum(weights, axis=1, keepdims=True)) * (1.0 / MEMBERS)
    gram_ref[...] = weights + rest
    for n, (a, b) in enumerate(PATHS):
        place = lax.rem(mem // 2 + a, 4) * 2 + lax.rem(core + b, 2)
        high, low = split(gram_ref[pl.ds(pl.multiple_of(place * OWN, OWN), OWN), :])
        out_ref[0, n * OWN : (n + 1) * OWN] = high
        out_ref[1, n * OWN : (n + 1) * OWN] = low


def product_kernel(mem_ref, weights_ref, early_ref, rest_ref, *out_refs):
    flat = [ref.reshape(OWN * CHUNK, LANES) for ref in out_refs]

    def compute(x_ref):
        weights = (weights_ref[0], weights_ref[1])
        for half in range(0, CHUNK, HALO):
            parts = [
                split(jnp.concatenate([x_ref[s, half + t] for s in range(N_MEM)], axis=0))
                for t in range(HALO)
            ]
            x = tuple(jnp.concatenate([p[n] for p in parts], axis=1) for n in range(2))
            y = dot3(weights, x)
            for t in range(HALO):
                for n, ref in enumerate(flat):
                    ref[pl.ds(half + t, OWN, stride=CHUNK), :] = y[
                        n * OWN : (n + 1) * OWN, t * LANES : (t + 1) * LANES
                    ]

    step = pl.program_id(0)
    pl.when(step == 1)(lambda: compute(early_ref))
    pl.when(step != 1)(lambda: compute(rest_ref))


def product(mem, weights, early, rest):
    outs = [pl.BlockSpec((OWN, CHUNK, LANES), lambda n, g: (0, n, g[0]))]
    outs += [pl.BlockSpec((OWN, CHUNK, LANES), lambda n, g: (0, n, 0))] * (N_MEM - 1)
    block = (N_MEM, CHUNK, OWN, LANES)
    return pl.pallas_call(
        product_kernel,
        grid_spec=pltpu.PrefetchScalarGridSpec(
            num_scalar_prefetch=1,
            grid=(ROWS // CHUNK,),
            in_specs=[
                pl.BlockSpec((2, MEMBERS, MEMBERS), lambda n, g: (0, 0, 0)),
                pl.BlockSpec(block, lambda n, g: (0, 0, 0, 0)),
                pl.BlockSpec(block, lambda n, g: (0, jnp.maximum(n - 1, 0), 0, 0)),
            ],
            out_specs=outs,
        ),
        out_shape=[f32(OWN, ROWS, WIDTH)] + [f32(OWN, ROWS, LANES)] * (N_MEM - 1),
        compiler_params=params(20),
        cost_estimate=cost(6),
    )(mem, weights, early, rest)


def place_kernel(group_ref, x_ref, before_ref, out_ref):
    out_ref[...] = x_ref[...]


def place(x, group, before):
    return pl.pallas_call(
        place_kernel,
        grid_spec=pltpu.PrefetchScalarGridSpec(
            num_scalar_prefetch=1,
            grid=(1,),
            in_specs=[
                pl.BlockSpec((OWN, ROWS, LANES), lambda n, g: (0, 0, 0)),
                pl.BlockSpec(memory_space=pl.ANY),
            ],
            out_specs=pl.BlockSpec((OWN, ROWS, LANES), lambda n, g: (0, 0, g[0])),
        ),
        out_shape=f32(OWN, ROWS, WIDTH),
        input_output_aliases={2: 0},
        compiler_params=params(8),
        cost_estimate=cost(1),
    )(group, x, before)


def f32(*shape):
    return jax.ShapeDtypeStruct(shape, jnp.float32)


def send_on(x, a, b):
    return lax.ppermute(
        x, "mem", [(i, ((i // 2 + a) % 4) * 2 + (i + b) % 2) for i in range(N_MEM)]
    )


def swap(x, axis, bit):
    count = lax.axis_size(axis)
    return lax.ppermute(x, axis, [(i, i ^ bit) for i in range(count)])


def local(
    prior_samples, horizontal_flow_ratio, vertical_flow_ratio, obs_index, obs_value, obs_weight
):
    h, v = horizontal_flow_ratio, vertical_flow_ratio
    anywhere = pl.BlockSpec(memory_space=pl.ANY)
    mem = lax.axis_index("mem").astype(jnp.int32)
    core = (mem % 2).reshape(1)
    parity = (lax.axis_index("reg").astype(jnp.int32) % 2).reshape(1)
    sources = [
        (((mem // 2 - a) % 4) * 2 + (mem % 2 + b) % 2).reshape(1) for a, b in PATHS
    ]
    mem = mem.reshape(1)

    halo_a, halo_b, facts, turned = pl.pallas_call(
        turn_kernel,
        out_shape=[f32(HALO, OWN + SUB, WIDTH)] * 2
        + [f32(N_MEM, SUB, OBS), f32(ROWS, OWN, WIDTH)],
        in_specs=[SMEM, anywhere] + [VMEM] * 5,
        out_specs=[VMEM, VMEM, VMEM, anywhere],
        scratch_shapes=[
            pltpu.VMEM((GROUPS, OWN * ROWS, LANES), jnp.float32),
            pltpu.VMEM((ROWS, OWN, WIDTH), jnp.float32),
            pltpu.SemaphoreType.DMA((GROUPS,)),
            pltpu.SemaphoreType.DMA((GROUPS,)),
        ],
        compiler_params=params(56),
    )(
        parity, prior_samples.reshape(OWN * ROWS, WIDTH), h, v, obs_index, obs_value, obs_weight
    )
    halo_a, halo_b, turned, h, v = lax.optimization_barrier((halo_a, halo_b, turned, h, v))
    halo_b = lax.ppermute(
        halo_b, "reg", [(i, (i - 1 if i % 2 == 0 else i + 1) % N_REG) for i in range(N_REG)]
    )
    halo_a = lax.ppermute(halo_a, "reg", [(i, i ^ 1) for i in range(N_REG)])

    facts = lax.all_to_all(facts, "mem", 0, 0, tiled=True)

    inner, early = pl.pallas_call(
        interior_kernel,
        out_shape=[
            f32(GROUPS, ROWS - EDGE, OWN, LANES),
            f32(GROUPS, CHUNK, OWN, LANES),
        ],
        in_specs=[anywhere, VMEM, VMEM],
        out_specs=[anywhere] * 2,
        scratch_shapes=[
            pltpu.VMEM((ROWS, OWN, WIDTH), jnp.float32),
            pltpu.VMEM((ROWS, OWN, WIDTH), jnp.float32),
            pltpu.VMEM((GROUPS, ROWS - EDGE, OWN, LANES), jnp.float32),
            pltpu.VMEM((2, ROWS, SUB, WIDTH), jnp.float32),
            pltpu.SemaphoreType.DMA((ROWS // CHUNK,)),
            pltpu.SemaphoreType.DMA((3,)),
        ],
        compiler_params=params(56),
        cost_estimate=cost(13),
    )(turned, h, v)
    early, halo_a, halo_b = lax.optimization_barrier((early, halo_a, halo_b))
    early = lax.all_to_all(early, "mem", 0, 0, tiled=True)
    same, flip, own, rest = pl.pallas_call(
        edge_kernel,
        out_shape=[
            f32(OWN, HALF_OBS),
            f32(OWN, HALF_OBS),
            f32(OWN + SUB, HALF_OBS),
            f32(GROUPS, ROWS - CHUNK, OWN, LANES),
        ],
        in_specs=[SMEM, SMEM, anywhere, anywhere] + [VMEM] * 5,
        out_specs=[VMEM, VMEM, VMEM, anywhere],
        scratch_shapes=[
            pltpu.VMEM((2, OWN, HALF_OBS), jnp.float32),
            pltpu.VMEM((GROUPS, ROWS, OWN, LANES), jnp.float32),
            pltpu.VMEM((2, HALO + EDGE, OWN, WIDTH), jnp.float32),
            pltpu.VMEM((HALO + EDGE, OWN, WIDTH), jnp.float32),
            pltpu.VMEM((2, HALO + EDGE, SUB, WIDTH), jnp.float32),
            pltpu.SemaphoreType.DMA,
            pltpu.SemaphoreType.DMA((2,)),
            pltpu.SemaphoreType.DMA((2,)),
        ],
        compiler_params=params(56),
        cost_estimate=cost(13),
    )(parity, core, inner, turned, halo_a, halo_b, h, v, facts)
    obs = [own] + [send_on(flip if b else same, a, b) for a, b in PATHS[1:]]
    early, *obs = lax.optimization_barrier((early, *obs))

    keep, send = pl.pallas_call(
        gram_kernel,
        out_shape=[f32(MEMBERS // 2 + 8, MEMBERS)] * 2,
        in_specs=[SMEM] + [VMEM] * N_MEM,
        out_specs=[VMEM, VMEM],
        scratch_shapes=[pltpu.VMEM((MEMBERS, HALF_OBS), jnp.float32)],
        compiler_params=params(12),
        cost_estimate=cost(3),
    )(mem, *obs)
    rest, send = lax.optimization_barrier((rest, send))
    rest = lax.all_to_all(rest, "mem", 0, 0, tiled=True)
    total = keep + swap(send, "mem", 1)
    for bit in (1, 2, 4, 8):
        total = total + swap(total, "reg", bit)
    other = swap(total, "mem", 1)

    weights = pl.pallas_call(
        weights_kernel,
        out_shape=jax.ShapeDtypeStruct((2, MEMBERS, MEMBERS), jnp.bfloat16),
        in_specs=[SMEM, VMEM, VMEM],
        out_specs=VMEM,
        scratch_shapes=[pltpu.VMEM((MEMBERS, MEMBERS), jnp.float32)],
        compiler_params=params(16),
        cost_estimate=cost(6),
    )(mem, total, other)

    result, *analysis = product(mem, weights, early, rest)
    for x, (a, b), source in zip(analysis, PATHS[1:], sources[1:]):
        arrived = send_on(x, a, b)
        result = place(arrived, source, result)
    return result


def solution(mesh):
    placed = (
        P("mem", "reg", None),
        P("reg", None),
        P("reg", None),
        P("reg", "mem"),
        P("reg", "mem"),
        P("reg", "mem"),
    )
    return jax.shard_map(
        local, mesh=mesh, in_specs=placed, out_specs=P("mem", "reg", None), check_vma=False
    )
```
